32 devices in a mesh: region: 2 (over y), tile: 4 (over z), epoch: 2 (over x), band: 2 (over core).
Axes of the slice: x: 2, y: 2, z: 4, core: 2. Of those that a mesh axis runs over, the one named last changes fastest.
Arguments:
- source_params: float32 [64, 44, 128], P(('region', 'tile')), parts along dimension 0, as said below
- pixel_data: float32 [16, 2, 2, 128, 128], P(('region', 'tile'), 'epoch', 'band'), parts along dimension 0, may hold values from -6 to 6
- pixel_weight: float32 [16, 2, 2, 128, 128], P(('region', 'tile'), 'epoch', 'band'), parts along dimension 0, may hold values from 0.5 to 2
- psf_width: float32 [4, 2], P(('region', 'epoch'), 'band'), parts along dimension 0, may hold values from 0.8 to 2
- block_lists: int32 [16, 8], P(('region', 'tile')), parts along dimension 0, may hold values from 0 to 31, as said below
- block_counts: int32 [16], P(('region', 'tile')), parts along dimension 0, may hold values from 1 to 8, as said below
- block_offsets: int32 [16, 8, 2], P(('region', 'tile')), parts along dimension 0, may hold values from 0 to 63
Outputs:
- updated_params: float32 [64, 44, 128], P(('region', 'tile')), parts along dimension 0
The draws below stay inside these ranges and needn't reach their ends.
There are 2 independent parts, one for each index of `region`. The reference program is written for one: setup_inputs(seed, part) draws one part's arguments, and reference() takes and returns one part's arrays. A program takes and returns all parts, laid end to end along the dimension named above; each array names one. Nothing has to cross between parts.
Inputs may be any that keep to these rules, and one draw needn't show every extreme that they name: `block_lists`: block g is owned by tile index g // 8. Among the 2 x 8 slots of one tile index no id repeats and no owner appears more than 4 times; on every tile index some owner appears exactly 4 times. `block_counts`: slots of a tile beyond its count are unused. `source_params`: rows 0 and 1 lie in 0 to 4; rows 2 + 6c + 2 lie in 0 to 1.4 and rows 2 + 6c + 3 in -0.3 to 0.3.
All inputs are finite; a program needn't handle non-finite values.
Results may differ from the reference program's by a relative error of at most 0.0003.
Values sent between devices are 32-bit elements; how exact they have to be, the bound alone decides.
No kernel may reach another device: no remote copies, remote signals or barrier semaphores. Data moves between devices by JAX's collectives and lax.ppermute only.
A program may use at most 64 MiB of HBM per device.

```python
import math
import jax
import jax.numpy as jnp
from jax import lax

PIX = 128
PARAMS = 44
SB = 128
NB_DEV = 8
TILES_DEV = 2
MAXB = 8
ITERS = 2
CAP = 4
NB = 32
NT = 8
EPOCHS = 2
BANDS = 2


def draw_source_params(key, part):
    key = jax.random.fold_in(key, 13)
    key_pos, key_shift, key_width, key_aniso, key_amp = jax.random.split(key, 5)
    positions = jax.random.uniform(key_pos, (NB, 2, SB), jnp.float32, 0.0, 4.0)
    shifts = jax.random.normal(key_shift, (NB, 7, 2, SB), jnp.float32)
    widths = jax.random.uniform(key_width, (NB, 7, 1, SB), jnp.float32, 0.2, 1.2)
    amplitudes = jax.random.uniform(key_amp, (NB, 7, 2, SB), jnp.float32, 0.2, 1.5)
    aniso_rows = jax.random.uniform(key_aniso, (NB, 7, 1, SB), jnp.float32, -0.3, 0.3)
    components = jnp.concatenate([shifts, widths, aniso_rows, amplitudes], axis=2).reshape(NB, 42, SB)
    return jnp.concatenate([positions, components], axis=1)


def draw_block_lists(key, part):
    key = jax.random.fold_in(key, 11)
    owners = NB // NB_DEV
    per_device = TILES_DEV * MAXB

    def for_device(device, sub_key):
        key_shuffle, key_order, key_local = jax.random.split(sub_key, 3)
        shuffled = jax.random.permutation(key_shuffle, jnp.arange((owners - 1) * CAP))[:per_device - CAP]
        other_owner = shuffled // CAP
        other_owner = other_owner + (other_owner >= device).astype(jnp.int32)
        owner_row = jnp.concatenate([jnp.full((CAP,), device, jnp.int32), other_owner.astype(jnp.int32)])
        rank_row = jnp.concatenate([jnp.arange(CAP), shuffled % CAP]).astype(jnp.int32)
        order = jax.random.permutation(key_order, per_device)
        owner_row = owner_row[order]
        rank_row = rank_row[order]
        local_perms = jax.vmap(lambda inner_key: jax.random.permutation(inner_key, NB_DEV))(jax.random.split(key_local, owners))
        local_ids = local_perms[owner_row, rank_row]
        return (owner_row * NB_DEV + local_ids).reshape(TILES_DEV, MAXB)
    lists_all = jax.vmap(for_device)(jnp.arange(owners).astype(jnp.int32), jax.random.split(key, owners))
    return lists_all.reshape(owners * TILES_DEV, MAXB).astype(jnp.int32)


def draw_block_counts(key, part):
    key = jax.random.fold_in(key, 12)
    key_counts, key_crowd = jax.random.split(key)
    draws_two = jax.random.randint(key_counts, (2, NT), 1, MAXB + 1)
    counts_high = jnp.max(draws_two, axis=0)
    crowded = jax.random.randint(key_crowd, (), 0, NT // TILES_DEV)
    device_of = jnp.arange(NT) // TILES_DEV
    return jnp.where(device_of == crowded, MAXB, counts_high).astype(jnp.int32)


def plant(result, key, smallest, largest):
    longest = result.shape.index(max(result.shape))
    spots = []
    for shift in (0, 1):
        where = [jax.random.randint(jax.random.fold_in(key, axis), (), 0, length) for axis, length in enumerate(result.shape)]
        where[longest] = (where[longest] + shift) % result.shape[longest]
        spots.append(tuple(where))
    return result.at[spots[0]].set(smallest).at[spots[1]].set(largest)


def level_of(stream_key, shape, pieces, low, high):
    level, own = 1.0, jax.random.fold_in(stream_key, 6)
    for position, parts in pieces:
        draws = jnp.exp(jax.random.uniform(jax.random.fold_in(own, position), (parts,), jnp.float32, low / len(pieces), high / len(pieces)))
        level = level * jnp.repeat(draws, shape[position] // parts).reshape([-1 if axis == position else 1 for axis in range(len(shape))])
    return level


def centred(key, shape, deviation, reach, cuts=(), dtype=jnp.bfloat16):
    entries = deviation * jax.random.normal(key, shape, jnp.float32)
    if cuts:
        entries = entries * level_of(key, shape, cuts, -0.22, 0.18)
    return jnp.clip(entries, -reach, reach).astype(dtype)


def setup_inputs(seed: int = 0, part: int = 0) -> dict:
    key_of = jax.random.split(jax.random.key(seed), 8)
    part_splits = jax.random.split(jax.random.fold_in(key_of[7], part), 8)
    source_params = draw_source_params(jax.random.fold_in(jax.random.fold_in(key_of[7], part), 71), part)
    pixel_data = centred(part_splits[1], (NT, EPOCHS, BANDS, PIX, PIX), 1.0, 6.0, ((0, 4), (1, 2), (2, 2)), jnp.float32)
    pixel_weight = jnp.clip(jnp.exp(math.log(2.0) - 1.3862944 * jax.random.uniform(part_splits[2], (NT, EPOCHS, BANDS, PIX, PIX), jnp.float32) ** level_of(part_splits[2], (NT, EPOCHS, BANDS, PIX, PIX), ((0, 4), (1, 2), (2, 2)), -0.2, 0.2)), 0.5, 2.0)
    psf_width = jnp.clip(jnp.exp(math.log(2.0) - 0.9162907 * jax.random.uniform(part_splits[3], (EPOCHS, BANDS), jnp.float32) ** level_of(part_splits[3], (EPOCHS, BANDS), ((0, 2), (1, 2)), -0.2, 0.2)), 0.8, 2.0)
    block_lists = draw_block_lists(jax.random.fold_in(jax.random.fold_in(key_of[7], part), 71), part)
    block_counts = draw_block_counts(jax.random.fold_in(jax.random.fold_in(key_of[7], part), 71), part)
    block_offsets = plant(jax.random.randint(part_splits[6], (NT, MAXB, 2), 0, PIX // 2), jax.random.fold_in(part_splits[6], 1), 0, (PIX // 2) - 1).astype(jnp.int32)
    return {"source_params": source_params, "pixel_data": pixel_data, "pixel_weight": pixel_weight, "psf_width": psf_width, "block_lists": block_lists, "block_counts": block_counts, "block_offsets": block_offsets}


step_scale = 0.005

def render(block_params, offset_pair, psf_value, band_index, pixels):
    components = block_params[2:].reshape(7, 6, block_params.shape[-1])
    spacing = pixels / 8.0
    centre_x = spacing * block_params[0] + components[:, 0] + offset_pair[0]
    centre_y = spacing * block_params[1] + components[:, 1] + offset_pair[1]
    variance_x = jnp.exp(2.0 * (components[:, 2] + components[:, 3])) + psf_value * psf_value
    variance_y = jnp.exp(2.0 * (components[:, 2] - components[:, 3])) + psf_value * psf_value
    amplitude = lax.dynamic_index_in_dim(components, 4 + band_index, 1, keepdims=False)
    pixel_grid = jnp.arange(pixels).astype(jnp.float32)
    profile_x = jnp.exp(-0.5 * (pixel_grid[None, None, :] - centre_x[:, :, None]) ** 2 / variance_x[:, :, None])
    profile_y = amplitude[:, :, None] * jnp.exp(-0.5 * (pixel_grid[None, None, :] - centre_y[:, :, None]) ** 2 / variance_y[:, :, None])
    return jnp.einsum('csi,csj->ij', profile_x, profile_y, precision=lax.Precision.HIGHEST)

def reference(source_params, pixel_data, pixel_weight, psf_width, block_lists, block_counts, block_offsets):
    row_scale = (step_scale * jnp.where(jnp.arange(PARAMS) < 2, 1.0 / 64.0, 1.0)).astype(jnp.float32)[:, None]
    current = source_params
    for section_index in range(ITERS):

        def tile_body(slot_grads, tile_index):
            tile_ids = block_lists[tile_index]
            used_slots = block_counts[tile_index]
            offset_rows = block_offsets[tile_index].astype(jnp.float32)
            for epoch_index in range(EPOCHS):
                for band_index in range(BANDS):
                    psf_value = psf_width[epoch_index, band_index]

                    def add_slot(slot_index, image_sum):
                        return image_sum + render(current[tile_ids[slot_index]], offset_rows[slot_index], psf_value, band_index, PIX)
                    model_image = lax.fori_loop(0, used_slots, add_slot, jnp.zeros((PIX, PIX), jnp.float32))
                    cotangent = pixel_weight[tile_index, epoch_index, band_index] * (model_image - pixel_data[tile_index, epoch_index, band_index])

                    def grad_slot(slot_index, partial_grads):
                        block_params = current[tile_ids[slot_index]]
                        unused, pullback = jax.vjp(lambda block_value: render(block_value, offset_rows[slot_index], psf_value, band_index, PIX), block_params)
                        return partial_grads.at[tile_ids[slot_index]].add(pullback(cotangent)[0])
                    slot_grads = lax.fori_loop(0, used_slots, grad_slot, slot_grads)
            return (slot_grads, None)
        gradient, unused = lax.scan(tile_body, jnp.zeros(current.shape, jnp.float32), jnp.arange(NT).astype(jnp.int32))
        current = current - row_scale * gradient
    return current
```

```python
import functools
import math

import jax
import jax.numpy as jnp
from jax import lax
from jax.experimental import pallas as pl
from jax.experimental.pallas import tpu as pltpu
from jax.sharding import PartitionSpec as P

ITERS = 2
STEP = 0.005
COMPS = 7
BANDS = 2
SHARED = [0, 1] + [2 + 6 * c + k for k in range(4) for c in range(COMPS)]
HALF = len(SHARED) // BANDS
LOG2E = math.log2(math.e)
F32 = jnp.float32
BF16 = jnp.bfloat16
VMEM_LIMIT = 56 * 1024 * 1024


def quarter_layout(epochs):
    shared_rows = -(-HALF // epochs)
    rows = -(-(HALF + COMPS) // epochs)
    pieces, amp = [], 0
    for q in range(epochs):
        piece = [("s", i) for i in range(q * shared_rows, min((q + 1) * shared_rows, HALF))]
        while len(piece) < rows and amp < COMPS:
            piece.append(("a", amp))
            amp += 1
        pieces.append(piece + [None] * (rows - len(piece)))
    return shared_rows, rows, pieces


def row_of(band, entry):
    if entry is None:
        return 0
    kind, i = entry
    return SHARED[HALF * band + i] if kind == "s" else 2 + 6 * i + 4 + band


def split3(x):
    hi = x.astype(BF16)
    rest = x - hi.astype(F32)
    mid = rest.astype(BF16)
    low = (rest - mid.astype(F32)).astype(BF16)
    return jnp.concatenate([hi, mid, low], axis=0)


def pick(matrix, rows):
    wide = jnp.concatenate([matrix, matrix, matrix], axis=1).astype(BF16)
    return jnp.dot(wide, split3(rows), preferred_element_type=F32)


def vmem():
    return pl.BlockSpec(memory_space=pltpu.VMEM)


def smem():
    return pl.BlockSpec(memory_space=pltpu.SMEM)


def f32(*shape):
    return jax.ShapeDtypeStruct(shape, F32)


def params():
    return pltpu.CompilerParams(vmem_limit_bytes=VMEM_LIMIT)


def pack_kernel(layout, lists_ref, params_ref, out_ref):
    shared_rows, rows, pieces = layout
    band, epoch = lax.axis_index("band"), lax.axis_index("epoch")
    for b in range(BANDS):
        for q in range(len(pieces)):

            @pl.when((band == b) & (epoch == q))
            def _():
                for p, entry in enumerate(pieces[q]):
                    out_ref[p] = params_ref[row_of(b, entry)]

    tiles, slots = lists_ref.shape
    lane = lax.broadcasted_iota(jnp.int32, (8, 128), 1) % slots
    line = lax.broadcasted_iota(jnp.int32, (8, 128), 0)
    ids = jnp.zeros((8, 128), jnp.int32)
    for t in range(tiles):
        for s in range(slots):
            ids = jnp.where((line == t) & (lane == s), lists_ref[t, s], ids)
    out_ref[rows] = ids.astype(F32)


def select_kernel(layout, lists_ref, *refs):
    shared_rows, rows, pieces = layout
    out_ref, match_ref = refs[-2:]
    got = refs[:-2]
    owners = len(got)
    tiles, slots = lists_ref.shape
    blocks = got[0].shape[1]
    wide = tiles * slots
    me = lax.axis_index("tile")

    def slot_ids(shape):
        line = lax.broadcasted_iota(jnp.int32, shape, 0)
        ids = jnp.zeros(shape, jnp.int32)
        for t in range(tiles):
            for s in range(slots):
                ids = jnp.where(line == t * slots + s, lists_ref[t, s], ids)
        return ids

    shape = (wide, owners * blocks)
    lane = lax.broadcasted_iota(jnp.int32, shape, 1)
    held = lax.rem(me - lane // blocks + owners, owners) * blocks + lane % blocks
    choose = (slot_ids(shape) == held).astype(F32)
    for p in range(rows):
        everything = jnp.concatenate([ref[p] for ref in got], axis=0)
        out_ref[p] = pick(choose, everything)

    shape = (wide + blocks, tiles * owners * slots)
    line = lax.broadcasted_iota(jnp.int32, shape, 0)
    own = jnp.where(line < wide, slot_ids(shape), me * blocks + line - wide).astype(F32)
    sent = jnp.concatenate(
        [got[k][rows, t : t + 1, :slots] for t in range(tiles) for k in range(owners)], axis=1
    )
    match_ref[...] = (own == sent).astype(F32)


def tile_kernel(layout, tile, counts_ref, offsets_ref, psf_ref, data_ref, weight_ref, *refs):
    shared_rows, rows, pieces = layout
    epochs = len(pieces)
    ins, refs = refs[: 2 * epochs], refs[2 * epochs :]
    outs, refs = refs[: 2 * epochs], refs[2 * epochs :]
    shared, amps, derived, prof_x, prof_y, pieces_x, pieces_y, image, sums, half_out, other_out = refs
    band, epoch = lax.axis_index("band"), lax.axis_index("epoch")
    slots = shared.shape[2]
    pixels = data_ref.shape[-1]
    used = counts_ref[tile]

    for k in range(epochs):
        half_out[lax.rem(epoch - k + epochs, epochs)] = ins[k][...]
        other_out[lax.rem(epoch - k + epochs, epochs)] = ins[epochs + k][...]
    for q, piece in enumerate(pieces):
        for p, entry in enumerate(piece):
            if entry is None:
                continue
            kind, i = entry
            if kind == "s":
                shared[band, i] = half_out[q, p]
                shared[1 - band, i] = other_out[q, p]
            else:
                amps[i] = half_out[q, p]

    def shared_row(r):
        return shared[r // HALF, r % HALF]

    psf = psf_ref[0, 0]
    spacing = pixels / 8.0
    lead = [2 + k * COMPS for k in range(4)]
    for c in range(COMPS):
        dx, dy, lw, an = (shared_row(lead[k] + c) for k in range(4))
        derived[0, c] = spacing * shared_row(0) + dx
        derived[1, c] = spacing * shared_row(1) + dy
        derived[2, c] = (-0.5 * LOG2E) / (jnp.exp(2.0 * (lw + an)) + psf * psf)
        derived[3, c] = (-0.5 * LOG2E) / (jnp.exp(2.0 * (lw - an)) + psf * psf)
        derived[4, c] = amps[c]

    grid = lax.broadcasted_iota(jnp.int32, (pixels, 128), 0).astype(F32)

    def line(index, c, s):
        return derived[index, c, pl.ds(s, 1), :]

    def cut(x):
        hi = x.astype(BF16)
        return jnp.concatenate([hi, (x - hi.astype(F32)).astype(BF16)], axis=0)

    image[...] = jnp.zeros_like(image)

    def render(s, carry):
        off_x = offsets_ref[tile, s, 0].astype(F32)
        off_y = offsets_ref[tile, s, 1].astype(F32)
        for first in range(0, COMPS, 2):
            cut_x, cut_y = [], []
            for c in range(first, min(first + 2, COMPS)):
                d = grid - (line(0, c, s) + off_x)
                e = jnp.exp2(d * d * line(2, c, s))
                prof_x[s * COMPS + c] = e
                cut_x.append(cut(e))
                d = grid - (line(1, c, s) + off_y)
                e = jnp.exp2(d * d * line(3, c, s))
                prof_y[s * COMPS + c] = e
                cut_y.append(cut(e * line(4, c, s)))
            span = pl.ds(first * 128, 128 * len(cut_x))
            both_x, both_y = jnp.concatenate(cut_x, axis=1), jnp.concatenate(cut_y, axis=1)
            pieces_x[s, :, span] = both_x
            pieces_y[s, :, span] = both_y
            image[...] += lax.dot_general(
                both_x, both_y, (((1,), (1,)), ((), ())), preferred_element_type=F32
            )
        return carry

    lax.fori_loop(0, used, render, 0)

    model = (image[:pixels, :pixels] + image[pixels:, pixels:]) + (
        image[:pixels, pixels:] + image[pixels:, :pixels]
    )
    cotangent = weight_ref[0, 0, 0] * (model - data_ref[0, 0, 0])

    def stack(x):
        both = cut(x)
        return jnp.concatenate([both, both], axis=1)

    left_x, left_y = stack(cotangent), stack(cotangent.T)
    sums[...] = jnp.zeros_like(sums)

    def total(x):
        return jnp.sum(x, axis=0, keepdims=True)

    def pull(s, carry):
        off_x = offsets_ref[tile, s, 0].astype(F32)
        off_y = offsets_ref[tile, s, 1].astype(F32)
        for first in range(0, COMPS, 2):
            here = min(2, COMPS - first)
            span = pl.ds(first * 128, 128 * here)
            by_x = jnp.dot(left_x, pieces_y[s, :, span], preferred_element_type=F32)
            by_y = jnp.dot(left_y, pieces_x[s, :, span], preferred_element_type=F32)
            by_x = by_x[:pixels] + by_x[pixels:]
            by_y = by_y[:pixels] + by_y[pixels:]
            for n in range(here):
                c = first + n
                d = grid - (line(0, c, s) + off_x)
                g = prof_x[s * COMPS + c] * by_x[:, n * 128 : (n + 1) * 128]
                g1 = g * d
                sums[0, c, pl.ds(s, 1), :] = total(g1)
                sums[1, c, pl.ds(s, 1), :] = total(g1 * d)
                d = grid - (line(1, c, s) + off_y)
                g = prof_y[s * COMPS + c] * by_y[:, n * 128 : (n + 1) * 128]
                g1 = g * d
                sums[2, c, pl.ds(s, 1), :] = total(g1)
                sums[3, c, pl.ds(s, 1), :] = total(g1 * d)
                sums[4, c, pl.ds(s, 1), :] = total(g)
        return carry

    lax.fori_loop(0, used, pull, 0)

    live = lax.broadcasted_iota(jnp.int32, (slots, 128), 0) < used

    def keep(x):
        return jnp.where(live, x, 0.0)

    sum_x = sum_y = 0.0
    grads = {}
    for c in range(COMPS):
        lw, an = shared_row(lead[2] + c), shared_row(lead[3] + c)
        wide_x, wide_y = jnp.exp(2.0 * (lw + an)), jnp.exp(2.0 * (lw - an))
        inv_x, inv_y = 1.0 / (wide_x + psf * psf), 1.0 / (wide_y + psf * psf)
        amp = amps[c]
        dx = keep(sums[0, c] * inv_x)
        dy = keep(amp * sums[2, c] * inv_y)
        var_x = keep(sums[1, c] * inv_x * inv_x * wide_x)
        var_y = keep(amp * sums[3, c] * inv_y * inv_y * wide_y)
        sum_x, sum_y = sum_x + dx, sum_y + dy
        for k, value in enumerate((dx, dy, var_x + var_y, var_x - var_y)):
            grads[lead[k] + c] = value
    grads[0], grads[1] = spacing * sum_x, spacing * sum_y
    for r, value in grads.items():
        shared[r // HALF, r % HALF] = value
    for q, piece in enumerate(pieces):
        for p, entry in enumerate(piece):
            if entry is None:
                half_out[q, p] = jnp.zeros((slots, 128), F32)
            elif entry[0] == "s":
                half_out[q, p] = shared[band, entry[1]]
            else:
                half_out[q, p] = keep(sums[4, entry[1]])
            if p < shared_rows:
                if entry is not None and entry[0] == "s":
                    other_out[q, p] = shared[1 - band, entry[1]]
                else:
                    other_out[q, p] = jnp.zeros((slots, 128), F32)
    for k in range(epochs):
        outs[k][...] = half_out[lax.rem(epoch + k, epochs)]
        outs[epochs + k][...] = other_out[lax.rem(epoch + k, epochs)]


def tile_gradient(layout, tile, counts, offsets, psf, data, weight, slot_rows):
    shared_rows, rows, pieces = layout
    epochs = len(pieces)
    slots = offsets.shape[1]
    pixels = data.shape[-1]
    shapes = [(rows, slots, 128)] * epochs + [(shared_rows, slots, 128)] * epochs
    image = pl.BlockSpec((1, 1, 1, pixels, pixels), lambda i: (tile, 0, 0, 0, 0))
    return pl.pallas_call(
        functools.partial(tile_kernel, layout, tile),
        grid=(1,),
        out_shape=[f32(*s) for s in shapes],
        in_specs=[smem(), smem(), smem(), image, image]
        + [pl.BlockSpec(s, lambda i: (0, tile, 0)) for s in shapes],
        out_specs=[pl.BlockSpec(s, lambda i: (0, 0, 0)) for s in shapes],
        scratch_shapes=[
            pltpu.VMEM((BANDS, HALF, slots, 128), F32),
            pltpu.VMEM((COMPS, slots, 128), F32),
            pltpu.VMEM((5, COMPS, slots, 128), F32),
            pltpu.VMEM((slots * COMPS, pixels, 128), F32),
            pltpu.VMEM((slots * COMPS, pixels, 128), F32),
            pltpu.VMEM((slots, 2 * pixels, COMPS * 128), BF16),
            pltpu.VMEM((slots, 2 * pixels, COMPS * 128), BF16),
            pltpu.VMEM((2 * pixels, 2 * pixels), F32),
            pltpu.VMEM((5, COMPS, slots, 128), F32),
            pltpu.VMEM((epochs, rows, slots, 128), F32),
            pltpu.VMEM((epochs, shared_rows, slots, 128), F32),
        ],
        compiler_params=params(),
        name=f"tile_{tile}",
    )(counts, offsets, psf, data, weight, *slot_rows)


def scale_of(p):
    first = (lax.axis_index("band") == 0) & (lax.axis_index("epoch") == 0)
    if p < 2:
        return jnp.where(first, F32(STEP / 64.0), F32(STEP))
    return F32(STEP)


def combine_kernel(rows, tiles, match_ref, slots_ref, own_ref, *refs):
    got, (new_slots, new_own) = refs[:-2], refs[-2:]
    wide = slots_ref.shape[1]
    match = match_ref[...]
    for p in range(rows):
        both = pick(match, jnp.concatenate([ref[p] for ref in got], axis=0)) * scale_of(p)
        new_slots[p] = slots_ref[p] - both[:wide]
        new_own[p] = own_ref[p] - both[wide:]


def dense_kernel(rows, lists_ref, *refs):
    tiles, slots = lists_ref.shape
    grads, outs = refs[:tiles], refs[tiles:]
    owners, blocks = len(outs), outs[0].shape[1]
    shape = (owners * blocks, tiles * slots)
    line = lax.broadcasted_iota(jnp.int32, shape, 0)
    lane = lax.broadcasted_iota(jnp.int32, shape, 1)
    me = lax.axis_index("tile")
    target = lax.rem(me + line // blocks, owners) * blocks + line % blocks
    ids = jnp.zeros(shape, jnp.int32)
    for t in range(tiles):
        for s in range(slots):
            ids = jnp.where(lane == t * slots + s, lists_ref[t, s], ids)
    match = (ids == target).astype(F32)
    for p in range(rows):
        dense = pick(match, jnp.concatenate([ref[p] for ref in grads], axis=0))
        for k, out in enumerate(outs):
            out[p] = dense[k * blocks : (k + 1) * blocks]


def update_kernel(rows, own_ref, *refs):
    got, out_ref = refs[:-1], refs[-1]
    for p in range(rows):
        out_ref[p] = own_ref[p] - scale_of(p) * functools.reduce(lambda a, b: a + b, [g[p] for g in got])


def final_kernel(layout, *refs):
    shared_rows, rows, pieces = layout
    epochs = len(pieces)
    ins, (out_ref, held) = refs[: 2 * epochs], refs[2 * epochs :]
    band, epoch = lax.axis_index("band"), lax.axis_index("epoch")
    for k in range(epochs):
        q = lax.rem(epoch - k + epochs, epochs)
        held[band, q] = ins[k][...]
        held[1 - band, q] = ins[epochs + k][...]
    for b in range(BANDS):
        for q, piece in enumerate(pieces):
            for p, entry in enumerate(piece):
                if entry is not None:
                    out_ref[row_of(b, entry)] = held[b, q, p]


def shards(source_params, pixel_data, pixel_weight, psf_width, block_lists, block_counts, block_offsets):
    owners, epochs = lax.axis_size("tile"), lax.axis_size("epoch")
    blocks, param_rows, sources = source_params.shape
    tiles, slots = block_lists.shape
    wide = tiles * slots
    layout = quarter_layout(epochs)
    shared_rows, rows, pieces = layout

    def to_peers(same, other):
        kept = [same[0]]
        for k in range(1, epochs):
            kept.append(lax.ppermute(same[k], "epoch", [(i, (i + k) % epochs) for i in range(epochs)]))
        for k in range(epochs):
            pairs = [
                (i * BANDS + b, (i + k) % epochs * BANDS + 1 - b)
                for i in range(epochs)
                for b in range(BANDS)
            ]
            kept.append(lax.ppermute(other[k], ("epoch", "band"), pairs))
        return kept

    def round_tiles(arrays):
        return [arrays[0]] + [
            lax.ppermute(arrays[k], "tile", [(i, (i + k) % owners) for i in range(owners)])
            for k in range(1, owners)
        ]

    def spread(piece, other_rows):
        return to_peers([piece] * epochs, [piece[:other_rows]] * epochs)

    def summed(parts):
        near = functools.reduce(lambda a, b: a + b, parts[:epochs])
        far = functools.reduce(lambda a, b: a + b, parts[epochs:])
        return near + jnp.pad(far, ((0, rows - shared_rows), (0, 0), (0, 0)))

    by_row = jnp.transpose(source_params, (1, 0, 2))
    packed = pl.pallas_call(
        functools.partial(pack_kernel, layout),
        out_shape=f32(rows + 1, blocks, sources),
        in_specs=[smem(), vmem()],
        out_specs=vmem(),
        compiler_params=params(),
        name="pack",
    )(block_lists, by_row)
    got = round_tiles([packed] * owners)
    slot_piece, match = pl.pallas_call(
        functools.partial(select_kernel, layout),
        out_shape=[f32(rows, wide, sources), f32(wide + blocks, owners * wide)],
        in_specs=[smem()] + [vmem()] * owners,
        out_specs=[vmem()] * 2,
        compiler_params=params(),
        name="select",
    )(block_lists, *got)
    own_piece = packed[:rows]

    for step in range(ITERS):
        slot_rows = spread(slot_piece, shared_rows)
        tile_sums = []
        for t in range(tiles):
            parts = tile_gradient(
                layout, t, block_counts, block_offsets, psf_width, pixel_data, pixel_weight, slot_rows
            )
            tile_sums.append(summed(to_peers(parts[:epochs], parts[epochs:])))
        if step < ITERS - 1:
            got = []
            for t in range(tiles):
                got += round_tiles([tile_sums[t]] * owners)
            slot_piece, own_piece = pl.pallas_call(
                functools.partial(combine_kernel, rows, tiles),
                out_shape=[f32(rows, wide, sources), f32(rows, blocks, sources)],
                in_specs=[vmem()] * (3 + len(got)),
                out_specs=[vmem()] * 2,
                compiler_params=params(),
                name="combine",
            )(match, slot_piece, own_piece, *got)
        else:
            dense = pl.pallas_call(
                functools.partial(dense_kernel, rows),
                out_shape=[f32(rows, blocks, sources)] * owners,
                in_specs=[smem()] + [vmem()] * tiles,
                out_specs=[vmem()] * owners,
                compiler_params=params(),
                name="dense",
            )(block_lists, *tile_sums)
            got = round_tiles(dense)
            own_piece = pl.pallas_call(
                functools.partial(update_kernel, rows),
                out_shape=f32(rows, blocks, sources),
                in_specs=[vmem()] * (1 + owners),
                out_specs=vmem(),
                compiler_params=params(),
                name="update",
            )(own_piece, *got)
    whole = pl.pallas_call(
        functools.partial(final_kernel, layout),
        out_shape=f32(param_rows, blocks, sources),
        in_specs=[vmem()] * (2 * epochs),
        out_specs=vmem(),
        scratch_shapes=[pltpu.VMEM((BANDS, epochs, rows, blocks, sources), F32)],
        compiler_params=params(),
        name="final",
    )(*spread(own_piece, rows))
    return jnp.transpose(whole, (1, 0, 2))


def solution(mesh):
    return jax.shard_map(
        shards,
        mesh=mesh,
        in_specs=(
            P(("region", "tile"), None, None),
            P(("region", "tile"), "epoch", "band", None, None),
            P(("region", "tile"), "epoch", "band", None, None),
            P(("region", "epoch"), "band"),
            P(("region", "tile"), None),
            P(("region", "tile")),
            P(("region", "tile"), None, None),
        ),
        out_specs=P(("region", "tile"), None, None),
        check_vma=False,
    )
```

```python
import functools
import math

import jax
import jax.numpy as jnp
from jax import lax
from jax.experimental import pallas as pl
from jax.experimental.pallas import tpu as pltpu
from jax.sharding import PartitionSpec as P

ITERS = 2
STEP = 0.005
POSITION_RATE = 1.0 / 64.0
COMPS = 7
BANDS = 2
SHARED = 4 * COMPS
HALF = SHARED // BANDS
LOG2E = math.log2(math.e)
F32 = jnp.float32
BF16 = jnp.bfloat16
MIB = 1024 * 1024


def quarter_layout(epochs):
    shared_rows = -(-HALF // epochs)
    rows = -(-(HALF + COMPS) // epochs)
    pieces, amp = [], 0
    for q in range(epochs):
        piece = [("s", i) for i in range(q * shared_rows, min((q + 1) * shared_rows, HALF))]
        while len(piece) < rows and amp < COMPS:
            piece.append(("a", amp))
            amp += 1
        pieces.append(piece + [None] * (rows - len(piece)))
    return shared_rows, rows, pieces


def row_of(band, entry):
    kind, i = entry
    if kind == "a":
        return 2 + 6 * i + 4 + band, None
    k, c = divmod(HALF * band + i, COMPS)
    return 2 + 6 * c + k, (k if k < 2 else None)


def split3(x):
    hi = x.astype(BF16)
    rest = x - hi.astype(F32)
    mid = rest.astype(BF16)
    low = (rest - mid.astype(F32)).astype(BF16)
    return jnp.concatenate([hi, mid, low], axis=0)


def pick(matrix, rows):
    wide = jnp.concatenate([matrix, matrix, matrix], axis=1).astype(BF16)
    return jnp.dot(wide, split3(rows), preferred_element_type=F32)


def vmem():
    return pl.BlockSpec(memory_space=pltpu.VMEM)


def smem():
    return pl.BlockSpec(memory_space=pltpu.SMEM)


def f32(*shape):
    return jax.ShapeDtypeStruct(shape, F32)


def params(mib=4):
    return pltpu.CompilerParams(vmem_limit_bytes=mib * MIB)


def pack_kernel(layout, spacing, lists_ref, params_ref, out_ref):
    shared_rows, rows, pieces = layout
    band, epoch = lax.axis_index("band"), lax.axis_index("epoch")
    for b in range(BANDS):
        for q in range(len(pieces)):

            @pl.when((band == b) & (epoch == q))
            def _():
                for p, entry in enumerate(pieces[q]):
                    if entry is None:
                        out_ref[p] = jnp.zeros(out_ref.shape[1:], F32)
                        continue
                    row, position = row_of(b, entry)
                    value = params_ref[row]
                    if position is not None:
                        value = spacing * params_ref[position] + value
                    out_ref[p] = value

    tiles, slots = lists_ref.shape
    lane = lax.broadcasted_iota(jnp.int32, (8, 128), 1)
    ids = jnp.zeros((8, 128), jnp.int32)
    for t in range(tiles):
        for s in range(slots):
            ids = jnp.where(lane == t * slots + s, lists_ref[t, s], ids)
    out_ref[rows] = ids.astype(F32)


def select_kernel(layout, lists_ref, *refs):
    shared_rows, rows, pieces = layout
    got, (out_ref, short_ref, match_ref) = refs[:-3], refs[-3:]
    owners = len(got)
    tiles, slots = lists_ref.shape
    blocks = got[0].shape[1]
    wide = tiles * slots
    me = lax.axis_index("tile")

    def slot_ids(shape):
        line = lax.broadcasted_iota(jnp.int32, shape, 0)
        ids = jnp.zeros(shape, jnp.int32)
        for t in range(tiles):
            for s in range(slots):
                ids = jnp.where(line == t * slots + s, lists_ref[t, s], ids)
        return ids

    shape = (wide, owners * blocks)
    lane = lax.broadcasted_iota(jnp.int32, shape, 1)
    held = lax.rem(me - lane // blocks + owners, owners) * blocks + lane % blocks
    choose = (slot_ids(shape) == held).astype(F32)
    for p in range(rows):
        chosen = pick(choose, jnp.concatenate([ref[p] for ref in got], axis=0))
        out_ref[p] = chosen
        if p < shared_rows:
            short_ref[p] = chosen

    shape = (wide + blocks, owners * wide)
    line = lax.broadcasted_iota(jnp.int32, shape, 0)
    own = jnp.where(line < wide, slot_ids(shape), me * blocks + line - wide).astype(F32)
    sent = jnp.concatenate([ref[rows, :1, :wide] for ref in got], axis=1)
    match_ref[...] = (own == sent).astype(F32)


def put_together(layout, band, epoch, ins, half, other, shared, amps):
    shared_rows, rows, pieces = layout
    epochs = len(pieces)
    for k in range(epochs):
        q = lax.rem(epoch - k + epochs, epochs)
        half[q] = ins[k][...]
        other[q] = ins[epochs + k][...]
    for q, piece in enumerate(pieces):
        for p, entry in enumerate(piece):
            if entry is None:
                continue
            kind, i = entry
            if kind == "s":
                shared[band, i] = half[q, p]
                shared[1 - band, i] = other[q, p]
            else:
                amps[i] = half[q, p]


def step_kernel(layout, later, counts_ref, offsets_ref, psf_ref, data_ref, weight_ref, *refs):
    shared_rows, rows, pieces = layout
    epochs = len(pieces)
    taken = 2 * epochs * (2 if later else 1)
    ins, refs = refs[:taken], refs[taken:]
    outs, refs = refs[: 2 * epochs], refs[2 * epochs :]
    shared, amps, derived, prof_x, prof_y, pieces_x, pieces_y, image, sums, half, other = refs[:11]
    band, epoch = lax.axis_index("band"), lax.axis_index("epoch")
    tiles = data_ref.shape[0]
    pixels = data_ref.shape[-1]
    wide = shared.shape[2]
    slots = wide // tiles
    spacing = pixels / 8.0

    put_together(layout, band, epoch, ins[: 2 * epochs], half, other, shared, amps)

    def row(k, c):
        r = k * COMPS + c
        return r // HALF, r % HALF

    if later:
        moved, moved_amps = refs[11:]
        put_together(layout, band, epoch, ins[2 * epochs :], half, other, moved, moved_amps)
        for k in range(4):
            shift = 0.0
            if k < 2:
                shift = functools.reduce(lambda a, b: a + b, [moved[row(k, c)] for c in range(COMPS)])
                shift = shift * (spacing * spacing * POSITION_RATE)
            for c in range(COMPS):
                shared[row(k, c)] = shared[row(k, c)] - STEP * (moved[row(k, c)] + shift)
        for c in range(COMPS):
            amps[c] = amps[c] - STEP * moved_amps[c]

    psf = psf_ref[0, 0]
    line_of = lax.broadcasted_iota(jnp.int32, (wide, 128), 0)
    live = jnp.zeros((wide, 128), jnp.bool_)
    for t in range(tiles):
        live = live | ((line_of >= t * slots) & (line_of < t * slots + counts_ref[t]))
    for c in range(COMPS):
        lw, an = shared[row(2, c)], shared[row(3, c)]
        derived[0, c] = shared[row(0, c)]
        derived[1, c] = shared[row(1, c)]
        derived[2, c] = (-0.5 * LOG2E) / (jnp.exp(2.0 * (lw + an)) + psf * psf)
        derived[3, c] = (-0.5 * LOG2E) / (jnp.exp(2.0 * (lw - an)) + psf * psf)
        derived[4, c] = jnp.where(live, amps[c], 0.0)
    sums[...] = jnp.zeros_like(sums)

    grid = lax.broadcasted_iota(jnp.int32, (pixels, 128), 0).astype(F32)

    def cut(x):
        hi = x.astype(BF16)
        return jnp.concatenate([hi, (x - hi.astype(F32)).astype(BF16)], axis=0)

    def stack(x):
        both = cut(x)
        return jnp.concatenate([both, both], axis=1)

    def total(x):
        return jnp.sum(x, axis=0, keepdims=True)

    def line(index, c, s):
        return derived[index, c, pl.ds(s, 1), :]

    together = 2
    for t in range(tiles):
        trips = (counts_ref[t] + together - 1) // together
        image[...] = jnp.zeros_like(image)

        def render(i, carry):
            for u in range(together):
                s = i * together + u
                g = t * slots + s
                off_x = offsets_ref[t, 0, s].astype(F32)
                off_y = offsets_ref[t, 1, s].astype(F32)
                for c in range(COMPS):
                    d = grid - (line(0, c, g) + off_x)
                    e = jnp.exp2(d * d * line(2, c, g))
                    prof_x[s * COMPS + c] = e
                    pieces_x[s, :, c * 128 : (c + 1) * 128] = cut(e)
                    d = grid - (line(1, c, g) + off_y)
                    e = jnp.exp2(d * d * line(3, c, g))
                    prof_y[s * COMPS + c] = e
                    pieces_y[s, :, c * 128 : (c + 1) * 128] = cut(e * line(4, c, g))
                image[...] += lax.dot_general(
                    pieces_x[s], pieces_y[s], (((1,), (1,)), ((), ())), preferred_element_type=F32
                )
            return carry

        lax.fori_loop(0, trips, render, 0)

        model = (image[:pixels, :pixels] + image[pixels:, pixels:]) + (
            image[:pixels, pixels:] + image[pixels:, :pixels]
        )
        cotangent = weight_ref[t, 0, 0] * (model - data_ref[t, 0, 0])
        left_x, left_y = stack(cotangent), stack(cotangent.T)

        def pull(i, carry):
            for u in range(together):
                s = i * together + u
                g = t * slots + s
                off_x = offsets_ref[t, 0, s].astype(F32)
                off_y = offsets_ref[t, 1, s].astype(F32)
                for first in range(0, COMPS, 2):
                    here = min(2, COMPS - first)
                    span = pl.ds(first * 128, 128 * here)
                    by_x = jnp.dot(left_x, pieces_y[s, :, span], preferred_element_type=F32)
                    by_y = jnp.dot(left_y, pieces_x[s, :, span], preferred_element_type=F32)
                    by_x = by_x[:pixels] + by_x[pixels:]
                    by_y = by_y[:pixels] + by_y[pixels:]
                    for n in range(here):
                        c = first + n
                        d = grid - (line(0, c, g) + off_x)
                        e = prof_x[s * COMPS + c] * by_x[:, n * 128 : (n + 1) * 128]
                        e1 = e * d
                        sums[0, c, pl.ds(g, 1), :] = total(e1)
                        sums[1, c, pl.ds(g, 1), :] = total(e1 * d)
                        d = grid - (line(1, c, g) + off_y)
                        e = prof_y[s * COMPS + c] * by_y[:, n * 128 : (n + 1) * 128]
                        e1 = e * d
                        sums[2, c, pl.ds(g, 1), :] = total(e1)
                        sums[3, c, pl.ds(g, 1), :] = total(e1 * d)
                        sums[4, c, pl.ds(g, 1), :] = total(e)
            return carry

        lax.fori_loop(0, trips, pull, 0)

    def keep(x):
        return jnp.where(live, x, 0.0)

    for c in range(COMPS):
        lw, an = shared[row(2, c)], shared[row(3, c)]
        wide_x, wide_y = jnp.exp(2.0 * (lw + an)), jnp.exp(2.0 * (lw - an))
        inv_x, inv_y = 1.0 / (wide_x + psf * psf), 1.0 / (wide_y + psf * psf)
        amp = amps[c]
        var_x = keep(sums[1, c] * inv_x * inv_x * wide_x)
        var_y = keep(amp * sums[3, c] * inv_y * inv_y * wide_y)
        shared[row(0, c)] = keep(sums[0, c] * inv_x)
        shared[row(1, c)] = keep(amp * sums[2, c] * inv_y)
        shared[row(2, c)] = var_x + var_y
        shared[row(3, c)] = var_x - var_y
        amps[c] = keep(sums[4, c])
    none = jnp.zeros((wide, 128), F32)
    for q, piece in enumerate(pieces):
        for p, entry in enumerate(piece):
            is_shared = entry is not None and entry[0] == "s"
            if is_shared:
                half[q, p] = shared[band, entry[1]]
            else:
                half[q, p] = none if entry is None else amps[entry[1]]
            if p < shared_rows:
                other[q, p] = shared[1 - band, entry[1]] if is_shared else none
    for k in range(epochs):
        outs[k][...] = half[lax.rem(epoch + k, epochs)]
        outs[epochs + k][...] = other[lax.rem(epoch + k, epochs)]


def step_gradient(layout, counts, offsets, psf, data, weight, slot_rows, moved):
    shared_rows, rows, pieces = layout
    epochs = len(pieces)
    later = moved is not None
    tiles, _, slots = offsets.shape
    pixels = data.shape[-1]
    wide = tiles * slots
    shapes = [(rows, wide, 128)] * epochs + [(shared_rows, wide, 128)] * epochs
    ins = slot_rows + (moved or [])
    together = [pltpu.VMEM((BANDS, HALF, wide, 128), F32), pltpu.VMEM((COMPS, wide, 128), F32)]
    return pl.pallas_call(
        functools.partial(step_kernel, layout, later),
        out_shape=[f32(*s) for s in shapes],
        in_specs=[smem()] * 3 + [vmem()] * (2 + len(ins)),
        out_specs=[vmem()] * len(shapes),
        scratch_shapes=together
        + [
            pltpu.VMEM((5, COMPS, wide, 128), F32),
            pltpu.VMEM((slots * COMPS, pixels, 128), F32),
            pltpu.VMEM((slots * COMPS, pixels, 128), F32),
            pltpu.VMEM((slots, 2 * pixels, COMPS * 128), BF16),
            pltpu.VMEM((slots, 2 * pixels, COMPS * 128), BF16),
            pltpu.VMEM((2 * pixels, 2 * pixels), F32),
            pltpu.VMEM((5, COMPS, wide, 128), F32),
            pltpu.VMEM((epochs, rows, wide, 128), F32),
            pltpu.VMEM((epochs, shared_rows, wide, 128), F32),
        ]
        + (together if later else []),
        compiler_params=params(32),
        name="later_step" if later else "first_step",
    )(counts, offsets, psf, data, weight, *ins)


def combine_kernel(layout, match_ref, *refs):
    shared_rows, rows, pieces = layout
    got, (out_ref, short_ref, own_ref) = refs[:-3], refs[-3:]
    wide = out_ref.shape[1]
    match = match_ref[...]
    for p in range(rows):
        both = pick(match, jnp.concatenate([ref[p] for ref in got], axis=0))
        out_ref[p] = both[:wide]
        if p < shared_rows:
            short_ref[p] = both[:wide]
        own_ref[p] = both[wide:]


def dense_kernel(rows, lists_ref, grads, *outs):
    tiles, slots = lists_ref.shape
    owners, blocks = len(outs), outs[0].shape[1]
    shape = (owners * blocks, tiles * slots)
    line = lax.broadcasted_iota(jnp.int32, shape, 0)
    lane = lax.broadcasted_iota(jnp.int32, shape, 1)
    me = lax.axis_index("tile")
    target = lax.rem(me + line // blocks, owners) * blocks + line % blocks
    ids = jnp.zeros(shape, jnp.int32)
    for t in range(tiles):
        for s in range(slots):
            ids = jnp.where(lane == t * slots + s, lists_ref[t, s], ids)
    match = (ids == target).astype(F32)
    for p in range(rows):
        dense = pick(match, grads[p])
        for k, out in enumerate(outs):
            out[p] = dense[k * blocks : (k + 1) * blocks]


def final_kernel(layout, spacing, params_ref, *refs):
    shared_rows, rows, pieces = layout
    epochs = len(pieces)
    ins, (out_ref, held) = refs[: 2 * epochs], refs[2 * epochs :]
    band, epoch = lax.axis_index("band"), lax.axis_index("epoch")
    for k in range(epochs):
        q = lax.rem(epoch - k + epochs, epochs)
        held[band, q] = ins[k][...]
        held[1 - band, q] = ins[epochs + k][...]
    shift = [0.0, 0.0]
    for b in range(BANDS):
        for q, piece in enumerate(pieces):
            for p, entry in enumerate(piece):
                if entry is None:
                    continue
                row, position = row_of(b, entry)
                grad = held[b, q, p]
                out_ref[row] = params_ref[row] - STEP * grad
                if position is not None:
                    shift[position] = shift[position] + grad
    for k in range(2):
        out_ref[k] = params_ref[k] - (STEP * POSITION_RATE * spacing) * shift[k]


def shards(source_params, pixel_data, pixel_weight, psf_width, block_lists, block_counts, block_offsets):
    owners, epochs = lax.axis_size("tile"), lax.axis_size("epoch")
    blocks, param_rows, sources = source_params.shape
    tiles, slots = block_lists.shape
    wide = tiles * slots
    spacing = pixel_data.shape[-1] / 8.0
    layout = quarter_layout(epochs)
    shared_rows, rows, pieces = layout

    def to_peers(same, other):
        kept = [same[0]]
        for k in range(1, epochs):
            kept.append(lax.ppermute(same[k], "epoch", [(i, (i + k) % epochs) for i in range(epochs)]))
        for k in range(epochs):
            pairs = [
                (i * BANDS + b, (i + k) % epochs * BANDS + 1 - b)
                for i in range(epochs)
                for b in range(BANDS)
            ]
            kept.append(lax.ppermute(other[k], ("epoch", "band"), pairs))
        return kept

    def round_tiles(arrays):
        return [arrays[0]] + [
            lax.ppermute(arrays[k], "tile", [(i, (i + k) % owners) for i in range(owners)])
            for k in range(1, owners)
        ]

    def spread(piece, other):
        return to_peers([piece] * epochs, [other] * epochs)

    def summed(parts):
        near = functools.reduce(lambda a, b: a + b, parts[:epochs])
        far = functools.reduce(lambda a, b: a + b, parts[epochs:])
        return near + jnp.pad(far, ((0, rows - shared_rows), (0, 0), (0, 0)))

    by_row = jnp.transpose(source_params, (1, 0, 2))
    offsets = jnp.transpose(block_offsets, (0, 2, 1))
    packed = pl.pallas_call(
        functools.partial(pack_kernel, layout, spacing),
        out_shape=f32(rows + 1, blocks, sources),
        in_specs=[smem(), vmem()],
        out_specs=vmem(),
        compiler_params=params(),
        name="pack",
    )(block_lists, by_row)
    got = round_tiles([packed] * owners)
    slot_piece, slot_short, match = pl.pallas_call(
        functools.partial(select_kernel, layout),
        out_shape=[
            f32(rows, wide, sources),
            f32(shared_rows, wide, sources),
            f32(wide + blocks, owners * wide),
        ],
        in_specs=[smem()] + [vmem()] * owners,
        out_specs=[vmem()] * 3,
        compiler_params=params(),
        name="select",
    )(block_lists, *got)
    slot_rows = spread(slot_piece, slot_short)

    def gradient(moved):
        parts = step_gradient(
            layout, block_counts, offsets, psf_width, pixel_data, pixel_weight, slot_rows, moved
        )
        return summed(to_peers(parts[:epochs], parts[epochs:]))

    got = round_tiles([gradient(None)] * owners)
    slot_piece, slot_short, own_first = pl.pallas_call(
        functools.partial(combine_kernel, layout),
        out_shape=[
            f32(rows, wide, sources),
            f32(shared_rows, wide, sources),
            f32(rows, blocks, sources),
        ],
        in_specs=[vmem()] * (1 + owners),
        out_specs=[vmem()] * 3,
        compiler_params=params(),
        name="combine",
    )(match, *got)

    dense = pl.pallas_call(
        functools.partial(dense_kernel, rows),
        out_shape=[f32(rows, blocks, sources)] * owners,
        in_specs=[smem(), vmem()],
        out_specs=[vmem()] * owners,
        compiler_params=params(),
        name="dense",
    )(block_lists, gradient(spread(slot_piece, slot_short)))
    own = functools.reduce(lambda a, b: a + b, round_tiles(dense), own_first)
    whole = pl.pallas_call(
        functools.partial(final_kernel, layout, spacing),
        out_shape=f32(param_rows, blocks, sources),
        in_specs=[vmem()] * (1 + 2 * epochs),
        out_specs=vmem(),
        scratch_shapes=[pltpu.VMEM((BANDS, epochs, rows, blocks, sources), F32)],
        compiler_params=params(),
        name="final",
    )(by_row, *spread(own, own))
    return jnp.transpose(whole, (1, 0, 2))


def solution(mesh):
    return jax.shard_map(
        shards,
        mesh=mesh,
        in_specs=(
            P(("region", "tile"), None, None),
            P(("region", "tile"), "epoch", "band", None, None),
            P(("region", "tile"), "epoch", "band", None, None),
            P(("region", "epoch"), "band"),
            P(("region", "tile"), None),
            P(("region", "tile")),
            P(("region", "tile"), None, None),
        ),
        out_specs=P(("region", "tile"), None, None),
        check_vma=False,
    )
```

```python
import functools
import math

import jax
import jax.numpy as jnp
from jax import lax
from jax.experimental import pallas as pl
from jax.experimental.pallas import tpu as pltpu
from jax.sharding import PartitionSpec as P

ITERS = 2
STEP = 0.005
POSITION_RATE = 1.0 / 64.0
COMPS = 7
BANDS = 2
TOGETHER = 2
SHARED = 4 * COMPS
HALF = SHARED // BANDS
LOG2E = math.log2(math.e)
F32 = jnp.float32
BF16 = jnp.bfloat16
MIB = 1024 * 1024


def quarter_layout(epochs):
    shared_rows = -(-HALF // epochs)
    rows = -(-(HALF + COMPS) // epochs)
    pieces, amp = [], 0
    for q in range(epochs):
        piece = [("s", i) for i in range(q * shared_rows, min((q + 1) * shared_rows, HALF))]
        while len(piece) < rows and amp < COMPS:
            piece.append(("a", amp))
            amp += 1
        pieces.append(piece + [None] * (rows - len(piece)))
    return shared_rows, rows, pieces


def row_of(band, entry):
    kind, i = entry
    if kind == "a":
        return 2 + 6 * i + 4 + band, None
    k, c = divmod(HALF * band + i, COMPS)
    return 2 + 6 * c + k, (k if k < 2 else None)


def split3(x):
    hi = x.astype(BF16)
    rest = x - hi.astype(F32)
    mid = rest.astype(BF16)
    low = (rest - mid.astype(F32)).astype(BF16)
    return jnp.concatenate([hi, mid, low], axis=0)


def pick(matrix, rows):
    wide = jnp.concatenate([matrix, matrix, matrix], axis=1).astype(BF16)
    return jnp.dot(wide, split3(rows), preferred_element_type=F32)


def vmem():
    return pl.BlockSpec(memory_space=pltpu.VMEM)


def smem():
    return pl.BlockSpec(memory_space=pltpu.SMEM)


def f32(*shape):
    return jax.ShapeDtypeStruct(shape, F32)


def params(mib=4):
    return pltpu.CompilerParams(vmem_limit_bytes=mib * MIB)


def pack_kernel(layout, spacing, lists_ref, params_ref, out_ref):
    shared_rows, rows, pieces = layout
    band, epoch = lax.axis_index("band"), lax.axis_index("epoch")
    for b in range(BANDS):
        for q in range(len(pieces)):

            @pl.when((band == b) & (epoch == q))
            def _():
                for p, entry in enumerate(pieces[q]):
                    if entry is None:
                        out_ref[p] = jnp.zeros(out_ref.shape[1:], F32)
                        continue
                    row, position = row_of(b, entry)
                    value = params_ref[row]
                    if position is not None:
                        value = spacing * params_ref[position] + value
                    out_ref[p] = value

    tiles, slots = lists_ref.shape
    lane = lax.broadcasted_iota(jnp.int32, (8, 128), 1)
    ids = jnp.zeros((8, 128), jnp.int32)
    for t in range(tiles):
        for s in range(slots):
            ids = jnp.where(lane == t * slots + s, lists_ref[t, s], ids)
    out_ref[rows] = ids.astype(F32)


def select_kernel(layout, lists_ref, *refs):
    shared_rows, rows, pieces = layout
    got_ref, out_ref, short_ref, match_ref = refs
    owners, _, blocks, _ = got_ref.shape
    tiles, slots = lists_ref.shape
    wide = tiles * slots
    me = lax.axis_index("tile")

    def slot_ids(shape):
        line = lax.broadcasted_iota(jnp.int32, shape, 0)
        ids = jnp.zeros(shape, jnp.int32)
        for t in range(tiles):
            for s in range(slots):
                ids = jnp.where(line == t * slots + s, lists_ref[t, s], ids)
        return ids

    shape = (wide, owners * blocks)
    choose = (slot_ids(shape) == lax.broadcasted_iota(jnp.int32, shape, 1)).astype(F32)
    for p in range(rows):
        chosen = pick(choose, jnp.concatenate([got_ref[k, p] for k in range(owners)], axis=0))
        out_ref[p] = chosen
        if p < shared_rows:
            short_ref[p] = chosen

    shape = (wide + blocks, owners * wide)
    line = lax.broadcasted_iota(jnp.int32, shape, 0)
    own = jnp.where(line < wide, slot_ids(shape), me * blocks + line - wide).astype(F32)
    sent = jnp.concatenate([got_ref[k, rows, :1, :wide] for k in range(owners)], axis=1)
    match_ref[...] = (own == sent).astype(F32)


def put_together(layout, band, epoch, ins, half, other, shared, amps):
    shared_rows, rows, pieces = layout
    epochs = len(pieces)
    for k in range(epochs):
        q = lax.rem(epoch - k + epochs, epochs)
        half[q] = ins[k][...]
        other[q] = ins[epochs + k][...]
    for q, piece in enumerate(pieces):
        for p, entry in enumerate(piece):
            if entry is None:
                continue
            kind, i = entry
            if kind == "s":
                shared[band, i] = half[q, p]
                shared[1 - band, i] = other[q, p]
            else:
                amps[i] = half[q, p]


def step_kernel(layout, later, counts_ref, offsets_ref, psf_ref, data_ref, weight_ref, *refs):
    shared_rows, rows, pieces = layout
    epochs = len(pieces)
    taken = 2 * epochs * (2 if later else 1)
    ins, refs = refs[:taken], refs[taken:]
    outs, refs = refs[: 2 * epochs], refs[2 * epochs :]
    shared, amps, derived, prof_x, prof_y, pieces_x, pieces_y, image, sums, half, other = refs[:11]
    band, epoch = lax.axis_index("band"), lax.axis_index("epoch")
    tiles = data_ref.shape[0]
    pixels = data_ref.shape[-1]
    wide = shared.shape[2]
    slots = wide // tiles
    spacing = pixels / 8.0

    put_together(layout, band, epoch, ins[: 2 * epochs], half, other, shared, amps)

    def row(k, c):
        r = k * COMPS + c
        return r // HALF, r % HALF

    if later:
        moved, moved_amps = refs[11:]
        put_together(layout, band, epoch, ins[2 * epochs :], half, other, moved, moved_amps)
        for k in range(4):
            shift = 0.0
            if k < 2:
                shift = functools.reduce(lambda a, b: a + b, [moved[row(k, c)] for c in range(COMPS)])
                shift = shift * (spacing * spacing * POSITION_RATE)
            for c in range(COMPS):
                shared[row(k, c)] = shared[row(k, c)] - STEP * (moved[row(k, c)] + shift)
        for c in range(COMPS):
            amps[c] = amps[c] - STEP * moved_amps[c]

    psf = psf_ref[0, 0]
    line_of = lax.broadcasted_iota(jnp.int32, (wide, 128), 0)
    live = jnp.zeros((wide, 128), jnp.bool_)
    for t in range(tiles):
        live = live | ((line_of >= t * slots) & (line_of < t * slots + counts_ref[t]))
    for c in range(COMPS):
        lw, an = shared[row(2, c)], shared[row(3, c)]
        derived[0, c] = shared[row(0, c)]
        derived[1, c] = shared[row(1, c)]
        derived[2, c] = (-0.5 * LOG2E) / (jnp.exp(2.0 * (lw + an)) + psf * psf)
        derived[3, c] = (-0.5 * LOG2E) / (jnp.exp(2.0 * (lw - an)) + psf * psf)
        derived[4, c] = jnp.where(live, amps[c], 0.0)
    sums[...] = jnp.zeros_like(sums)

    grid = lax.broadcasted_iota(jnp.int32, (pixels, 128), 0).astype(F32)

    def cut(x):
        hi = x.astype(BF16)
        return jnp.concatenate([hi, (x - hi.astype(F32)).astype(BF16)], axis=0)

    def stack(x):
        hi = x.astype(BF16)
        lo = (x - hi.astype(F32)).astype(BF16)
        turns = [part[r : r + 16] for r in range(0, pixels, 16) for part in (hi, lo)]
        one = jnp.concatenate(turns, axis=0)
        return jnp.concatenate([one, one], axis=1)

    def join(x):
        return jnp.concatenate([x[r : r + 16] + x[r + 16 : r + 32] for r in range(0, 2 * pixels, 32)], axis=0)

    def total(x):
        return jnp.sum(x, axis=0, keepdims=True)

    def line(index, c, s):
        return derived[index, c, pl.ds(s, 1), :]

    both = TOGETHER * COMPS
    for t in range(tiles):
        trips = (counts_ref[t] + TOGETHER - 1) // TOGETHER
        image[...] = jnp.zeros_like(image)

        def render(i, carry):
            for u in range(TOGETHER):
                s = i * TOGETHER + u
                g = t * slots + s
                off_x = offsets_ref[t, 0, s].astype(F32)
                off_y = offsets_ref[t, 1, s].astype(F32)
                for c in range(COMPS):
                    n = u * COMPS + c
                    d = grid - (line(0, c, g) + off_x)
                    e = jnp.exp2(d * d * line(2, c, g))
                    prof_x[i * both + n] = e
                    pieces_x[i, :, n * 128 : (n + 1) * 128] = cut(e)
                    d = grid - (line(1, c, g) + off_y)
                    e = jnp.exp2(d * d * line(3, c, g))
                    prof_y[i * both + n] = e
                    pieces_y[i, :, n * 128 : (n + 1) * 128] = cut(e * line(4, c, g))
            image[...] += lax.dot_general(
                pieces_x[i], pieces_y[i], (((1,), (1,)), ((), ())), preferred_element_type=F32
            )
            return carry

        lax.fori_loop(0, trips, render, 0)

        model = (image[:pixels, :pixels] + image[pixels:, pixels:]) + (
            image[:pixels, pixels:] + image[pixels:, :pixels]
        )
        cotangent = weight_ref[t, 0, 0] * (model - data_ref[t, 0, 0])
        left_x, left_y = stack(cotangent), stack(cotangent.T)

        def pull(i, carry):
            for first in range(0, both, 2):
                span = pl.ds(first * 128, 256)
                by_x = join(jnp.dot(left_x, pieces_y[i, :, span], preferred_element_type=F32))
                by_y = join(jnp.dot(left_y, pieces_x[i, :, span], preferred_element_type=F32))
                for n in (first, first + 1):
                    u, c = divmod(n, COMPS)
                    at = slice((n - first) * 128, (n - first + 1) * 128)
                    s = i * TOGETHER + u
                    g = t * slots + s
                    d = grid - (line(0, c, g) + offsets_ref[t, 0, s].astype(F32))
                    e = prof_x[i * both + n] * by_x[:, at]
                    e1 = e * d
                    sums[0, c, pl.ds(g, 1), :] = total(e1)
                    sums[1, c, pl.ds(g, 1), :] = total(e1 * d)
                    d = grid - (line(1, c, g) + offsets_ref[t, 1, s].astype(F32))
                    e = prof_y[i * both + n] * by_y[:, at]
                    e1 = e * d
                    sums[2, c, pl.ds(g, 1), :] = total(e1)
                    sums[3, c, pl.ds(g, 1), :] = total(e1 * d)
                    sums[4, c, pl.ds(g, 1), :] = total(e)
            return carry

        lax.fori_loop(0, trips, pull, 0)

    def keep(x):
        return jnp.where(live, x, 0.0)

    for c in range(COMPS):
        lw, an = shared[row(2, c)], shared[row(3, c)]
        wide_x, wide_y = jnp.exp(2.0 * (lw + an)), jnp.exp(2.0 * (lw - an))
        inv_x, inv_y = 1.0 / (wide_x + psf * psf), 1.0 / (wide_y + psf * psf)
        amp = amps[c]
        var_x = keep(sums[1, c] * inv_x * inv_x * wide_x)
        var_y = keep(amp * sums[3, c] * inv_y * inv_y * wide_y)
        shared[row(0, c)] = keep(sums[0, c] * inv_x)
        shared[row(1, c)] = keep(amp * sums[2, c] * inv_y)
        shared[row(2, c)] = var_x + var_y
        shared[row(3, c)] = var_x - var_y
        amps[c] = keep(sums[4, c])
    none = jnp.zeros((wide, 128), F32)
    for q, piece in enumerate(pieces):
        for p, entry in enumerate(piece):
            is_shared = entry is not None and entry[0] == "s"
            if is_shared:
                half[q, p] = shared[band, entry[1]]
            else:
                half[q, p] = none if entry is None else amps[entry[1]]
            if p < shared_rows:
                other[q, p] = shared[1 - band, entry[1]] if is_shared else none
    for k in range(epochs):
        outs[k][...] = half[lax.rem(epoch + k, epochs)]
        outs[epochs + k][...] = other[lax.rem(epoch + k, epochs)]


def step_gradient(layout, counts, offsets, psf, data, weight, slot_rows, moved):
    shared_rows, rows, pieces = layout
    epochs = len(pieces)
    later = moved is not None
    tiles, _, slots = offsets.shape
    pixels = data.shape[-1]
    wide = tiles * slots
    shapes = [(rows, wide, 128)] * epochs + [(shared_rows, wide, 128)] * epochs
    ins = slot_rows + (moved or [])
    together = [pltpu.VMEM((BANDS, HALF, wide, 128), F32), pltpu.VMEM((COMPS, wide, 128), F32)]
    return pl.pallas_call(
        functools.partial(step_kernel, layout, later),
        out_shape=[f32(*s) for s in shapes],
        in_specs=[smem()] * 3 + [vmem()] * (2 + len(ins)),
        out_specs=[vmem()] * len(shapes),
        scratch_shapes=together
        + [
            pltpu.VMEM((5, COMPS, wide, 128), F32),
            pltpu.VMEM((slots * COMPS, pixels, 128), F32),
            pltpu.VMEM((slots * COMPS, pixels, 128), F32),
            pltpu.VMEM((slots // TOGETHER, 2 * pixels, TOGETHER * COMPS * 128), BF16),
            pltpu.VMEM((slots // TOGETHER, 2 * pixels, TOGETHER * COMPS * 128), BF16),
            pltpu.VMEM((2 * pixels, 2 * pixels), F32),
            pltpu.VMEM((5, COMPS, wide, 128), F32),
            pltpu.VMEM((epochs, rows, wide, 128), F32),
            pltpu.VMEM((epochs, shared_rows, wide, 128), F32),
        ]
        + (together if later else []),
        compiler_params=params(32),
        name="later_step" if later else "first_step",
    )(counts, offsets, psf, data, weight, *ins)


def combine_kernel(layout, match_ref, *refs):
    shared_rows, rows, pieces = layout
    got_ref, out_ref, short_ref, own_ref = refs
    owners = got_ref.shape[0]
    wide = out_ref.shape[1]
    match = match_ref[...]
    for p in range(rows):
        both = pick(match, jnp.concatenate([got_ref[k, p] for k in range(owners)], axis=0))
        out_ref[p] = both[:wide]
        if p < shared_rows:
            short_ref[p] = both[:wide]
        own_ref[p] = both[wide:]


def dense_kernel(rows, lists_ref, grads, out_ref):
    tiles, slots = lists_ref.shape
    owners, _, blocks, _ = out_ref.shape
    shape = (owners * blocks, tiles * slots)
    line = lax.broadcasted_iota(jnp.int32, shape, 0)
    lane = lax.broadcasted_iota(jnp.int32, shape, 1)
    ids = jnp.zeros(shape, jnp.int32)
    for t in range(tiles):
        for s in range(slots):
            ids = jnp.where(lane == t * slots + s, lists_ref[t, s], ids)
    match = (ids == line).astype(F32)
    for p in range(rows):
        dense = pick(match, grads[p])
        for k in range(owners):
            out_ref[k, p] = dense[k * blocks : (k + 1) * blocks]


def final_kernel(layout, spacing, params_ref, got_ref, out_ref):
    shared_rows, rows, pieces = layout
    shift = [0.0, 0.0]
    for b in range(BANDS):
        for q, piece in enumerate(pieces):
            for p, entry in enumerate(piece):
                if entry is None:
                    continue
                row, position = row_of(b, entry)
                grad = got_ref[q * BANDS + b, p]
                out_ref[row] = params_ref[row] - STEP * grad
                if position is not None:
                    shift[position] = shift[position] + grad
    for k in range(2):
        out_ref[k] = params_ref[k] - (STEP * POSITION_RATE * spacing) * shift[k]


def shards(source_params, pixel_data, pixel_weight, psf_width, block_lists, block_counts, block_offsets):
    owners, epochs = lax.axis_size("tile"), lax.axis_size("epoch")
    blocks, param_rows, sources = source_params.shape
    tiles, slots = block_lists.shape
    wide = tiles * slots
    spacing = pixel_data.shape[-1] / 8.0
    layout = quarter_layout(epochs)
    shared_rows, rows, pieces = layout

    def to_peers(same, other):
        kept = [same[0]]
        for k in range(1, epochs):
            kept.append(lax.ppermute(same[k], "epoch", [(i, (i + k) % epochs) for i in range(epochs)]))
        for k in range(epochs):
            pairs = [
                (i * BANDS + b, (i + k) % epochs * BANDS + 1 - b)
                for i in range(epochs)
                for b in range(BANDS)
            ]
            kept.append(lax.ppermute(other[k], ("epoch", "band"), pairs))
        return kept

    def to_all(x, axes, size):
        return lax.all_to_all(jnp.broadcast_to(x, (size,) + x.shape), axes, 0, 0)

    def spread(piece, other):
        return to_peers([piece] * epochs, [other] * epochs)

    def summed(parts):
        near = functools.reduce(lambda a, b: a + b, parts[:epochs])
        far = functools.reduce(lambda a, b: a + b, parts[epochs:])
        return near + jnp.pad(far, ((0, rows - shared_rows), (0, 0), (0, 0)))

    by_row = jnp.transpose(source_params, (1, 0, 2))
    offsets = jnp.transpose(block_offsets, (0, 2, 1))
    packed = pl.pallas_call(
        functools.partial(pack_kernel, layout, spacing),
        out_shape=f32(rows + 1, blocks, sources),
        in_specs=[smem(), vmem()],
        out_specs=vmem(),
        compiler_params=params(),
        name="pack",
    )(block_lists, by_row)
    got = to_all(packed, "tile", owners)
    slot_piece, slot_short, match = pl.pallas_call(
        functools.partial(select_kernel, layout),
        out_shape=[
            f32(rows, wide, sources),
            f32(shared_rows, wide, sources),
            f32(wide + blocks, owners * wide),
        ],
        in_specs=[smem(), vmem()],
        out_specs=[vmem()] * 3,
        compiler_params=params(),
        name="select",
    )(block_lists, got)
    slot_rows = spread(slot_piece, slot_short)

    def gradient(moved):
        parts = step_gradient(
            layout, block_counts, offsets, psf_width, pixel_data, pixel_weight, slot_rows, moved
        )
        return summed(to_peers(parts[:epochs], parts[epochs:]))

    got = to_all(gradient(None), "tile", owners)
    slot_piece, slot_short, own_first = pl.pallas_call(
        functools.partial(combine_kernel, layout),
        out_shape=[
            f32(rows, wide, sources),
            f32(shared_rows, wide, sources),
            f32(rows, blocks, sources),
        ],
        in_specs=[vmem()] * 2,
        out_specs=[vmem()] * 3,
        compiler_params=params(),
        name="combine",
    )(match, got)

    dense = pl.pallas_call(
        functools.partial(dense_kernel, rows),
        out_shape=f32(owners, rows, blocks, sources),
        in_specs=[smem(), vmem()],
        out_specs=vmem(),
        compiler_params=params(),
        name="dense",
    )(block_lists, gradient(spread(slot_piece, slot_short)))
    own = own_first + jnp.sum(lax.all_to_all(dense, "tile", 0, 0), axis=0)
    whole = pl.pallas_call(
        functools.partial(final_kernel, layout, spacing),
        out_shape=f32(param_rows, blocks, sources),
        in_specs=[vmem()] * 2,
        out_specs=vmem(),
        compiler_params=params(),
        name="final",
    )(by_row, to_all(own, ("epoch", "band"), epochs * BANDS))
    return jnp.transpose(whole, (1, 0, 2))


def solution(mesh):
    return jax.shard_map(
        shards,
        mesh=mesh,
        in_specs=(
            P(("region", "tile"), None, None),
            P(("region", "tile"), "epoch", "band", None, None),
            P(("region", "tile"), "epoch", "band", None, None),
            P(("region", "epoch"), "band"),
            P(("region", "tile"), None),
            P(("region", "tile")),
            P(("region", "tile"), None, None),
        ),
        out_specs=P(("region", "tile"), None, None),
        check_vma=False,
    )
```

```python
import functools
import math

import jax
import jax.numpy as jnp
from jax import lax
from jax.experimental import pallas as pl
from jax.experimental.pallas import tpu as pltpu
from jax.sharding import PartitionSpec as P

ITERS = 2
STEP = 0.005
POSITION_RATE = 1.0 / 64.0
COMPS = 7
BANDS = 2
TOGETHER = 2
SHARED = 4 * COMPS
HALF = SHARED // BANDS
LOG2E = math.log2(math.e)
F32 = jnp.float32
BF16 = jnp.bfloat16
MIB = 1024 * 1024


def quarter_layout(epochs):
    shared_rows = -(-HALF // epochs)
    rows = -(-(HALF + COMPS) // epochs)
    pieces, amp = [], 0
    for q in range(epochs):
        piece = [("s", i) for i in range(q * shared_rows, min((q + 1) * shared_rows, HALF))]
        while len(piece) < rows and amp < COMPS:
            piece.append(("a", amp))
            amp += 1
        pieces.append(piece + [None] * (rows - len(piece)))
    return shared_rows, rows, pieces


def row_of(band, entry):
    kind, i = entry
    if kind == "a":
        return 2 + 6 * i + 4 + band, None
    k, c = divmod(HALF * band + i, COMPS)
    return 2 + 6 * c + k, (k if k < 2 else None)


def split3(x):
    hi = x.astype(BF16)
    rest = x - hi.astype(F32)
    mid = rest.astype(BF16)
    low = (rest - mid.astype(F32)).astype(BF16)
    return jnp.concatenate([hi, mid, low], axis=0)


def pick(matrix, rows):
    wide = jnp.concatenate([matrix, matrix, matrix], axis=1).astype(BF16)
    return jnp.dot(wide, split3(rows), preferred_element_type=F32)


def vmem():
    return pl.BlockSpec(memory_space=pltpu.VMEM)


def smem():
    return pl.BlockSpec(memory_space=pltpu.SMEM)


def f32(*shape):
    return jax.ShapeDtypeStruct(shape, F32)


def params(mib=4):
    return pltpu.CompilerParams(vmem_limit_bytes=mib * MIB)


def pack_kernel(layout, spacing, lists_ref, params_ref, out_ref):
    shared_rows, rows, pieces = layout
    band, epoch = lax.axis_index("band"), lax.axis_index("epoch")
    for b in range(BANDS):
        for q in range(len(pieces)):

            @pl.when((band == b) & (epoch == q))
            def _():
                for p, entry in enumerate(pieces[q]):
                    if entry is None:
                        out_ref[p] = jnp.zeros(out_ref.shape[1:], F32)
                        continue
                    row, position = row_of(b, entry)
                    value = params_ref[row]
                    if position is not None:
                        value = spacing * params_ref[position] + value
                    out_ref[p] = value

    tiles, slots = lists_ref.shape
    lane = lax.broadcasted_iota(jnp.int32, (8, 128), 1)
    ids = jnp.zeros((8, 128), jnp.int32)
    for t in range(tiles):
        for s in range(slots):
            ids = jnp.where(lane == t * slots + s, lists_ref[t, s], ids)
    out_ref[rows] = ids.astype(F32)


def select_kernel(layout, lists_ref, *refs):
    shared_rows, rows, pieces = layout
    got, (out_ref, short_ref, match_ref) = refs[:-3], refs[-3:]
    owners = len(got)
    tiles, slots = lists_ref.shape
    blocks = got[0].shape[1]
    wide = tiles * slots
    me = lax.axis_index("tile")

    def slot_ids(shape):
        line = lax.broadcasted_iota(jnp.int32, shape, 0)
        ids = jnp.zeros(shape, jnp.int32)
        for t in range(tiles):
            for s in range(slots):
                ids = jnp.where(line == t * slots + s, lists_ref[t, s], ids)
        return ids

    shape = (wide, owners * blocks)
    lane = lax.broadcasted_iota(jnp.int32, shape, 1)
    held = lax.rem(me - lane // blocks + owners, owners) * blocks + lane % blocks
    choose = (slot_ids(shape) == held).astype(F32)
    for p in range(rows):
        chosen = pick(choose, jnp.concatenate([ref[p] for ref in got], axis=0))
        out_ref[p] = chosen
        if p < shared_rows:
            short_ref[p] = chosen

    shape = (wide + blocks, owners * wide)
    line = lax.broadcasted_iota(jnp.int32, shape, 0)
    own = jnp.where(line < wide, slot_ids(shape), me * blocks + line - wide).astype(F32)
    sent = jnp.concatenate([ref[rows, :1, :wide] for ref in got], axis=1)
    match_ref[...] = (own == sent).astype(F32)


def put_together(layout, band, epoch, ins, half, other, shared, amps):
    shared_rows, rows, pieces = layout
    epochs = len(pieces)
    for k in range(epochs):
        q = lax.rem(epoch - k + epochs, epochs)
        half[q] = ins[k][...]
        other[q] = ins[epochs + k][...]
    for q, piece in enumerate(pieces):
        for p, entry in enumerate(piece):
            if entry is None:
                continue
            kind, i = entry
            if kind == "s":
                shared[band, i] = half[q, p]
                shared[1 - band, i] = other[q, p]
            else:
                amps[i] = half[q, p]


def step_kernel(layout, later, counts_ref, offsets_ref, psf_ref, data_ref, weight_ref, *refs):
    shared_rows, rows, pieces = layout
    epochs = len(pieces)
    taken = 2 * epochs * (2 if later else 1)
    ins, refs = refs[:taken], refs[taken:]
    outs, refs = refs[: 2 * epochs], refs[2 * epochs :]
    shared, amps, derived, here, prof_x, prof_y, pieces_x, pieces_y, image, sums, here_sums = refs[:11]
    half, other = refs[11:13]
    band, epoch = lax.axis_index("band"), lax.axis_index("epoch")
    tiles = data_ref.shape[0]
    pixels = data_ref.shape[-1]
    wide = shared.shape[2]
    slots = wide // tiles
    spacing = pixels / 8.0

    put_together(layout, band, epoch, ins[: 2 * epochs], half, other, shared, amps)

    def row(k, c):
        r = k * COMPS + c
        return r // HALF, r % HALF

    if later:
        moved, moved_amps = refs[13:]
        put_together(layout, band, epoch, ins[2 * epochs :], half, other, moved, moved_amps)
        for k in range(4):
            shift = 0.0
            if k < 2:
                shift = functools.reduce(lambda a, b: a + b, [moved[row(k, c)] for c in range(COMPS)])
                shift = shift * (spacing * spacing * POSITION_RATE)
            for c in range(COMPS):
                shared[row(k, c)] = shared[row(k, c)] - STEP * (moved[row(k, c)] + shift)
        for c in range(COMPS):
            amps[c] = amps[c] - STEP * moved_amps[c]

    psf = psf_ref[0, 0]
    line_of = lax.broadcasted_iota(jnp.int32, (slots, 128), 0)
    live = []
    for t in range(tiles):
        live.append(line_of < counts_ref[t])
        off_x = off_y = jnp.zeros((slots, 128), jnp.int32)
        for s in range(slots):
            off_x = jnp.where(line_of == s, offsets_ref[t, 0, s], off_x)
            off_y = jnp.where(line_of == s, offsets_ref[t, 1, s], off_y)
        off_x, off_y = off_x.astype(F32), off_y.astype(F32)
        at = slice(t * slots, (t + 1) * slots)
        for c in range(COMPS):
            cx, cy, lw, an = (shared[(*row(k, c), at)] for k in range(4))
            derived[t, 0, c] = cx + off_x
            derived[t, 1, c] = cy + off_y
            derived[t, 2, c] = (-0.5 * LOG2E) / (jnp.exp(2.0 * (lw + an)) + psf * psf)
            derived[t, 3, c] = (-0.5 * LOG2E) / (jnp.exp(2.0 * (lw - an)) + psf * psf)
            derived[t, 4, c] = jnp.where(live[t], amps[c, at], 0.0)
    live = jnp.concatenate(live, axis=0)

    grid = lax.broadcasted_iota(jnp.int32, (pixels, 128), 0).astype(F32)

    def cut(x):
        hi = x.astype(BF16)
        return jnp.concatenate([hi, (x - hi.astype(F32)).astype(BF16)], axis=0)

    def stack(x):
        hi = x.astype(BF16)
        lo = (x - hi.astype(F32)).astype(BF16)
        turns = [part[r : r + 16] for r in range(0, pixels, 16) for part in (hi, lo)]
        one = jnp.concatenate(turns, axis=0)
        return jnp.concatenate([one, one], axis=1)

    def join(x):
        return jnp.concatenate([x[r : r + 16] + x[r + 16 : r + 32] for r in range(0, 2 * pixels, 32)], axis=0)

    def total(x):
        return jnp.sum(x, axis=0, keepdims=True)

    both = TOGETHER * COMPS

    def tile_body(t, carry):
        here[...] = derived[t]

        def line(index, c, s):
            return here[index, c, s : s + 1, :]

        for i in range(slots // TOGETHER):
            for n in range(both):
                u, c = divmod(n, COMPS)
                s = i * TOGETHER + u
                d = grid - line(0, c, s)
                e = jnp.exp2(d * d * line(2, c, s))
                prof_x[i * both + n] = e
                pieces_x[i, :, n * 128 : (n + 1) * 128] = cut(e)
                d = grid - line(1, c, s)
                e = jnp.exp2(d * d * line(3, c, s))
                prof_y[i * both + n] = e
                pieces_y[i, :, n * 128 : (n + 1) * 128] = cut(e * line(4, c, s))
            part = lax.dot_general(
                pieces_x[i], pieces_y[i], (((1,), (1,)), ((), ())), preferred_element_type=F32
            )
            image[...] = part if i == 0 else image[...] + part

        model = (image[:pixels, :pixels] + image[pixels:, pixels:]) + (
            image[:pixels, pixels:] + image[pixels:, :pixels]
        )
        cotangent = weight_ref[t, 0, 0] * (model - data_ref[t, 0, 0])
        left_x, left_y = stack(cotangent), stack(cotangent.T)

        for i in range(slots // TOGETHER):
            for first in range(0, both, 2):
                span = pl.ds(first * 128, 256)
                by_x = join(jnp.dot(left_x, pieces_y[i, :, span], preferred_element_type=F32))
                by_y = join(jnp.dot(left_y, pieces_x[i, :, span], preferred_element_type=F32))
                for n in (first, first + 1):
                    u, c = divmod(n, COMPS)
                    s = i * TOGETHER + u
                    at = slice((n - first) * 128, (n - first + 1) * 128)
                    d = grid - line(0, c, s)
                    e = prof_x[i * both + n] * by_x[:, at]
                    e1 = e * d
                    here_sums[0, c, s : s + 1, :] = total(e1)
                    here_sums[1, c, s : s + 1, :] = total(e1 * d)
                    d = grid - line(1, c, s)
                    e = prof_y[i * both + n] * by_y[:, at]
                    e1 = e * d
                    here_sums[2, c, s : s + 1, :] = total(e1)
                    here_sums[3, c, s : s + 1, :] = total(e1 * d)
                    here_sums[4, c, s : s + 1, :] = total(e)
        sums[t] = here_sums[...]
        return carry

    lax.fori_loop(0, tiles, tile_body, 0)

    def sum_of(index, c):
        return jnp.concatenate([sums[t, index, c] for t in range(tiles)], axis=0)

    def keep(x):
        return jnp.where(live, x, 0.0)

    for c in range(COMPS):
        lw, an = shared[row(2, c)], shared[row(3, c)]
        wide_x, wide_y = jnp.exp(2.0 * (lw + an)), jnp.exp(2.0 * (lw - an))
        inv_x, inv_y = 1.0 / (wide_x + psf * psf), 1.0 / (wide_y + psf * psf)
        amp = amps[c]
        var_x = keep(sum_of(1, c) * inv_x * (inv_x * wide_x))
        var_y = keep(amp * sum_of(3, c) * inv_y * (inv_y * wide_y))
        shared[row(0, c)] = keep(sum_of(0, c) * inv_x)
        shared[row(1, c)] = keep(amp * sum_of(2, c) * inv_y)
        shared[row(2, c)] = var_x + var_y
        shared[row(3, c)] = var_x - var_y
        amps[c] = keep(sum_of(4, c))
    none = jnp.zeros((wide, 128), F32)
    for q, piece in enumerate(pieces):
        for p, entry in enumerate(piece):
            is_shared = entry is not None and entry[0] == "s"
            if is_shared:
                half[q, p] = shared[band, entry[1]]
            else:
                half[q, p] = none if entry is None else amps[entry[1]]
            if p < shared_rows:
                other[q, p] = shared[1 - band, entry[1]] if is_shared else none
    for k in range(epochs):
        outs[k][...] = half[lax.rem(epoch + k, epochs)]
        outs[epochs + k][...] = other[lax.rem(epoch + k, epochs)]


def step_gradient(layout, counts, offsets, psf, data, weight, slot_rows, moved):
    shared_rows, rows, pieces = layout
    epochs = len(pieces)
    later = moved is not None
    tiles, _, slots = offsets.shape
    pixels = data.shape[-1]
    wide = tiles * slots
    shapes = [(rows, wide, 128)] * epochs + [(shared_rows, wide, 128)] * epochs
    ins = slot_rows + (moved or [])
    together = [pltpu.VMEM((BANDS, HALF, wide, 128), F32), pltpu.VMEM((COMPS, wide, 128), F32)]
    return pl.pallas_call(
        functools.partial(step_kernel, layout, later),
        out_shape=[f32(*s) for s in shapes],
        in_specs=[smem()] * 3 + [vmem()] * (2 + len(ins)),
        out_specs=[vmem()] * len(shapes),
        scratch_shapes=together
        + [
            pltpu.VMEM((tiles, 5, COMPS, slots, 128), F32),
            pltpu.VMEM((5, COMPS, slots, 128), F32),
            pltpu.VMEM((slots * COMPS, pixels, 128), F32),
            pltpu.VMEM((slots * COMPS, pixels, 128), F32),
            pltpu.VMEM((slots // TOGETHER, 2 * pixels, TOGETHER * COMPS * 128), BF16),
            pltpu.VMEM((slots // TOGETHER, 2 * pixels, TOGETHER * COMPS * 128), BF16),
            pltpu.VMEM((2 * pixels, 2 * pixels), F32),
            pltpu.VMEM((tiles, 5, COMPS, slots, 128), F32),
            pltpu.VMEM((5, COMPS, slots, 128), F32),
            pltpu.VMEM((epochs, rows, wide, 128), F32),
            pltpu.VMEM((epochs, shared_rows, wide, 128), F32),
        ]
        + (together if later else []),
        compiler_params=params(32),
        name="later_step" if later else "first_step",
    )(counts, offsets, psf, data, weight, *ins)


def combine_kernel(layout, match_ref, *refs):
    shared_rows, rows, pieces = layout
    got, (out_ref, short_ref, own_ref) = refs[:-3], refs[-3:]
    wide = out_ref.shape[1]
    match = match_ref[...]
    for p in range(rows):
        both = pick(match, jnp.concatenate([ref[p] for ref in got], axis=0))
        out_ref[p] = both[:wide]
        if p < shared_rows:
            short_ref[p] = both[:wide]
        own_ref[p] = both[wide:]


def dense_kernel(rows, lists_ref, grads, *outs):
    tiles, slots = lists_ref.shape
    owners, blocks = len(outs), outs[0].shape[1]
    shape = (owners * blocks, tiles * slots)
    line = lax.broadcasted_iota(jnp.int32, shape, 0)
    lane = lax.broadcasted_iota(jnp.int32, shape, 1)
    me = lax.axis_index("tile")
    target = lax.rem(me + line // blocks, owners) * blocks + line % blocks
    ids = jnp.zeros(shape, jnp.int32)
    for t in range(tiles):
        for s in range(slots):
            ids = jnp.where(lane == t * slots + s, lists_ref[t, s], ids)
    match = (ids == target).astype(F32)
    for p in range(rows):
        dense = pick(match, grads[p])
        for k, out in enumerate(outs):
            out[p] = dense[k * blocks : (k + 1) * blocks]


def final_kernel(layout, spacing, params_ref, *refs):
    shared_rows, rows, pieces = layout
    epochs = len(pieces)
    ins, (out_ref, held) = refs[: 2 * epochs], refs[2 * epochs :]
    band, epoch = lax.axis_index("band"), lax.axis_index("epoch")
    for k in range(epochs):
        q = lax.rem(epoch - k + epochs, epochs)
        held[band, q] = ins[k][...]
        held[1 - band, q] = ins[epochs + k][...]
    shift = [0.0, 0.0]
    for b in range(BANDS):
        for q, piece in enumerate(pieces):
            for p, entry in enumerate(piece):
                if entry is None:
                    continue
                row, position = row_of(b, entry)
                grad = held[b, q, p]
                out_ref[row] = params_ref[row] - STEP * grad
                if position is not None:
                    shift[position] = shift[position] + grad
    for k in range(2):
        out_ref[k] = params_ref[k] - (STEP * POSITION_RATE * spacing) * shift[k]


def shards(source_params, pixel_data, pixel_weight, psf_width, block_lists, block_counts, block_offsets):
    owners, epochs = lax.axis_size("tile"), lax.axis_size("epoch")
    blocks, param_rows, sources = source_params.shape
    tiles, slots = block_lists.shape
    wide = tiles * slots
    spacing = pixel_data.shape[-1] / 8.0
    layout = quarter_layout(epochs)
    shared_rows, rows, pieces = layout

    def to_peers(same, other):
        kept = [same[0]]
        for k in range(1, epochs):
            kept.append(lax.ppermute(same[k], "epoch", [(i, (i + k) % epochs) for i in range(epochs)]))
        for k in range(epochs):
            pairs = [
                (i * BANDS + b, (i + k) % epochs * BANDS + 1 - b)
                for i in range(epochs)
                for b in range(BANDS)
            ]
            kept.append(lax.ppermute(other[k], ("epoch", "band"), pairs))
        return kept

    def round_tiles(arrays):
        return [arrays[0]] + [
            lax.ppermute(arrays[k], "tile", [(i, (i + k) % owners) for i in range(owners)])
            for k in range(1, owners)
        ]

    def spread(piece, other):
        return to_peers([piece] * epochs, [other] * epochs)

    def summed(parts):
        near = functools.reduce(lambda a, b: a + b, parts[:epochs])
        far = functools.reduce(lambda a, b: a + b, parts[epochs:])
        return near + jnp.pad(far, ((0, rows - shared_rows), (0, 0), (0, 0)))

    by_row = jnp.transpose(source_params, (1, 0, 2))
    offsets = jnp.transpose(block_offsets, (0, 2, 1))
    packed = pl.pallas_call(
        functools.partial(pack_kernel, layout, spacing),
        out_shape=f32(rows + 1, blocks, sources),
        in_specs=[smem(), vmem()],
        out_specs=vmem(),
        compiler_params=params(),
        name="pack",
    )(block_lists, by_row)
    got = round_tiles([packed] * owners)
    slot_piece, slot_short, match = pl.pallas_call(
        functools.partial(select_kernel, layout),
        out_shape=[
            f32(rows, wide, sources),
            f32(shared_rows, wide, sources),
            f32(wide + blocks, owners * wide),
        ],
        in_specs=[smem()] + [vmem()] * owners,
        out_specs=[vmem()] * 3,
        compiler_params=params(),
        name="select",
    )(block_lists, *got)
    slot_rows = spread(slot_piece, slot_short)

    def gradient(moved):
        parts = step_gradient(
            layout, block_counts, offsets, psf_width, pixel_data, pixel_weight, slot_rows, moved
        )
        return summed(to_peers(parts[:epochs], parts[epochs:]))

    got = round_tiles([gradient(None)] * owners)
    slot_piece, slot_short, own_first = pl.pallas_call(
        functools.partial(combine_kernel, layout),
        out_shape=[
            f32(rows, wide, sources),
            f32(shared_rows, wide, sources),
            f32(rows, blocks, sources),
        ],
        in_specs=[vmem()] * (1 + owners),
        out_specs=[vmem()] * 3,
        compiler_params=params(),
        name="combine",
    )(match, *got)

    dense = pl.pallas_call(
        functools.partial(dense_kernel, rows),
        out_shape=[f32(rows, blocks, sources)] * owners,
        in_specs=[smem(), vmem()],
        out_specs=[vmem()] * owners,
        compiler_params=params(),
        name="dense",
    )(block_lists, gradient(spread(slot_piece, slot_short)))
    own = functools.reduce(lambda a, b: a + b, round_tiles(dense), own_first)
    whole = pl.pallas_call(
        functools.partial(final_kernel, layout, spacing),
        out_shape=f32(param_rows, blocks, sources),
        in_specs=[vmem()] * (1 + 2 * epochs),
        out_specs=vmem(),
        scratch_shapes=[pltpu.VMEM((BANDS, epochs, rows, blocks, sources), F32)],
        compiler_params=params(),
        name="final",
    )(by_row, *spread(own, own))
    return jnp.transpose(whole, (1, 0, 2))


def solution(mesh):
    return jax.shard_map(
        shards,
        mesh=mesh,
        in_specs=(
            P(("region", "tile"), None, None),
            P(("region", "tile"), "epoch", "band", None, None),
            P(("region", "tile"), "epoch", "band", None, None),
            P(("region", "epoch"), "band"),
            P(("region", "tile"), None),
            P(("region", "tile")),
            P(("region", "tile"), None, None),
        ),
        out_specs=P(("region", "tile"), None, None),
        check_vma=False,
    )
```

```python
import functools
import math

import jax
import jax.numpy as jnp
from jax import lax
from jax.experimental import pallas as pl
from jax.experimental.pallas import tpu as pltpu
from jax.sharding import PartitionSpec as P

ITERS = 2
STEP = 0.005
POSITION_RATE = 1.0 / 64.0
COMPS = 7
BANDS = 2
SHARED = 4 * COMPS
HALF = SHARED // BANDS
LOG2E = math.log2(math.e)
F32 = jnp.float32
BF16 = jnp.bfloat16
MIB = 1024 * 1024


def quarter_layout(epochs):
    shared_rows = -(-HALF // epochs)
    rows = -(-(HALF + COMPS) // epochs)
    pieces, amp = [], 0
    for q in range(epochs):
        piece = [("s", i) for i in range(q * shared_rows, min((q + 1) * shared_rows, HALF))]
        while len(piece) < rows and amp < COMPS:
            piece.append(("a", amp))
            amp += 1
        pieces.append(piece + [None] * (rows - len(piece)))
    return shared_rows, rows, pieces


def row_of(band, entry):
    kind, i = entry
    if kind == "a":
        return 2 + 6 * i + 4 + band, None
    k, c = divmod(HALF * band + i, COMPS)
    return 2 + 6 * c + k, (k if k < 2 else None)


def split3(x):
    hi = x.astype(BF16)
    rest = x - hi.astype(F32)
    mid = rest.astype(BF16)
    low = (rest - mid.astype(F32)).astype(BF16)
    return jnp.concatenate([hi, mid, low], axis=0)


def pick(matrix, rows):
    wide = jnp.concatenate([matrix, matrix, matrix], axis=1).astype(BF16)
    return jnp.dot(wide, split3(rows), preferred_element_type=F32)


def vmem():
    return pl.BlockSpec(memory_space=pltpu.VMEM)


def smem():
    return pl.BlockSpec(memory_space=pltpu.SMEM)


def f32(*shape):
    return jax.ShapeDtypeStruct(shape, F32)


def params(mib=4):
    return pltpu.CompilerParams(vmem_limit_bytes=mib * MIB)


def pack_kernel(layout, spacing, lists_hbm, params_hbm, out_ref, lists_ref, positions, fetched, sems):
    shared_rows, rows, pieces = layout
    band, epoch = lax.axis_index("band"), lax.axis_index("epoch")
    lists_copy = pltpu.make_async_copy(lists_hbm, lists_ref, sems.at[0])
    lists_copy.start()
    positions_copy = pltpu.make_async_copy(params_hbm.at[pl.ds(0, 2)], positions, sems.at[1])
    positions_copy.start()

    def pick_row(p):
        row, position = jnp.int32(0), jnp.int32(2)
        for b in range(BANDS):
            for q, piece in enumerate(pieces):
                if piece[p] is None:
                    continue
                mine = (band == b) & (epoch == q)
                its_row, its_position = row_of(b, piece[p])
                row = jnp.where(mine, its_row, row)
                if its_position is not None:
                    position = jnp.where(mine, its_position, position)
        return row, position

    chosen = [pick_row(p) for p in range(rows)]
    copies = [
        pltpu.make_async_copy(params_hbm.at[row], fetched.at[p], sems.at[2 + p])
        for p, (row, _) in enumerate(chosen)
    ]
    for copy in copies:
        copy.start()
    lists_copy.wait()
    tiles, slots = lists_ref.shape
    lane = lax.broadcasted_iota(jnp.int32, (8, 128), 1)
    ids = jnp.zeros((8, 128), jnp.int32)
    for t in range(tiles):
        for s in range(slots):
            ids = jnp.where(lane == t * slots + s, lists_ref[t, s], ids)
    out_ref[rows] = ids.astype(F32)
    positions_copy.wait()
    for p, (copy, (_, position)) in enumerate(zip(copies, chosen)):
        copy.wait()
        added = jnp.where(position == 0, positions[0], jnp.where(position == 1, positions[1], 0.0))
        out_ref[p] = spacing * added + fetched[p]


def select_kernel(layout, lists_ref, *refs):
    shared_rows, rows, pieces = layout
    got, (out_ref, short_ref, match_ref) = refs[:-3], refs[-3:]
    owners = len(got)
    tiles, slots = lists_ref.shape
    blocks = got[0].shape[1]
    wide = tiles * slots
    me = lax.axis_index("tile")

    def slot_ids(shape):
        line = lax.broadcasted_iota(jnp.int32, shape, 0)
        ids = jnp.zeros(shape, jnp.int32)
        for t in range(tiles):
            for s in range(slots):
                ids = jnp.where(line == t * slots + s, lists_ref[t, s], ids)
        return ids

    shape = (wide, owners * blocks)
    lane = lax.broadcasted_iota(jnp.int32, shape, 1)
    held = lax.rem(me - lane // blocks + owners, owners) * blocks + lane % blocks
    choose = (slot_ids(shape) == held).astype(F32)
    for p in range(rows):
        chosen = pick(choose, jnp.concatenate([ref[p] for ref in got], axis=0))
        out_ref[p] = chosen
        if p < shared_rows:
            short_ref[p] = chosen

    shape = (wide + blocks, owners * wide)
    line = lax.broadcasted_iota(jnp.int32, shape, 0)
    own = jnp.where(line < wide, slot_ids(shape), me * blocks + line - wide).astype(F32)
    sent = jnp.concatenate([ref[rows, :1, :wide] for ref in got], axis=1)
    match_ref[...] = (own == sent).astype(F32)


def put_together(layout, band, epoch, ins, half, other, shared, amps):
    shared_rows, rows, pieces = layout
    epochs = len(pieces)
    for k in range(epochs):
        q = lax.rem(epoch - k + epochs, epochs)
        half[q] = ins[k][...]
        other[q] = ins[epochs + k][...]
    for q, piece in enumerate(pieces):
        for p, entry in enumerate(piece):
            if entry is None:
                continue
            kind, i = entry
            if kind == "s":
                shared[band, i] = half[q, p]
                shared[1 - band, i] = other[q, p]
            else:
                amps[i] = half[q, p]


def step_kernel(layout, later, counts_ref, offsets_ref, psf_ref, data_ref, weight_ref, *refs):
    shared_rows, rows, pieces = layout
    epochs = len(pieces)
    taken = 2 * epochs * (2 if later else 1)
    ins, refs = refs[:taken], refs[taken:]
    outs, refs = refs[: 2 * epochs], refs[2 * epochs :]
    shared, amps, derived, prof_x, prof_y, pieces_x, pieces_y, image, sums, half, other = refs[:11]
    band, epoch = lax.axis_index("band"), lax.axis_index("epoch")
    tiles = data_ref.shape[0]
    pixels = data_ref.shape[-1]
    wide = shared.shape[2]
    slots = wide // tiles
    spacing = pixels / 8.0

    put_together(layout, band, epoch, ins[: 2 * epochs], half, other, shared, amps)

    def row(k, c):
        r = k * COMPS + c
        return r // HALF, r % HALF

    if later:
        moved, moved_amps = refs[11:]
        put_together(layout, band, epoch, ins[2 * epochs :], half, other, moved, moved_amps)
        for k in range(4):
            shift = 0.0
            if k < 2:
                shift = functools.reduce(lambda a, b: a + b, [moved[row(k, c)] for c in range(COMPS)])
                shift = shift * (spacing * spacing * POSITION_RATE)
            for c in range(COMPS):
                shared[row(k, c)] = shared[row(k, c)] - STEP * (moved[row(k, c)] + shift)
        for c in range(COMPS):
            amps[c] = amps[c] - STEP * moved_amps[c]

    psf = psf_ref[0, 0]
    line_of = lax.broadcasted_iota(jnp.int32, (wide, 128), 0)
    live = jnp.zeros((wide, 128), jnp.bool_)
    for t in range(tiles):
        live = live | ((line_of >= t * slots) & (line_of < t * slots + counts_ref[t]))
    for c in range(COMPS):
        lw, an = shared[row(2, c)], shared[row(3, c)]
        derived[0, c] = shared[row(0, c)]
        derived[1, c] = shared[row(1, c)]
        derived[2, c] = (-0.5 * LOG2E) / (jnp.exp(2.0 * (lw + an)) + psf * psf)
        derived[3, c] = (-0.5 * LOG2E) / (jnp.exp(2.0 * (lw - an)) + psf * psf)
        derived[4, c] = jnp.where(live, amps[c], 0.0)
    sums[...] = jnp.zeros_like(sums)

    grid = lax.broadcasted_iota(jnp.int32, (pixels, 128), 0).astype(F32)

    def cut(x):
        hi = x.astype(BF16)
        return jnp.concatenate([hi, (x - hi.astype(F32)).astype(BF16)], axis=0)

    def stack(x):
        hi = x.astype(BF16)
        return jnp.concatenate([hi, hi], axis=1), (x - hi.astype(F32)).astype(BF16)

    def times(left, right):
        near = jnp.dot(left[0], right, preferred_element_type=F32)
        return near + jnp.dot(left[1], right[:pixels], preferred_element_type=F32)

    def total(x):
        return jnp.sum(x, axis=0, keepdims=True)

    def line(index, c, s):
        return derived[index, c, pl.ds(s, 1), :]

    together = 2
    for t in range(tiles):
        trips = (counts_ref[t] + together - 1) // together
        image[...] = jnp.zeros_like(image)

        def render(i, carry):
            for u in range(together):
                s = i * together + u
                g = t * slots + s
                off_x = offsets_ref[t, 0, s].astype(F32)
                off_y = offsets_ref[t, 1, s].astype(F32)
                for c in range(COMPS):
                    d = grid - (line(0, c, g) + off_x)
                    e = jnp.exp2(d * d * line(2, c, g))
                    prof_x[s * COMPS + c] = e
                    pieces_x[s, :, c * 128 : (c + 1) * 128] = cut(e)
                    d = grid - (line(1, c, g) + off_y)
                    e = jnp.exp2(d * d * line(3, c, g))
                    prof_y[s * COMPS + c] = e
                    pieces_y[s, :, c * 128 : (c + 1) * 128] = cut(e * line(4, c, g))
                image[...] += lax.dot_general(
                    pieces_x[s], pieces_y[s], (((1,), (1,)), ((), ())), preferred_element_type=F32
                )
            return carry

        lax.fori_loop(0, trips, render, 0)

        model = (image[:pixels, :pixels] + image[pixels:, pixels:]) + (
            image[:pixels, pixels:] + image[pixels:, :pixels]
        )
        cotangent = weight_ref[t, 0, 0] * (model - data_ref[t, 0, 0])
        left_x, left_y = stack(cotangent), stack(cotangent.T)

        def pull(i, carry):
            for u in range(together):
                s = i * together + u
                g = t * slots + s
                off_x = offsets_ref[t, 0, s].astype(F32)
                off_y = offsets_ref[t, 1, s].astype(F32)
                for first in range(0, COMPS, 2):
                    here = min(2, COMPS - first)
                    span = pl.ds(first * 128, 128 * here)
                    by_x = times(left_x, pieces_y[s, :, span])
                    by_y = times(left_y, pieces_x[s, :, span])
                    for n in range(here):
                        c = first + n
                        d = grid - (line(0, c, g) + off_x)
                        e = prof_x[s * COMPS + c] * by_x[:, n * 128 : (n + 1) * 128]
                        e1 = e * d
                        sums[0, c, pl.ds(g, 1), :] = total(e1)
                        sums[1, c, pl.ds(g, 1), :] = total(e1 * d)
                        d = grid - (line(1, c, g) + off_y)
                        e = prof_y[s * COMPS + c] * by_y[:, n * 128 : (n + 1) * 128]
                        e1 = e * d
                        sums[2, c, pl.ds(g, 1), :] = total(e1)
                        sums[3, c, pl.ds(g, 1), :] = total(e1 * d)
                        sums[4, c, pl.ds(g, 1), :] = total(e)
            return carry

        lax.fori_loop(0, trips, pull, 0)

    def keep(x):
        return jnp.where(live, x, 0.0)

    for c in range(COMPS):
        lw, an = shared[row(2, c)], shared[row(3, c)]
        wide_x, wide_y = jnp.exp(2.0 * (lw + an)), jnp.exp(2.0 * (lw - an))
        inv_x, inv_y = 1.0 / (wide_x + psf * psf), 1.0 / (wide_y + psf * psf)
        amp = amps[c]
        var_x = keep(sums[1, c] * inv_x * (inv_x * wide_x))
        var_y = keep(amp * sums[3, c] * inv_y * (inv_y * wide_y))
        shared[row(0, c)] = keep(sums[0, c] * inv_x)
        shared[row(1, c)] = keep(amp * sums[2, c] * inv_y)
        shared[row(2, c)] = var_x + var_y
        shared[row(3, c)] = var_x - var_y
        amps[c] = keep(sums[4, c])
    none = jnp.zeros((wide, 128), F32)
    for q, piece in enumerate(pieces):
        for p, entry in enumerate(piece):
            is_shared = entry is not None and entry[0] == "s"
            if is_shared:
                half[q, p] = shared[band, entry[1]]
            else:
                half[q, p] = none if entry is None else amps[entry[1]]
            if p < shared_rows:
                other[q, p] = shared[1 - band, entry[1]] if is_shared else none
    for k in range(epochs):
        outs[k][...] = half[lax.rem(epoch + k, epochs)]
        outs[epochs + k][...] = other[lax.rem(epoch + k, epochs)]


def step_gradient(layout, counts, offsets, psf, data, weight, slot_rows, moved):
    shared_rows, rows, pieces = layout
    epochs = len(pieces)
    later = moved is not None
    tiles, _, slots = offsets.shape
    pixels = data.shape[-1]
    wide = tiles * slots
    shapes = [(rows, wide, 128)] * epochs + [(shared_rows, wide, 128)] * epochs
    ins = slot_rows + (moved or [])
    together = [pltpu.VMEM((BANDS, HALF, wide, 128), F32), pltpu.VMEM((COMPS, wide, 128), F32)]
    return pl.pallas_call(
        functools.partial(step_kernel, layout, later),
        out_shape=[f32(*s) for s in shapes],
        in_specs=[smem()] * 3 + [vmem()] * (2 + len(ins)),
        out_specs=[vmem()] * len(shapes),
        scratch_shapes=together
        + [
            pltpu.VMEM((5, COMPS, wide, 128), F32),
            pltpu.VMEM((slots * COMPS, pixels, 128), F32),
            pltpu.VMEM((slots * COMPS, pixels, 128), F32),
            pltpu.VMEM((slots, 2 * pixels, COMPS * 128), BF16),
            pltpu.VMEM((slots, 2 * pixels, COMPS * 128), BF16),
            pltpu.VMEM((2 * pixels, 2 * pixels), F32),
            pltpu.VMEM((5, COMPS, wide, 128), F32),
            pltpu.VMEM((epochs, rows, wide, 128), F32),
            pltpu.VMEM((epochs, shared_rows, wide, 128), F32),
        ]
        + (together if later else []),
        compiler_params=params(32),
        name="later_step" if later else "first_step",
    )(counts, offsets, psf, data, weight, *ins)


def combine_kernel(layout, match_ref, *refs):
    shared_rows, rows, pieces = layout
    got, (out_ref, short_ref, own_ref) = refs[:-3], refs[-3:]
    wide = out_ref.shape[1]
    match = match_ref[...]
    for p in range(rows):
        both = pick(match, jnp.concatenate([ref[p] for ref in got], axis=0))
        out_ref[p] = both[:wide]
        if p < shared_rows:
            short_ref[p] = both[:wide]
        own_ref[p] = both[wide:]


def dense_kernel(rows, lists_ref, grads, *outs):
    tiles, slots = lists_ref.shape
    owners, blocks = len(outs), outs[0].shape[1]
    shape = (owners * blocks, tiles * slots)
    line = lax.broadcasted_iota(jnp.int32, shape, 0)
    lane = lax.broadcasted_iota(jnp.int32, shape, 1)
    me = lax.axis_index("tile")
    target = lax.rem(me + line // blocks, owners) * blocks + line % blocks
    ids = jnp.zeros(shape, jnp.int32)
    for t in range(tiles):
        for s in range(slots):
            ids = jnp.where(lane == t * slots + s, lists_ref[t, s], ids)
    match = (ids == target).astype(F32)
    for p in range(rows):
        dense = pick(match, grads[p])
        for k, out in enumerate(outs):
            out[p] = dense[k * blocks : (k + 1) * blocks]


def final_kernel(layout, spacing, params_ref, *refs):
    shared_rows, rows, pieces = layout
    epochs = len(pieces)
    ins, (out_ref, held) = refs[: 2 * epochs], refs[2 * epochs :]
    band, epoch = lax.axis_index("band"), lax.axis_index("epoch")
    for k in range(epochs):
        q = lax.rem(epoch - k + epochs, epochs)
        held[band, q] = ins[k][...]
        held[1 - band, q] = ins[epochs + k][...]
    shift = [0.0, 0.0]
    for b in range(BANDS):
        for q, piece in enumerate(pieces):
            for p, entry in enumerate(piece):
                if entry is None:
                    continue
                row, position = row_of(b, entry)
                grad = held[b, q, p]
                out_ref[row] = params_ref[row] - STEP * grad
                if position is not None:
                    shift[position] = shift[position] + grad
    for k in range(2):
        out_ref[k] = params_ref[k] - (STEP * POSITION_RATE * spacing) * shift[k]


def shards(source_params, pixel_data, pixel_weight, psf_width, block_lists, block_counts, block_offsets):
    owners, epochs = lax.axis_size("tile"), lax.axis_size("epoch")
    blocks, param_rows, sources = source_params.shape
    tiles, slots = block_lists.shape
    wide = tiles * slots
    spacing = pixel_data.shape[-1] / 8.0
    layout = quarter_layout(epochs)
    shared_rows, rows, pieces = layout

    def to_peers(same, other):
        kept = [same[0]]
        for k in range(1, epochs):
            kept.append(lax.ppermute(same[k], "epoch", [(i, (i + k) % epochs) for i in range(epochs)]))
        for k in range(epochs):
            pairs = [
                (i * BANDS + b, (i + k) % epochs * BANDS + 1 - b)
                for i in range(epochs)
                for b in range(BANDS)
            ]
            kept.append(lax.ppermute(other[k], ("epoch", "band"), pairs))
        return kept

    def round_tiles(arrays):
        return [arrays[0]] + [
            lax.ppermute(arrays[k], "tile", [(i, (i + k) % owners) for i in range(owners)])
            for k in range(1, owners)
        ]

    def spread(piece, other):
        return to_peers([piece] * epochs, [other] * epochs)

    def summed(parts):
        near = functools.reduce(lambda a, b: a + b, parts[:epochs])
        far = functools.reduce(lambda a, b: a + b, parts[epochs:])
        return near + jnp.pad(far, ((0, rows - shared_rows), (0, 0), (0, 0)))

    by_row = jnp.transpose(source_params, (1, 0, 2))
    offsets = jnp.transpose(block_offsets, (0, 2, 1))
    packed = pl.pallas_call(
        functools.partial(pack_kernel, layout, spacing),
        out_shape=f32(rows + 1, blocks, sources),
        in_specs=[pl.BlockSpec(memory_space=pltpu.HBM)] * 2,
        out_specs=vmem(),
        scratch_shapes=[
            pltpu.SMEM((tiles, slots), jnp.int32),
            pltpu.VMEM((2, blocks, sources), F32),
            pltpu.VMEM((rows, blocks, sources), F32),
            pltpu.SemaphoreType.DMA((rows + 2,)),
        ],
        compiler_params=params(56),
        name="pack",
    )(block_lists, by_row)
    got = round_tiles([packed] * owners)
    slot_piece, slot_short, match = pl.pallas_call(
        functools.partial(select_kernel, layout),
        out_shape=[
            f32(rows, wide, sources),
            f32(shared_rows, wide, sources),
            f32(wide + blocks, owners * wide),
        ],
        in_specs=[smem()] + [vmem()] * owners,
        out_specs=[vmem()] * 3,
        compiler_params=params(),
        name="select",
    )(block_lists, *got)
    slot_rows = spread(slot_piece, slot_short)

    def gradient(moved):
        parts = step_gradient(
            layout, block_counts, offsets, psf_width, pixel_data, pixel_weight, slot_rows, moved
        )
        return summed(to_peers(parts[:epochs], parts[epochs:]))

    got = round_tiles([gradient(None)] * owners)
    slot_piece, slot_short, own_first = pl.pallas_call(
        functools.partial(combine_kernel, layout),
        out_shape=[
            f32(rows, wide, sources),
            f32(shared_rows, wide, sources),
            f32(rows, blocks, sources),
        ],
        in_specs=[vmem()] * (1 + owners),
        out_specs=[vmem()] * 3,
        compiler_params=params(),
        name="combine",
    )(match, *got)

    dense = pl.pallas_call(
        functools.partial(dense_kernel, rows),
        out_shape=[f32(rows, blocks, sources)] * owners,
        in_specs=[smem(), vmem()],
        out_specs=[vmem()] * owners,
        compiler_params=params(),
        name="dense",
    )(block_lists, gradient(spread(slot_piece, slot_short)))
    own = functools.reduce(lambda a, b: a + b, round_tiles(dense), own_first)
    whole = pl.pallas_call(
        functools.partial(final_kernel, layout, spacing),
        out_shape=f32(param_rows, blocks, sources),
        in_specs=[vmem()] * (1 + 2 * epochs),
        out_specs=vmem(),
        scratch_shapes=[pltpu.VMEM((BANDS, epochs, rows, blocks, sources), F32)],
        compiler_params=params(),
        name="final",
    )(by_row, *spread(own, own))
    return jnp.transpose(whole, (1, 0, 2))


def solution(mesh):
    return jax.shard_map(
        shards,
        mesh=mesh,
        in_specs=(
            P(("region", "tile"), None, None),
            P(("region", "tile"), "epoch", "band", None, None),
            P(("region", "tile"), "epoch", "band", None, None),
            P(("region", "epoch"), "band"),
            P(("region", "tile"), None),
            P(("region", "tile")),
            P(("region", "tile"), None, None),
        ),
        out_specs=P(("region", "tile"), None, None),
        check_vma=False,
    )
```

```python
import functools
import math

import jax
import jax.numpy as jnp
from jax import lax
from jax.experimental import pallas as pl
from jax.experimental.pallas import tpu as pltpu
from jax.sharding import PartitionSpec as P

ITERS = 2
STEP = 0.005
POSITION_RATE = 1.0 / 64.0
COMPS = 7
BANDS = 2
SHARED = 4 * COMPS
HALF = SHARED // BANDS
LOG2E = math.log2(math.e)
F32 = jnp.float32
BF16 = jnp.bfloat16
MIB = 1024 * 1024


def quarter_layout(epochs):
    shared_rows = -(-HALF // epochs)
    rows = -(-(HALF + COMPS) // epochs)
    pieces, amp = [], 0
    for q in range(epochs):
        piece = [("s", i) for i in range(q * shared_rows, min((q + 1) * shared_rows, HALF))]
        while len(piece) < rows and amp < COMPS:
            piece.append(("a", amp))
            amp += 1
        pieces.append(piece + [None] * (rows - len(piece)))
    return shared_rows, rows, pieces


def row_of(band, entry):
    kind, i = entry
    if kind == "a":
        return 2 + 6 * i + 4 + band, None
    k, c = divmod(HALF * band + i, COMPS)
    return 2 + 6 * c + k, (k if k < 2 else None)


def split3(x):
    hi = x.astype(BF16)
    rest = x - hi.astype(F32)
    mid = rest.astype(BF16)
    low = (rest - mid.astype(F32)).astype(BF16)
    return jnp.concatenate([hi, mid, low], axis=0)


def pick(matrix, rows):
    wide = jnp.concatenate([matrix, matrix, matrix], axis=1).astype(BF16)
    return jnp.dot(wide, split3(rows), preferred_element_type=F32)


def vmem():
    return pl.BlockSpec(memory_space=pltpu.VMEM)


def smem():
    return pl.BlockSpec(memory_space=pltpu.SMEM)


def f32(*shape):
    return jax.ShapeDtypeStruct(shape, F32)


def params(mib=4):
    return pltpu.CompilerParams(vmem_limit_bytes=mib * MIB)


def pack_kernel(layout, spacing, lists_ref, params_ref, out_ref):
    shared_rows, rows, pieces = layout
    band, epoch = lax.axis_index("band"), lax.axis_index("epoch")
    for b in range(BANDS):
        for q in range(len(pieces)):

            @pl.when((band == b) & (epoch == q))
            def _():
                for p, entry in enumerate(pieces[q]):
                    if entry is None:
                        out_ref[p] = jnp.zeros(out_ref.shape[1:], F32)
                        continue
                    row, position = row_of(b, entry)
                    value = params_ref[row]
                    if position is not None:
                        value = spacing * params_ref[position] + value
                    out_ref[p] = value

    tiles, slots = lists_ref.shape
    lane = lax.broadcasted_iota(jnp.int32, (8, 128), 1)
    ids = jnp.zeros((8, 128), jnp.int32)
    for t in range(tiles):
        for s in range(slots):
            ids = jnp.where(lane == t * slots + s, lists_ref[t, s], ids)
    out_ref[rows] = ids.astype(F32)


def select_kernel(layout, lists_ref, *refs):
    shared_rows, rows, pieces = layout
    got, (out_ref, short_ref, match_ref) = refs[:-3], refs[-3:]
    owners = len(got)
    tiles, slots = lists_ref.shape
    blocks = got[0].shape[1]
    wide = tiles * slots
    me = lax.axis_index("tile")

    def slot_ids(shape):
        line = lax.broadcasted_iota(jnp.int32, shape, 0)
        ids = jnp.zeros(shape, jnp.int32)
        for t in range(tiles):
            for s in range(slots):
                ids = jnp.where(line == t * slots + s, lists_ref[t, s], ids)
        return ids

    shape = (wide, owners * blocks)
    lane = lax.broadcasted_iota(jnp.int32, shape, 1)
    held = lax.rem(me - lane // blocks + owners, owners) * blocks + lane % blocks
    choose = (slot_ids(shape) == held).astype(F32)
    for p in range(rows):
        chosen = pick(choose, jnp.concatenate([ref[p] for ref in got], axis=0))
        out_ref[p] = chosen
        if p < shared_rows:
            short_ref[p] = chosen

    shape = (wide + blocks, owners * wide)
    line = lax.broadcasted_iota(jnp.int32, shape, 0)
    own = jnp.where(line < wide, slot_ids(shape), me * blocks + line - wide).astype(F32)
    sent = jnp.concatenate([ref[rows, :1, :wide] for ref in got], axis=1)
    match_ref[...] = (own == sent).astype(F32)


def put_together(layout, band, epoch, ins, half, other, shared, amps):
    shared_rows, rows, pieces = layout
    epochs = len(pieces)
    for k in range(epochs):
        q = lax.rem(epoch - k + epochs, epochs)
        half[q] = ins[k][...]
        other[q] = ins[epochs + k][...]
    for q, piece in enumerate(pieces):
        for p, entry in enumerate(piece):
            if entry is None:
                continue
            kind, i = entry
            if kind == "s":
                shared[band, i] = half[q, p]
                shared[1 - band, i] = other[q, p]
            else:
                amps[i] = half[q, p]


def step_kernel(layout, later, counts_ref, offsets_ref, psf_ref, data_ref, weight_ref, *refs):
    shared_rows, rows, pieces = layout
    epochs = len(pieces)
    taken = 2 * epochs * (2 if later else 1)
    ins, refs = refs[:taken], refs[taken:]
    outs, refs = refs[: 2 * epochs], refs[2 * epochs :]
    shared, amps, derived, pieces_x, pieces_y, image, sums, half, other = refs[:9]
    band, epoch = lax.axis_index("band"), lax.axis_index("epoch")
    tiles = data_ref.shape[0]
    pixels = data_ref.shape[-1]
    wide = shared.shape[2]
    slots = wide // tiles
    spacing = pixels / 8.0

    put_together(layout, band, epoch, ins[: 2 * epochs], half, other, shared, amps)

    def row(k, c):
        r = k * COMPS + c
        return r // HALF, r % HALF

    if later:
        moved, moved_amps = refs[9:]
        put_together(layout, band, epoch, ins[2 * epochs :], half, other, moved, moved_amps)
        for k in range(4):
            shift = 0.0
            if k < 2:
                shift = functools.reduce(lambda a, b: a + b, [moved[row(k, c)] for c in range(COMPS)])
                shift = shift * (spacing * spacing * POSITION_RATE)
            for c in range(COMPS):
                shared[row(k, c)] = shared[row(k, c)] - STEP * (moved[row(k, c)] + shift)
        for c in range(COMPS):
            amps[c] = amps[c] - STEP * moved_amps[c]

    psf = psf_ref[0, 0]
    line_of = lax.broadcasted_iota(jnp.int32, (wide, 128), 0)
    live = jnp.zeros((wide, 128), jnp.bool_)
    for t in range(tiles):
        live = live | ((line_of >= t * slots) & (line_of < t * slots + counts_ref[t]))
    for c in range(COMPS):
        lw, an = shared[row(2, c)], shared[row(3, c)]
        derived[0, c] = shared[row(0, c)]
        derived[1, c] = shared[row(1, c)]
        derived[2, c] = (-0.5 * LOG2E) / (jnp.exp(2.0 * (lw + an)) + psf * psf)
        derived[3, c] = (-0.5 * LOG2E) / (jnp.exp(2.0 * (lw - an)) + psf * psf)
        derived[4, c] = jnp.where(live, amps[c], 0.0)
    sums[...] = jnp.zeros_like(sums)

    grid = lax.broadcasted_iota(jnp.int32, (pixels, 128), 0).astype(F32)

    def cut(x):
        hi = x.astype(BF16)
        return jnp.concatenate([hi, (x - hi.astype(F32)).astype(BF16)], axis=0)

    def stack(x):
        hi = x.astype(BF16)
        return jnp.concatenate([hi, hi], axis=1), (x - hi.astype(F32)).astype(BF16)

    def times(left, right):
        near = jnp.dot(left[0], right, preferred_element_type=F32)
        return near + jnp.dot(left[1], right[:pixels], preferred_element_type=F32)

    def total(x):
        return jnp.sum(x, axis=0, keepdims=True)

    def line(index, c, s):
        return derived[index, c, pl.ds(s, 1), :]

    together = 2
    for t in range(tiles):
        trips = (counts_ref[t] + together - 1) // together
        image[...] = jnp.zeros_like(image)

        def render(i, carry):
            for u in range(together):
                s = i * together + u
                g = t * slots + s
                off_x = offsets_ref[t, 0, s].astype(F32)
                off_y = offsets_ref[t, 1, s].astype(F32)
                for c in range(COMPS):
                    d = grid - (line(0, c, g) + off_x)
                    e = jnp.exp2(d * d * line(2, c, g))
                    pieces_x[s, :, c * 128 : (c + 1) * 128] = cut(e)
                    d = grid - (line(1, c, g) + off_y)
                    e = jnp.exp2(d * d * line(3, c, g))
                    pieces_y[s, :, c * 128 : (c + 1) * 128] = cut(e * line(4, c, g))
                image[...] += lax.dot_general(
                    pieces_x[s], pieces_y[s], (((1,), (1,)), ((), ())), preferred_element_type=F32
                )
            return carry

        lax.fori_loop(0, trips, render, 0)

        model = (image[:pixels, :pixels] + image[pixels:, pixels:]) + (
            image[:pixels, pixels:] + image[pixels:, :pixels]
        )
        cotangent = weight_ref[t, 0, 0] * (model - data_ref[t, 0, 0])
        left_x, left_y = stack(cotangent), stack(cotangent.T)

        def pull(i, carry):
            for u in range(together):
                s = i * together + u
                g = t * slots + s
                off_x = offsets_ref[t, 0, s].astype(F32)
                off_y = offsets_ref[t, 1, s].astype(F32)
                for first in range(0, COMPS, 2):
                    here = min(2, COMPS - first)
                    span = pl.ds(first * 128, 128 * here)
                    by_x = times(left_x, pieces_y[s, :, span])
                    by_y = times(left_y, pieces_x[s, :, span])
                    for n in range(here):
                        c = first + n
                        d = grid - (line(0, c, g) + off_x)
                        e = jnp.exp2(d * d * line(2, c, g)) * by_x[:, n * 128 : (n + 1) * 128]
                        e1 = e * d
                        sums[0, c, pl.ds(g, 1), :] = total(e1)
                        sums[1, c, pl.ds(g, 1), :] = total(e1 * d)
                        d = grid - (line(1, c, g) + off_y)
                        e = jnp.exp2(d * d * line(3, c, g)) * by_y[:, n * 128 : (n + 1) * 128]
                        e1 = e * d
                        sums[2, c, pl.ds(g, 1), :] = total(e1)
                        sums[3, c, pl.ds(g, 1), :] = total(e1 * d)
                        sums[4, c, pl.ds(g, 1), :] = total(e)
            return carry

        lax.fori_loop(0, trips, pull, 0)

    def keep(x):
        return jnp.where(live, x, 0.0)

    for c in range(COMPS):
        lw, an = shared[row(2, c)], shared[row(3, c)]
        wide_x, wide_y = jnp.exp(2.0 * (lw + an)), jnp.exp(2.0 * (lw - an))
        inv_x, inv_y = 1.0 / (wide_x + psf * psf), 1.0 / (wide_y + psf * psf)
        amp = amps[c]
        var_x = keep(sums[1, c] * inv_x * (inv_x * wide_x))
        var_y = keep(amp * sums[3, c] * inv_y * (inv_y * wide_y))
        shared[row(0, c)] = keep(sums[0, c] * inv_x)
        shared[row(1, c)] = keep(amp * sums[2, c] * inv_y)
        shared[row(2, c)] = var_x + var_y
        shared[row(3, c)] = var_x - var_y
        amps[c] = keep(sums[4, c])
    none = jnp.zeros((wide, 128), F32)
    for q, piece in enumerate(pieces):
        for p, entry in enumerate(piece):
            is_shared = entry is not None and entry[0] == "s"
            if is_shared:
                half[q, p] = shared[band, entry[1]]
            else:
                half[q, p] = none if entry is None else amps[entry[1]]
            if p < shared_rows:
                other[q, p] = shared[1 - band, entry[1]] if is_shared else none
    for k in range(epochs):
        outs[k][...] = half[lax.rem(epoch + k, epochs)]
        outs[epochs + k][...] = other[lax.rem(epoch + k, epochs)]


def step_gradient(layout, counts, offsets, psf, data, weight, slot_rows, moved):
    shared_rows, rows, pieces = layout
    epochs = len(pieces)
    later = moved is not None
    tiles, _, slots = offsets.shape
    pixels = data.shape[-1]
    wide = tiles * slots
    shapes = [(rows, wide, 128)] * epochs + [(shared_rows, wide, 128)] * epochs
    ins = slot_rows + (moved or [])
    together = [pltpu.VMEM((BANDS, HALF, wide, 128), F32), pltpu.VMEM((COMPS, wide, 128), F32)]
    return pl.pallas_call(
        functools.partial(step_kernel, layout, later),
        out_shape=[f32(*s) for s in shapes],
        in_specs=[smem()] * 3 + [vmem()] * (2 + len(ins)),
        out_specs=[vmem()] * len(shapes),
        scratch_shapes=together
        + [
            pltpu.VMEM((5, COMPS, wide, 128), F32),
            pltpu.VMEM((slots, 2 * pixels, COMPS * 128), BF16),
            pltpu.VMEM((slots, 2 * pixels, COMPS * 128), BF16),
            pltpu.VMEM((2 * pixels, 2 * pixels), F32),
            pltpu.VMEM((5, COMPS, wide, 128), F32),
            pltpu.VMEM((epochs, rows, wide, 128), F32),
            pltpu.VMEM((epochs, shared_rows, wide, 128), F32),
        ]
        + (together if later else []),
        compiler_params=params(32),
        name="later_step" if later else "first_step",
    )(counts, offsets, psf, data, weight, *ins)


def combine_kernel(layout, match_ref, *refs):
    shared_rows, rows, pieces = layout
    got, (out_ref, short_ref, own_ref) = refs[:-3], refs[-3:]
    wide = out_ref.shape[1]
    match = match_ref[...]
    for p in range(rows):
        both = pick(match, jnp.concatenate([ref[p] for ref in got], axis=0))
        out_ref[p] = both[:wide]
        if p < shared_rows:
            short_ref[p] = both[:wide]
        own_ref[p] = both[wide:]


def dense_kernel(rows, lists_ref, grads, *outs):
    tiles, slots = lists_ref.shape
    owners, blocks = len(outs), outs[0].shape[1]
    shape = (owners * blocks, tiles * slots)
    line = lax.broadcasted_iota(jnp.int32, shape, 0)
    lane = lax.broadcasted_iota(jnp.int32, shape, 1)
    me = lax.axis_index("tile")
    target = lax.rem(me + line // blocks, owners) * blocks + line % blocks
    ids = jnp.zeros(shape, jnp.int32)
    for t in range(tiles):
        for s in range(slots):
            ids = jnp.where(lane == t * slots + s, lists_ref[t, s], ids)
    match = (ids == target).astype(F32)
    for p in range(rows):
        dense = pick(match, grads[p])
        for k, out in enumerate(outs):
            out[p] = dense[k * blocks : (k + 1) * blocks]


def final_kernel(layout, spacing, params_ref, *refs):
    shared_rows, rows, pieces = layout
    epochs = len(pieces)
    ins, (out_ref, held) = refs[: 2 * epochs], refs[2 * epochs :]
    band, epoch = lax.axis_index("band"), lax.axis_index("epoch")
    for k in range(epochs):
        q = lax.rem(epoch - k + epochs, epochs)
        held[band, q] = ins[k][...]
        held[1 - band, q] = ins[epochs + k][...]
    shift = [0.0, 0.0]
    for b in range(BANDS):
        for q, piece in enumerate(pieces):
            for p, entry in enumerate(piece):
                if entry is None:
                    continue
                row, position = row_of(b, entry)
                grad = held[b, q, p]
                out_ref[row] = params_ref[row] - STEP * grad
                if position is not None:
                    shift[position] = shift[position] + grad
    for k in range(2):
        out_ref[k] = params_ref[k] - (STEP * POSITION_RATE * spacing) * shift[k]


def shards(source_params, pixel_data, pixel_weight, psf_width, block_lists, block_counts, block_offsets):
    owners, epochs = lax.axis_size("tile"), lax.axis_size("epoch")
    blocks, param_rows, sources = source_params.shape
    tiles, slots = block_lists.shape
    wide = tiles * slots
    spacing = pixel_data.shape[-1] / 8.0
    layout = quarter_layout(epochs)
    shared_rows, rows, pieces = layout

    def to_peers(same, other):
        kept = [same[0]]
        for k in range(1, epochs):
            kept.append(lax.ppermute(same[k], "epoch", [(i, (i + k) % epochs) for i in range(epochs)]))
        for k in range(epochs):
            pairs = [
                (i * BANDS + b, (i + k) % epochs * BANDS + 1 - b)
                for i in range(epochs)
                for b in range(BANDS)
            ]
            kept.append(lax.ppermute(other[k], ("epoch", "band"), pairs))
        return kept

    def round_tiles(arrays):
        return [arrays[0]] + [
            lax.ppermute(arrays[k], "tile", [(i, (i + k) % owners) for i in range(owners)])
            for k in range(1, owners)
        ]

    def spread(piece, other):
        return to_peers([piece] * epochs, [other] * epochs)

    def summed(parts):
        near = functools.reduce(lambda a, b: a + b, parts[:epochs])
        far = functools.reduce(lambda a, b: a + b, parts[epochs:])
        return near + jnp.pad(far, ((0, rows - shared_rows), (0, 0), (0, 0)))

    by_row = jnp.transpose(source_params, (1, 0, 2))
    offsets = jnp.transpose(block_offsets, (0, 2, 1))
    packed = pl.pallas_call(
        functools.partial(pack_kernel, layout, spacing),
        out_shape=f32(rows + 1, blocks, sources),
        in_specs=[smem(), vmem()],
        out_specs=vmem(),
        compiler_params=params(),
        name="pack",
    )(block_lists, by_row)
    got = round_tiles([packed] * owners)
    slot_piece, slot_short, match = pl.pallas_call(
        functools.partial(select_kernel, layout),
        out_shape=[
            f32(rows, wide, sources),
            f32(shared_rows, wide, sources),
            f32(wide + blocks, owners * wide),
        ],
        in_specs=[smem()] + [vmem()] * owners,
        out_specs=[vmem()] * 3,
        compiler_params=params(),
        name="select",
    )(block_lists, *got)
    slot_rows = spread(slot_piece, slot_short)

    def gradient(moved):
        parts = step_gradient(
            layout, block_counts, offsets, psf_width, pixel_data, pixel_weight, slot_rows, moved
        )
        return summed(to_peers(parts[:epochs], parts[epochs:]))

    got = round_tiles([gradient(None)] * owners)
    slot_piece, slot_short, own_first = pl.pallas_call(
        functools.partial(combine_kernel, layout),
        out_shape=[
            f32(rows, wide, sources),
            f32(shared_rows, wide, sources),
            f32(rows, blocks, sources),
        ],
        in_specs=[vmem()] * (1 + owners),
        out_specs=[vmem()] * 3,
        compiler_params=params(),
        name="combine",
    )(match, *got)

    dense = pl.pallas_call(
        functools.partial(dense_kernel, rows),
        out_shape=[f32(rows, blocks, sources)] * owners,
        in_specs=[smem(), vmem()],
        out_specs=[vmem()] * owners,
        compiler_params=params(),
        name="dense",
    )(block_lists, gradient(spread(slot_piece, slot_short)))
    own = functools.reduce(lambda a, b: a + b, round_tiles(dense), own_first)
    whole = pl.pallas_call(
        functools.partial(final_kernel, layout, spacing),
        out_shape=f32(param_rows, blocks, sources),
        in_specs=[vmem()] * (1 + 2 * epochs),
        out_specs=vmem(),
        scratch_shapes=[pltpu.VMEM((BANDS, epochs, rows, blocks, sources), F32)],
        compiler_params=params(),
        name="final",
    )(by_row, *spread(own, own))
    return jnp.transpose(whole, (1, 0, 2))


def solution(mesh):
    return jax.shard_map(
        shards,
        mesh=mesh,
        in_specs=(
            P(("region", "tile"), None, None),
            P(("region", "tile"), "epoch", "band", None, None),
            P(("region", "tile"), "epoch", "band", None, None),
            P(("region", "epoch"), "band"),
            P(("region", "tile"), None),
            P(("region", "tile")),
            P(("region", "tile"), None, None),
        ),
        out_specs=P(("region", "tile"), None, None),
        check_vma=False,
    )
```

```python
import functools
import math

import jax
import jax.numpy as jnp
from jax import lax
from jax.experimental import pallas as pl
from jax.experimental.pallas import tpu as pltpu
from jax.sharding import PartitionSpec as P

ITERS = 2
STEP = 0.005
POSITION_RATE = 1.0 / 64.0
COMPS = 7
BANDS = 2
SHARED = 4 * COMPS
HALF = SHARED // BANDS
LOG2E = math.log2(math.e)
F32 = jnp.float32
BF16 = jnp.bfloat16
MIB = 1024 * 1024


def quarter_layout(epochs):
    shared_rows = -(-HALF // epochs)
    rows = -(-(HALF + COMPS) // epochs)
    pieces, amp = [], 0
    for q in range(epochs):
        piece = [("s", i) for i in range(q * shared_rows, min((q + 1) * shared_rows, HALF))]
        while len(piece) < rows and amp < COMPS:
            piece.append(("a", amp))
            amp += 1
        pieces.append(piece + [None] * (rows - len(piece)))
    return shared_rows, rows, pieces


def row_of(band, entry):
    kind, i = entry
    if kind == "a":
        return 2 + 6 * i + 4 + band, None
    k, c = divmod(HALF * band + i, COMPS)
    return 2 + 6 * c + k, (k if k < 2 else None)


def split3(x):
    hi = x.astype(BF16)
    rest = x - hi.astype(F32)
    mid = rest.astype(BF16)
    low = (rest - mid.astype(F32)).astype(BF16)
    return jnp.concatenate([hi, mid, low], axis=0)


def pick(matrix, rows):
    wide = jnp.concatenate([matrix, matrix, matrix], axis=1).astype(BF16)
    return jnp.dot(wide, split3(rows), preferred_element_type=F32)


def vmem():
    return pl.BlockSpec(memory_space=pltpu.VMEM)


def smem():
    return pl.BlockSpec(memory_space=pltpu.SMEM)


def f32(*shape):
    return jax.ShapeDtypeStruct(shape, F32)


def params(mib=4):
    return pltpu.CompilerParams(vmem_limit_bytes=mib * MIB)


def pack_kernel(layout, spacing, lists_ref, params_ref, out_ref):
    shared_rows, rows, pieces = layout
    band, epoch = lax.axis_index("band"), lax.axis_index("epoch")
    for b in range(BANDS):
        for q in range(len(pieces)):

            @pl.when((band == b) & (epoch == q))
            def _():
                for p, entry in enumerate(pieces[q]):
                    if entry is None:
                        out_ref[p] = jnp.zeros(out_ref.shape[1:], F32)
                        continue
                    row, position = row_of(b, entry)
                    value = params_ref[row]
                    if position is not None:
                        value = spacing * params_ref[position] + value
                    out_ref[p] = value

    tiles, slots = lists_ref.shape
    lane = lax.broadcasted_iota(jnp.int32, (8, 128), 1)
    ids = jnp.zeros((8, 128), jnp.int32)
    for t in range(tiles):
        for s in range(slots):
            ids = jnp.where(lane == t * slots + s, lists_ref[t, s], ids)
    out_ref[rows] = ids.astype(F32)


def select_kernel(layout, lists_ref, *refs):
    shared_rows, rows, pieces = layout
    got, (out_ref, short_ref, match_ref) = refs[:-3], refs[-3:]
    owners = len(got)
    tiles, slots = lists_ref.shape
    blocks = got[0].shape[1]
    wide = tiles * slots
    me = lax.axis_index("tile")

    def slot_ids(shape):
        line = lax.broadcasted_iota(jnp.int32, shape, 0)
        ids = jnp.zeros(shape, jnp.int32)
        for t in range(tiles):
            for s in range(slots):
                ids = jnp.where(line == t * slots + s, lists_ref[t, s], ids)
        return ids

    shape = (wide, owners * blocks)
    lane = lax.broadcasted_iota(jnp.int32, shape, 1)
    held = lax.rem(me - lane // blocks + owners, owners) * blocks + lane % blocks
    choose = (slot_ids(shape) == held).astype(F32)
    for p in range(rows):
        chosen = pick(choose, jnp.concatenate([ref[p] for ref in got], axis=0))
        out_ref[p] = chosen
        if p < shared_rows:
            short_ref[p] = chosen

    shape = (wide + blocks, owners * wide)
    line = lax.broadcasted_iota(jnp.int32, shape, 0)
    own = jnp.where(line < wide, slot_ids(shape), me * blocks + line - wide).astype(F32)
    sent = jnp.concatenate([ref[rows, :1, :wide] for ref in got], axis=1)
    match_ref[...] = (own == sent).astype(F32)


def put_together(layout, band, epoch, ins, half, other, shared, amps):
    shared_rows, rows, pieces = layout
    epochs = len(pieces)
    for k in range(epochs):
        q = lax.rem(epoch - k + epochs, epochs)
        half[q] = ins[k][...]
        other[q] = ins[epochs + k][...]
    for q, piece in enumerate(pieces):
        for p, entry in enumerate(piece):
            if entry is None:
                continue
            kind, i = entry
            if kind == "s":
                shared[band, i] = half[q, p]
                shared[1 - band, i] = other[q, p]
            else:
                amps[i] = half[q, p]


def row_at(k, c):
    r = k * COMPS + c
    return r // HALF, r % HALF


def cut(x):
    hi = x.astype(BF16)
    return jnp.concatenate([hi, (x - hi.astype(F32)).astype(BF16)], axis=0)


def render_kernel(layout, later, counts_ref, offsets_ref, psf_ref, data_ref, weight_ref, *refs):
    shared_rows, rows, pieces = layout
    epochs = len(pieces)
    taken = 2 * epochs * (2 if later else 1)
    ins, refs = refs[:taken], refs[taken:]
    tiles = data_ref.shape[0]
    cotangents, shared, amps, derived = refs[:4]
    pieces_x, pieces_y, refs = refs[4 : 4 + tiles], refs[4 + tiles : 4 + 2 * tiles], refs[4 + 2 * tiles :]
    image, half, other = refs[:3]
    band, epoch = lax.axis_index("band"), lax.axis_index("epoch")
    pixels = data_ref.shape[-1]
    wide = shared.shape[2]
    slots = wide // tiles
    spacing = pixels / 8.0

    put_together(layout, band, epoch, ins[: 2 * epochs], half, other, shared, amps)
    if later:
        moved, moved_amps = refs[3:]
        put_together(layout, band, epoch, ins[2 * epochs :], half, other, moved, moved_amps)
        for k in range(4):
            shift = 0.0
            if k < 2:
                shift = functools.reduce(lambda a, b: a + b, [moved[row_at(k, c)] for c in range(COMPS)])
                shift = shift * (spacing * spacing * POSITION_RATE)
            for c in range(COMPS):
                shared[row_at(k, c)] = shared[row_at(k, c)] - STEP * (moved[row_at(k, c)] + shift)
        for c in range(COMPS):
            amps[c] = amps[c] - STEP * moved_amps[c]

    psf = psf_ref[0, 0]
    for c in range(COMPS):
        lw, an = shared[row_at(2, c)], shared[row_at(3, c)]
        derived[0, c] = shared[row_at(0, c)]
        derived[1, c] = shared[row_at(1, c)]
        derived[2, c] = (-0.5 * LOG2E) / (jnp.exp(2.0 * (lw + an)) + psf * psf)
        derived[3, c] = (-0.5 * LOG2E) / (jnp.exp(2.0 * (lw - an)) + psf * psf)

    grid = lax.broadcasted_iota(jnp.int32, (pixels, 128), 0).astype(F32)

    for t in range(tiles):
        image[...] = jnp.zeros_like(image)

        def render(s, carry):
            g = t * slots + s
            off_x = offsets_ref[t, 0, s].astype(F32)
            off_y = offsets_ref[t, 1, s].astype(F32)
            for c in range(COMPS):
                d = grid - (derived[0, c, pl.ds(g, 1), :] + off_x)
                e = jnp.exp2(d * d * derived[2, c, pl.ds(g, 1), :])
                pieces_x[t][s, :, c * 128 : (c + 1) * 128] = cut(e)
                d = grid - (derived[1, c, pl.ds(g, 1), :] + off_y)
                e = jnp.exp2(d * d * derived[3, c, pl.ds(g, 1), :])
                pieces_y[t][s, :, c * 128 : (c + 1) * 128] = cut(e * amps[c, pl.ds(g, 1), :])
            image[...] += lax.dot_general(
                pieces_x[t][s], pieces_y[t][s], (((1,), (1,)), ((), ())), preferred_element_type=F32
            )
            return carry

        lax.fori_loop(0, counts_ref[t], render, 0)

        model = (image[:pixels, :pixels] + image[pixels:, pixels:]) + (
            image[:pixels, pixels:] + image[pixels:, :pixels]
        )
        cotangents[t] = weight_ref[t, 0, 0] * (model - data_ref[t, 0, 0])


def pull_kernel(layout, tile, counts_ref, offsets_ref, psf_ref, *refs):
    shared_rows, rows, pieces = layout
    epochs = len(pieces)
    (cotangents, shared, amps, derived, pieces_x, pieces_y), refs = refs[:6], refs[6:]
    outs, (sums, half, other, grads) = refs[: 2 * epochs], refs[2 * epochs :]
    band, epoch = lax.axis_index("band"), lax.axis_index("epoch")
    pixels = cotangents.shape[-1]
    slots = sums.shape[2]
    used = counts_ref[tile]
    cotangent = cotangents[tile]
    grid = lax.broadcasted_iota(jnp.int32, (pixels, 128), 0).astype(F32)

    def stack(x):
        hi = x.astype(BF16)
        return jnp.concatenate([hi, hi], axis=1), (x - hi.astype(F32)).astype(BF16)

    def times(left, right):
        near = jnp.dot(left[0], right, preferred_element_type=F32)
        return near + jnp.dot(left[1], right[:pixels], preferred_element_type=F32)

    def total(x):
        return jnp.sum(x, axis=0, keepdims=True)

    left_x, left_y = stack(cotangent), stack(cotangent.T)
    sums[...] = jnp.zeros_like(sums)

    def pull(s, carry):
        g = tile * slots + s
        off_x = offsets_ref[tile, 0, s].astype(F32)
        off_y = offsets_ref[tile, 1, s].astype(F32)
        for first in range(0, COMPS, 2):
            here = min(2, COMPS - first)
            span = pl.ds(first * 128, 128 * here)
            by_x = times(left_x, pieces_y[s, :, span])
            by_y = times(left_y, pieces_x[s, :, span])
            for n in range(here):
                c = first + n
                d = grid - (derived[0, c, pl.ds(g, 1), :] + off_x)
                e = jnp.exp2(d * d * derived[2, c, pl.ds(g, 1), :]) * by_x[:, n * 128 : (n + 1) * 128]
                e1 = e * d
                sums[0, c, pl.ds(s, 1), :] = total(e1)
                sums[1, c, pl.ds(s, 1), :] = total(e1 * d)
                d = grid - (derived[1, c, pl.ds(g, 1), :] + off_y)
                e = jnp.exp2(d * d * derived[3, c, pl.ds(g, 1), :]) * by_y[:, n * 128 : (n + 1) * 128]
                e1 = e * d
                sums[2, c, pl.ds(s, 1), :] = total(e1)
                sums[3, c, pl.ds(s, 1), :] = total(e1 * d)
                sums[4, c, pl.ds(s, 1), :] = total(e)
        return carry

    lax.fori_loop(0, used, pull, 0)

    live = lax.broadcasted_iota(jnp.int32, (slots, 128), 0) < used
    psf = psf_ref[0, 0]
    at = slice(tile * slots, (tile + 1) * slots)

    def keep(x):
        return jnp.where(live, x, 0.0)

    for c in range(COMPS):
        lw, an = shared[(*row_at(2, c), at)], shared[(*row_at(3, c), at)]
        wide_x, wide_y = jnp.exp(2.0 * (lw + an)), jnp.exp(2.0 * (lw - an))
        inv_x, inv_y = 1.0 / (wide_x + psf * psf), 1.0 / (wide_y + psf * psf)
        amp = amps[c, at]
        var_x = keep(sums[1, c] * inv_x * (inv_x * wide_x))
        var_y = keep(amp * sums[3, c] * inv_y * (inv_y * wide_y))
        grads[row_at(0, c)] = keep(sums[0, c] * inv_x)
        grads[row_at(1, c)] = keep(amp * sums[2, c] * inv_y)
        grads[row_at(2, c)] = var_x + var_y
        grads[row_at(3, c)] = var_x - var_y
    none = jnp.zeros((slots, 128), F32)
    for q, piece in enumerate(pieces):
        for p, entry in enumerate(piece):
            is_shared = entry is not None and entry[0] == "s"
            if is_shared:
                half[q, p] = grads[band, entry[1]]
            else:
                half[q, p] = none if entry is None else keep(sums[4, entry[1]])
            if p < shared_rows:
                other[q, p] = grads[1 - band, entry[1]] if is_shared else none
    for k in range(epochs):
        outs[k][...] = half[lax.rem(epoch + k, epochs)]
        outs[epochs + k][...] = other[lax.rem(epoch + k, epochs)]


def step_gradients(layout, counts, offsets, psf, data, weight, slot_rows, moved):
    shared_rows, rows, pieces = layout
    epochs = len(pieces)
    later = moved is not None
    tiles, _, slots = offsets.shape
    pixels = data.shape[-1]
    wide = tiles * slots
    ins = slot_rows + (moved or [])
    shared, amps = (BANDS, HALF, wide, 128), (COMPS, wide, 128)
    kept = jax.ShapeDtypeStruct((slots, 2 * pixels, COMPS * 128), BF16)
    cotangents, *rest = pl.pallas_call(
        functools.partial(render_kernel, layout, later),
        out_shape=[f32(tiles, pixels, pixels), f32(*shared), f32(*amps), f32(4, *amps)] + [kept] * (2 * tiles),
        in_specs=[smem()] * 3 + [vmem()] * (2 + len(ins)),
        out_specs=[vmem()] * (4 + 2 * tiles),
        scratch_shapes=[
            pltpu.VMEM((2 * pixels, 2 * pixels), F32),
            pltpu.VMEM((epochs, rows, wide, 128), F32),
            pltpu.VMEM((epochs, shared_rows, wide, 128), F32),
        ]
        + ([pltpu.VMEM(shared, F32), pltpu.VMEM(amps, F32)] if later else []),
        compiler_params=params(20),
        name="later_render" if later else "first_render",
    )(counts, offsets, psf, data, weight, *ins)
    tables, kept_x, kept_y = rest[:3], rest[3 : 3 + tiles], rest[3 + tiles :]
    shapes = [(rows, slots, 128)] * epochs + [(shared_rows, slots, 128)] * epochs
    return [
        pl.pallas_call(
            functools.partial(pull_kernel, layout, t),
            out_shape=[f32(*s) for s in shapes],
            in_specs=[smem()] * 3 + [vmem()] * 6,
            out_specs=[vmem()] * len(shapes),
            scratch_shapes=[
                pltpu.VMEM((5, COMPS, slots, 128), F32),
                pltpu.VMEM((epochs, rows, slots, 128), F32),
                pltpu.VMEM((epochs, shared_rows, slots, 128), F32),
                pltpu.VMEM((BANDS, HALF, slots, 128), F32),
            ],
            compiler_params=params(12),
            name=f"pull_{t}",
        )(counts, offsets, psf, cotangents, *tables, kept_x[t], kept_y[t])
        for t in range(tiles)
    ]


def combine_kernel(layout, match_ref, *refs):
    shared_rows, rows, pieces = layout
    got, (out_ref, short_ref, own_ref) = refs[:-3], refs[-3:]
    wide = out_ref.shape[1]
    match = match_ref[...]
    for p in range(rows):
        both = pick(match, jnp.concatenate([ref[p] for ref in got], axis=0))
        out_ref[p] = both[:wide]
        if p < shared_rows:
            short_ref[p] = both[:wide]
        own_ref[p] = both[wide:]


def dense_kernel(rows, lists_ref, grads, *outs):
    tiles, slots = lists_ref.shape
    owners, blocks = len(outs), outs[0].shape[1]
    shape = (owners * blocks, tiles * slots)
    line = lax.broadcasted_iota(jnp.int32, shape, 0)
    lane = lax.broadcasted_iota(jnp.int32, shape, 1)
    me = lax.axis_index("tile")
    target = lax.rem(me + line // blocks, owners) * blocks + line % blocks
    ids = jnp.zeros(shape, jnp.int32)
    for t in range(tiles):
        for s in range(slots):
            ids = jnp.where(lane == t * slots + s, lists_ref[t, s], ids)
    match = (ids == target).astype(F32)
    for p in range(rows):
        dense = pick(match, grads[p])
        for k, out in enumerate(outs):
            out[p] = dense[k * blocks : (k + 1) * blocks]


def final_kernel(layout, spacing, params_ref, *refs):
    shared_rows, rows, pieces = layout
    epochs = len(pieces)
    ins, (out_ref, held) = refs[: 2 * epochs], refs[2 * epochs :]
    band, epoch = lax.axis_index("band"), lax.axis_index("epoch")
    for k in range(epochs):
        q = lax.rem(epoch - k + epochs, epochs)
        held[band, q] = ins[k][...]
        held[1 - band, q] = ins[epochs + k][...]
    shift = [0.0, 0.0]
    for b in range(BANDS):
        for q, piece in enumerate(pieces):
            for p, entry in enumerate(piece):
                if entry is None:
                    continue
                row, position = row_of(b, entry)
                grad = held[b, q, p]
                out_ref[row] = params_ref[row] - STEP * grad
                if position is not None:
                    shift[position] = shift[position] + grad
    for k in range(2):
        out_ref[k] = params_ref[k] - (STEP * POSITION_RATE * spacing) * shift[k]


def shards(source_params, pixel_data, pixel_weight, psf_width, block_lists, block_counts, block_offsets):
    owners, epochs = lax.axis_size("tile"), lax.axis_size("epoch")
    blocks, param_rows, sources = source_params.shape
    tiles, slots = block_lists.shape
    wide = tiles * slots
    spacing = pixel_data.shape[-1] / 8.0
    layout = quarter_layout(epochs)
    shared_rows, rows, pieces = layout

    def to_peers(same, other):
        kept = [same[0]]
        for k in range(1, epochs):
            kept.append(lax.ppermute(same[k], "epoch", [(i, (i + k) % epochs) for i in range(epochs)]))
        for k in range(epochs):
            pairs = [
                (i * BANDS + b, (i + k) % epochs * BANDS + 1 - b)
                for i in range(epochs)
                for b in range(BANDS)
            ]
            kept.append(lax.ppermute(other[k], ("epoch", "band"), pairs))
        return kept

    def round_tiles(arrays):
        return [arrays[0]] + [
            lax.ppermute(arrays[k], "tile", [(i, (i + k) % owners) for i in range(owners)])
            for k in range(1, owners)
        ]

    def spread(piece, other):
        return to_peers([piece] * epochs, [other] * epochs)

    def summed(parts):
        near = functools.reduce(lambda a, b: a + b, parts[:epochs])
        far = functools.reduce(lambda a, b: a + b, parts[epochs:])
        return near + jnp.pad(far, ((0, rows - shared_rows), (0, 0), (0, 0)))

    by_row = jnp.transpose(source_params, (1, 0, 2))
    offsets = jnp.transpose(block_offsets, (0, 2, 1))
    packed = pl.pallas_call(
        functools.partial(pack_kernel, layout, spacing),
        out_shape=f32(rows + 1, blocks, sources),
        in_specs=[smem(), vmem()],
        out_specs=vmem(),
        compiler_params=params(),
        name="pack",
    )(block_lists, by_row)
    got = round_tiles([packed] * owners)
    slot_piece, slot_short, match = pl.pallas_call(
        functools.partial(select_kernel, layout),
        out_shape=[
            f32(rows, wide, sources),
            f32(shared_rows, wide, sources),
            f32(wide + blocks, owners * wide),
        ],
        in_specs=[smem()] + [vmem()] * owners,
        out_specs=[vmem()] * 3,
        compiler_params=params(),
        name="select",
    )(block_lists, *got)
    slot_rows = spread(slot_piece, slot_short)

    def gradient(moved):
        sums = []
        for parts in step_gradients(
            layout, block_counts, offsets, psf_width, pixel_data, pixel_weight, slot_rows, moved
        ):
            sums.append(summed(to_peers(parts[:epochs], parts[epochs:])))
        return jnp.concatenate(sums, axis=1)

    got = round_tiles([gradient(None)] * owners)
    slot_piece, slot_short, own_first = pl.pallas_call(
        functools.partial(combine_kernel, layout),
        out_shape=[
            f32(rows, wide, sources),
            f32(shared_rows, wide, sources),
            f32(rows, blocks, sources),
        ],
        in_specs=[vmem()] * (1 + owners),
        out_specs=[vmem()] * 3,
        compiler_params=params(),
        name="combine",
    )(match, *got)

    dense = pl.pallas_call(
        functools.partial(dense_kernel, rows),
        out_shape=[f32(rows, blocks, sources)] * owners,
        in_specs=[smem(), vmem()],
        out_specs=[vmem()] * owners,
        compiler_params=params(),
        name="dense",
    )(block_lists, gradient(spread(slot_piece, slot_short)))
    own = functools.reduce(lambda a, b: a + b, round_tiles(dense), own_first)
    whole = pl.pallas_call(
        functools.partial(final_kernel, layout, spacing),
        out_shape=f32(param_rows, blocks, sources),
        in_specs=[vmem()] * (1 + 2 * epochs),
        out_specs=vmem(),
        scratch_shapes=[pltpu.VMEM((BANDS, epochs, rows, blocks, sources), F32)],
        compiler_params=params(),
        name="final",
    )(by_row, *spread(own, own))
    return jnp.transpose(whole, (1, 0, 2))


def solution(mesh):
    return jax.shard_map(
        shards,
        mesh=mesh,
        in_specs=(
            P(("region", "tile"), None, None),
            P(("region", "tile"), "epoch", "band", None, None),
            P(("region", "tile"), "epoch", "band", None, None),
            P(("region", "epoch"), "band"),
            P(("region", "tile"), None),
            P(("region", "tile")),
            P(("region", "tile"), None, None),
        ),
        out_specs=P(("region", "tile"), None, None),
        check_vma=False,
    )
```

```python
import functools
import math

import jax
import jax.numpy as jnp
from jax import lax
from jax.experimental import pallas as pl
from jax.experimental.pallas import tpu as pltpu
from jax.sharding import PartitionSpec as P

ITERS = 2
STEP = 0.005
POSITION_RATE = 1.0 / 64.0
COMPS = 7
BANDS = 2
SHARED = 4 * COMPS
HALF = SHARED // BANDS
SPLIT_UNIT = 49152.0
SPLIT_SCALE = 65536.0
LOG2E = math.log2(math.e)
F32 = jnp.float32
BF16 = jnp.bfloat16
MIB = 1024 * 1024


def quarter_layout(epochs):
    shared_rows = -(-HALF // epochs)
    rows = -(-(HALF + COMPS) // epochs)
    pieces, amp = [], 0
    for q in range(epochs):
        piece = [("s", i) for i in range(q * shared_rows, min((q + 1) * shared_rows, HALF))]
        while len(piece) < rows and amp < COMPS:
            piece.append(("a", amp))
            amp += 1
        pieces.append(piece + [None] * (rows - len(piece)))
    return shared_rows, rows, pieces


def row_of(band, entry):
    kind, i = entry
    if kind == "a":
        return 2 + 6 * i + 4 + band, None
    k, c = divmod(HALF * band + i, COMPS)
    return 2 + 6 * c + k, (k if k < 2 else None)


def split3(x):
    hi = x.astype(BF16)
    rest = x - hi.astype(F32)
    mid = rest.astype(BF16)
    low = (rest - mid.astype(F32)).astype(BF16)
    return jnp.concatenate([hi, mid, low], axis=0)


def pick(matrix, rows):
    wide = jnp.concatenate([matrix, matrix, matrix], axis=1).astype(BF16)
    return jnp.dot(wide, split3(rows), preferred_element_type=F32)


def vmem():
    return pl.BlockSpec(memory_space=pltpu.VMEM)


def smem():
    return pl.BlockSpec(memory_space=pltpu.SMEM)


def f32(*shape):
    return jax.ShapeDtypeStruct(shape, F32)


def params(mib=4):
    return pltpu.CompilerParams(vmem_limit_bytes=mib * MIB)


def pack_kernel(layout, spacing, lists_ref, params_ref, out_ref):
    shared_rows, rows, pieces = layout
    band, epoch = lax.axis_index("band"), lax.axis_index("epoch")
    for b in range(BANDS):
        for q in range(len(pieces)):

            @pl.when((band == b) & (epoch == q))
            def _():
                for p, entry in enumerate(pieces[q]):
                    if entry is None:
                        out_ref[p] = jnp.zeros(out_ref.shape[1:], F32)
                        continue
                    row, position = row_of(b, entry)
                    value = params_ref[row]
                    if position is not None:
                        value = spacing * params_ref[position] + value
                    out_ref[p] = value

    tiles, slots = lists_ref.shape
    lane = lax.broadcasted_iota(jnp.int32, (8, 128), 1)
    ids = jnp.zeros((8, 128), jnp.int32)
    for t in range(tiles):
        for s in range(slots):
            ids = jnp.where(lane == t * slots + s, lists_ref[t, s], ids)
    out_ref[rows] = ids.astype(F32)


def select_kernel(layout, lists_ref, *refs):
    shared_rows, rows, pieces = layout
    got, (out_ref, short_ref, match_ref) = refs[:-3], refs[-3:]
    owners = len(got)
    tiles, slots = lists_ref.shape
    blocks = got[0].shape[1]
    wide = tiles * slots
    me = lax.axis_index("tile")

    def slot_ids(shape):
        line = lax.broadcasted_iota(jnp.int32, shape, 0)
        ids = jnp.zeros(shape, jnp.int32)
        for t in range(tiles):
            for s in range(slots):
                ids = jnp.where(line == t * slots + s, lists_ref[t, s], ids)
        return ids

    shape = (wide, owners * blocks)
    lane = lax.broadcasted_iota(jnp.int32, shape, 1)
    held = lax.rem(me - lane // blocks + owners, owners) * blocks + lane % blocks
    choose = (slot_ids(shape) == held).astype(F32)
    for p in range(rows):
        chosen = pick(choose, jnp.concatenate([ref[p] for ref in got], axis=0))
        out_ref[p] = chosen
        if p < shared_rows:
            short_ref[p] = chosen

    shape = (wide + blocks, owners * wide)
    line = lax.broadcasted_iota(jnp.int32, shape, 0)
    own = jnp.where(line < wide, slot_ids(shape), me * blocks + line - wide).astype(F32)
    sent = jnp.concatenate([ref[rows, :1, :wide] for ref in got], axis=1)
    match_ref[...] = (own == sent).astype(F32)


def put_together(layout, band, epoch, ins, half, other, shared, amps):
    shared_rows, rows, pieces = layout
    epochs = len(pieces)
    for k in range(epochs):
        q = lax.rem(epoch - k + epochs, epochs)
        half[q] = ins[k][...]
        other[q] = ins[epochs + k][...]
    for q, piece in enumerate(pieces):
        for p, entry in enumerate(piece):
            if entry is None:
                continue
            kind, i = entry
            if kind == "s":
                shared[band, i] = half[q, p]
                shared[1 - band, i] = other[q, p]
            else:
                amps[i] = half[q, p]


def step_kernel(layout, later, counts_ref, offsets_ref, psf_ref, data_ref, weight_ref, *refs):
    shared_rows, rows, pieces = layout
    epochs = len(pieces)
    taken = 2 * epochs * (2 if later else 1)
    ins, refs = refs[:taken], refs[taken:]
    outs, refs = refs[: 2 * epochs], refs[2 * epochs :]
    shared, amps, derived, prof_y, pieces_x, pieces_y, image, sums, half, other = refs[:10]
    band, epoch = lax.axis_index("band"), lax.axis_index("epoch")
    tiles = data_ref.shape[0]
    pixels = data_ref.shape[-1]
    wide = shared.shape[2]
    slots = wide // tiles
    spacing = pixels / 8.0

    put_together(layout, band, epoch, ins[: 2 * epochs], half, other, shared, amps)

    def row(k, c):
        r = k * COMPS + c
        return r // HALF, r % HALF

    if later:
        moved, moved_amps = refs[10:]
        put_together(layout, band, epoch, ins[2 * epochs :], half, other, moved, moved_amps)
        for k in range(4):
            shift = 0.0
            if k < 2:
                shift = functools.reduce(lambda a, b: a + b, [moved[row(k, c)] for c in range(COMPS)])
                shift = shift * (spacing * spacing * POSITION_RATE)
            for c in range(COMPS):
                shared[row(k, c)] = shared[row(k, c)] - STEP * (moved[row(k, c)] + shift)
        for c in range(COMPS):
            amps[c] = amps[c] - STEP * moved_amps[c]

    psf = psf_ref[0, 0]
    line_of = lax.broadcasted_iota(jnp.int32, (wide, 128), 0)
    live = jnp.zeros((wide, 128), jnp.bool_)
    for t in range(tiles):
        live = live | ((line_of >= t * slots) & (line_of < t * slots + counts_ref[t]))
    for c in range(COMPS):
        lw, an = shared[row(2, c)], shared[row(3, c)]
        derived[0, c] = shared[row(0, c)]
        derived[1, c] = shared[row(1, c)]
        derived[2, c] = (-0.5 * LOG2E) / (jnp.exp(2.0 * (lw + an)) + psf * psf)
        derived[3, c] = (-0.5 * LOG2E) / (jnp.exp(2.0 * (lw - an)) + psf * psf)
        derived[4, c] = jnp.where(live, amps[c], 0.0)
        derived[5, c] = derived[4, c] * SPLIT_SCALE
    sums[...] = jnp.zeros_like(sums)

    grid = lax.broadcasted_iota(jnp.int32, (pixels, 128), 0).astype(F32)

    def cut(x, large):
        hi = (x + large) - large
        return jnp.concatenate([hi, x - hi], axis=0)

    def stack(x):
        hi = x.astype(BF16).astype(F32)
        return jnp.concatenate([hi, hi], axis=1), x - hi

    def times(left, right):
        near = jnp.dot(left[0], right, preferred_element_type=F32)
        return near + jnp.dot(left[1], right[:pixels], preferred_element_type=F32)

    def total(x):
        return jnp.sum(x, axis=0, keepdims=True)

    def line(index, c, s):
        return derived[index, c, pl.ds(s, 1), :]

    together = 2
    for t in range(tiles):
        trips = (counts_ref[t] + together - 1) // together
        image[...] = jnp.zeros_like(image)

        def render(i, carry):
            for u in range(together):
                s = i * together + u
                g = t * slots + s
                off_x = offsets_ref[t, 0, s].astype(F32)
                off_y = offsets_ref[t, 1, s].astype(F32)
                for c in range(COMPS):
                    d = grid - (line(0, c, g) + off_x)
                    e = jnp.exp2(d * d * line(2, c, g))
                    pieces_x[s, :, c * 128 : (c + 1) * 128] = cut(e, SPLIT_UNIT)
                    d = grid - (line(1, c, g) + off_y)
                    e = jnp.exp2(d * d * line(3, c, g))
                    prof_y[s * COMPS + c] = e
                    pieces_y[s, :, c * 128 : (c + 1) * 128] = cut(e * line(4, c, g), line(5, c, g))
                image[...] += lax.dot_general(
                    pieces_x[s], pieces_y[s], (((1,), (1,)), ((), ())), preferred_element_type=F32
                )
            return carry

        lax.fori_loop(0, trips, render, 0)

        model = (image[:pixels, :pixels] + image[pixels:, pixels:]) + (
            image[:pixels, pixels:] + image[pixels:, :pixels]
        )
        cotangent = weight_ref[t, 0, 0] * (model - data_ref[t, 0, 0])
        left_x, left_y = stack(cotangent), stack(cotangent.T)

        def pull(i, carry):
            for u in range(together):
                s = i * together + u
                g = t * slots + s
                off_x = offsets_ref[t, 0, s].astype(F32)
                off_y = offsets_ref[t, 1, s].astype(F32)
                for first in range(0, COMPS, 2):
                    here = min(2, COMPS - first)
                    span = pl.ds(first * 128, 128 * here)
                    by_x = times(left_x, pieces_y[s, :, span])
                    by_y = times(left_y, pieces_x[s, :, span])
                    for n in range(here):
                        c = first + n
                        d = grid - (line(0, c, g) + off_x)
                        at = slice(c * 128, (c + 1) * 128)
                        e = pieces_x[s, :pixels, at] + pieces_x[s, pixels:, at]
                        e = e * by_x[:, n * 128 : (n + 1) * 128]
                        e1 = e * d
                        sums[0, c, pl.ds(g, 1), :] = total(e1)
                        sums[1, c, pl.ds(g, 1), :] = total(e1 * d)
                        d = grid - (line(1, c, g) + off_y)
                        e = prof_y[s * COMPS + c] * by_y[:, n * 128 : (n + 1) * 128]
                        e1 = e * d
                        sums[2, c, pl.ds(g, 1), :] = total(e1)
                        sums[3, c, pl.ds(g, 1), :] = total(e1 * d)
                        sums[4, c, pl.ds(g, 1), :] = total(e)
            return carry

        lax.fori_loop(0, trips, pull, 0)

    def keep(x):
        return jnp.where(live, x, 0.0)

    for c in range(COMPS):
        lw, an = shared[row(2, c)], shared[row(3, c)]
        wide_x, wide_y = jnp.exp(2.0 * (lw + an)), jnp.exp(2.0 * (lw - an))
        inv_x, inv_y = 1.0 / (wide_x + psf * psf), 1.0 / (wide_y + psf * psf)
        amp = amps[c]
        var_x = keep(sums[1, c] * inv_x * (inv_x * wide_x))
        var_y = keep(amp * sums[3, c] * inv_y * (inv_y * wide_y))
        shared[row(0, c)] = keep(sums[0, c] * inv_x)
        shared[row(1, c)] = keep(amp * sums[2, c] * inv_y)
        shared[row(2, c)] = var_x + var_y
        shared[row(3, c)] = var_x - var_y
        amps[c] = keep(sums[4, c])
    none = jnp.zeros((wide, 128), F32)
    for q, piece in enumerate(pieces):
        for p, entry in enumerate(piece):
            is_shared = entry is not None and entry[0] == "s"
            if is_shared:
                half[q, p] = shared[band, entry[1]]
            else:
                half[q, p] = none if entry is None else amps[entry[1]]
            if p < shared_rows:
                other[q, p] = shared[1 - band, entry[1]] if is_shared else none
    for k in range(epochs):
        outs[k][...] = half[lax.rem(epoch + k, epochs)]
        outs[epochs + k][...] = other[lax.rem(epoch + k, epochs)]


def step_gradient(layout, counts, offsets, psf, data, weight, slot_rows, moved):
    shared_rows, rows, pieces = layout
    epochs = len(pieces)
    later = moved is not None
    tiles, _, slots = offsets.shape
    pixels = data.shape[-1]
    wide = tiles * slots
    shapes = [(rows, wide, 128)] * epochs + [(shared_rows, wide, 128)] * epochs
    ins = slot_rows + (moved or [])
    together = [pltpu.VMEM((BANDS, HALF, wide, 128), F32), pltpu.VMEM((COMPS, wide, 128), F32)]
    return pl.pallas_call(
        functools.partial(step_kernel, layout, later),
        out_shape=[f32(*s) for s in shapes],
        in_specs=[smem()] * 3 + [vmem()] * (2 + len(ins)),
        out_specs=[vmem()] * len(shapes),
        scratch_shapes=together
        + [
            pltpu.VMEM((6, COMPS, wide, 128), F32),
            pltpu.VMEM((slots * COMPS, pixels, 128), F32),
            pltpu.VMEM((slots, 2 * pixels, COMPS * 128), F32),
            pltpu.VMEM((slots, 2 * pixels, COMPS * 128), F32),
            pltpu.VMEM((2 * pixels, 2 * pixels), F32),
            pltpu.VMEM((5, COMPS, wide, 128), F32),
            pltpu.VMEM((epochs, rows, wide, 128), F32),
            pltpu.VMEM((epochs, shared_rows, wide, 128), F32),
        ]
        + (together if later else []),
        compiler_params=params(40),
        name="later_step" if later else "first_step",
    )(counts, offsets, psf, data, weight, *ins)


def combine_kernel(layout, match_ref, *refs):
    shared_rows, rows, pieces = layout
    got, (out_ref, short_ref, own_ref) = refs[:-3], refs[-3:]
    wide = out_ref.shape[1]
    match = match_ref[...]
    for p in range(rows):
        both = pick(match, jnp.concatenate([ref[p] for ref in got], axis=0))
        out_ref[p] = both[:wide]
        if p < shared_rows:
            short_ref[p] = both[:wide]
        own_ref[p] = both[wide:]


def dense_kernel(rows, lists_ref, grads, *outs):
    tiles, slots = lists_ref.shape
    owners, blocks = len(outs), outs[0].shape[1]
    shape = (owners * blocks, tiles * slots)
    line = lax.broadcasted_iota(jnp.int32, shape, 0)
    lane = lax.broadcasted_iota(jnp.int32, shape, 1)
    me = lax.axis_index("tile")
    target = lax.rem(me + line // blocks, owners) * blocks + line % blocks
    ids = jnp.zeros(shape, jnp.int32)
    for t in range(tiles):
        for s in range(slots):
            ids = jnp.where(lane == t * slots + s, lists_ref[t, s], ids)
    match = (ids == target).astype(F32)
    for p in range(rows):
        dense = pick(match, grads[p])
        for k, out in enumerate(outs):
            out[p] = dense[k * blocks : (k + 1) * blocks]


def final_kernel(layout, spacing, params_ref, *refs):
    shared_rows, rows, pieces = layout
    epochs = len(pieces)
    ins, (out_ref, held) = refs[: 2 * epochs], refs[2 * epochs :]
    band, epoch = lax.axis_index("band"), lax.axis_index("epoch")
    for k in range(epochs):
        q = lax.rem(epoch - k + epochs, epochs)
        held[band, q] = ins[k][...]
        held[1 - band, q] = ins[epochs + k][...]
    shift = [0.0, 0.0]
    for b in range(BANDS):
        for q, piece in enumerate(pieces):
            for p, entry in enumerate(piece):
                if entry is None:
                    continue
                row, position = row_of(b, entry)
                grad = held[b, q, p]
                out_ref[row] = params_ref[row] - STEP * grad
                if position is not None:
                    shift[position] = shift[position] + grad
    for k in range(2):
        out_ref[k] = params_ref[k] - (STEP * POSITION_RATE * spacing) * shift[k]


def shards(source_params, pixel_data, pixel_weight, psf_width, block_lists, block_counts, block_offsets):
    owners, epochs = lax.axis_size("tile"), lax.axis_size("epoch")
    blocks, param_rows, sources = source_params.shape
    tiles, slots = block_lists.shape
    wide = tiles * slots
    spacing = pixel_data.shape[-1] / 8.0
    layout = quarter_layout(epochs)
    shared_rows, rows, pieces = layout

    def to_peers(same, other):
        kept = [same[0]]
        for k in range(1, epochs):
            kept.append(lax.ppermute(same[k], "epoch", [(i, (i + k) % epochs) for i in range(epochs)]))
        for k in range(epochs):
            pairs = [
                (i * BANDS + b, (i + k) % epochs * BANDS + 1 - b)
                for i in range(epochs)
                for b in range(BANDS)
            ]
            kept.append(lax.ppermute(other[k], ("epoch", "band"), pairs))
        return kept

    def round_tiles(arrays):
        return [arrays[0]] + [
            lax.ppermute(arrays[k], "tile", [(i, (i + k) % owners) for i in range(owners)])
            for k in range(1, owners)
        ]

    def spread(piece, other):
        return to_peers([piece] * epochs, [other] * epochs)

    def summed(parts):
        near = functools.reduce(lambda a, b: a + b, parts[:epochs])
        far = functools.reduce(lambda a, b: a + b, parts[epochs:])
        return near + jnp.pad(far, ((0, rows - shared_rows), (0, 0), (0, 0)))

    by_row = jnp.transpose(source_params, (1, 0, 2))
    offsets = jnp.transpose(block_offsets, (0, 2, 1))
    packed = pl.pallas_call(
        functools.partial(pack_kernel, layout, spacing),
        out_shape=f32(rows + 1, blocks, sources),
        in_specs=[smem(), vmem()],
        out_specs=vmem(),
        compiler_params=params(),
        name="pack",
    )(block_lists, by_row)
    got = round_tiles([packed] * owners)
    slot_piece, slot_short, match = pl.pallas_call(
        functools.partial(select_kernel, layout),
        out_shape=[
            f32(rows, wide, sources),
            f32(shared_rows, wide, sources),
            f32(wide + blocks, owners * wide),
        ],
        in_specs=[smem()] + [vmem()] * owners,
        out_specs=[vmem()] * 3,
        compiler_params=params(),
        name="select",
    )(block_lists, *got)
    slot_rows = spread(slot_piece, slot_short)

    def gradient(moved):
        parts = step_gradient(
            layout, block_counts, offsets, psf_width, pixel_data, pixel_weight, slot_rows, moved
        )
        return summed(to_peers(parts[:epochs], parts[epochs:]))

    got = round_tiles([gradient(None)] * owners)
    slot_piece, slot_short, own_first = pl.pallas_call(
        functools.partial(combine_kernel, layout),
        out_shape=[
            f32(rows, wide, sources),
            f32(shared_rows, wide, sources),
            f32(rows, blocks, sources),
        ],
        in_specs=[vmem()] * (1 + owners),
        out_specs=[vmem()] * 3,
        compiler_params=params(),
        name="combine",
    )(match, *got)

    dense = pl.pallas_call(
        functools.partial(dense_kernel, rows),
        out_shape=[f32(rows, blocks, sources)] * owners,
        in_specs=[smem(), vmem()],
        out_specs=[vmem()] * owners,
        compiler_params=params(),
        name="dense",
    )(block_lists, gradient(spread(slot_piece, slot_short)))
    own = functools.reduce(lambda a, b: a + b, round_tiles(dense), own_first)
    whole = pl.pallas_call(
        functools.partial(final_kernel, layout, spacing),
        out_shape=f32(param_rows, blocks, sources),
        in_specs=[vmem()] * (1 + 2 * epochs),
        out_specs=vmem(),
        scratch_shapes=[pltpu.VMEM((BANDS, epochs, rows, blocks, sources), F32)],
        compiler_params=params(),
        name="final",
    )(by_row, *spread(own, own))
    return jnp.transpose(whole, (1, 0, 2))


def solution(mesh):
    return jax.shard_map(
        shards,
        mesh=mesh,
        in_specs=(
            P(("region", "tile"), None, None),
            P(("region", "tile"), "epoch", "band", None, None),
            P(("region", "tile"), "epoch", "band", None, None),
            P(("region", "epoch"), "band"),
            P(("region", "tile"), None),
            P(("region", "tile")),
            P(("region", "tile"), None, None),
        ),
        out_specs=P(("region", "tile"), None, None),
        check_vma=False,
    )
```

```python
import functools
import math

import jax
import jax.numpy as jnp
from jax import lax
from jax.experimental import pallas as pl
from jax.experimental.pallas import tpu as pltpu
from jax.sharding import PartitionSpec as P

ITERS = 2
STEP = 0.005
POSITION_RATE = 1.0 / 64.0
COMPS = 7
BANDS = 2
SHARED = 4 * COMPS
HALF = SHARED // BANDS
SPLIT_UNIT = 49152.0
SPLIT_SCALE = 65536.0
LOG2E = math.log2(math.e)
F32 = jnp.float32
BF16 = jnp.bfloat16
MIB = 1024 * 1024


def quarter_layout(epochs):
    shared_rows = -(-HALF // epochs)
    rows = -(-(HALF + COMPS) // epochs)
    pieces, amp = [], 0
    for q in range(epochs):
        piece = [("s", i) for i in range(q * shared_rows, min((q + 1) * shared_rows, HALF))]
        while len(piece) < rows and amp < COMPS:
            piece.append(("a", amp))
            amp += 1
        pieces.append(piece + [None] * (rows - len(piece)))
    return shared_rows, rows, pieces


def row_of(band, entry):
    kind, i = entry
    if kind == "a":
        return 2 + 6 * i + 4 + band, None
    k, c = divmod(HALF * band + i, COMPS)
    return 2 + 6 * c + k, (k if k < 2 else None)


def split3(x):
    hi = x.astype(BF16)
    rest = x - hi.astype(F32)
    mid = rest.astype(BF16)
    low = (rest - mid.astype(F32)).astype(BF16)
    return jnp.concatenate([hi, mid, low], axis=0)


def pick(matrix, rows):
    wide = jnp.concatenate([matrix, matrix, matrix], axis=1).astype(BF16)
    return jnp.dot(wide, split3(rows), preferred_element_type=F32)


def vmem():
    return pl.BlockSpec(memory_space=pltpu.VMEM)


def smem():
    return pl.BlockSpec(memory_space=pltpu.SMEM)


def f32(*shape):
    return jax.ShapeDtypeStruct(shape, F32)


def params(mib=4):
    return pltpu.CompilerParams(vmem_limit_bytes=mib * MIB)


def pack_kernel(layout, spacing, lists_ref, params_ref, out_ref):
    shared_rows, rows, pieces = layout
    band, epoch = lax.axis_index("band"), lax.axis_index("epoch")
    for b in range(BANDS):
        for q in range(len(pieces)):

            @pl.when((band == b) & (epoch == q))
            def _():
                for p, entry in enumerate(pieces[q]):
                    if entry is None:
                        out_ref[p] = jnp.zeros(out_ref.shape[1:], F32)
                        continue
                    row, position = row_of(b, entry)
                    value = params_ref[row]
                    if position is not None:
                        value = spacing * params_ref[position] + value
                    out_ref[p] = value

    tiles, slots = lists_ref.shape
    lane = lax.broadcasted_iota(jnp.int32, (8, 128), 1)
    ids = jnp.zeros((8, 128), jnp.int32)
    for t in range(tiles):
        for s in range(slots):
            ids = jnp.where(lane == t * slots + s, lists_ref[t, s], ids)
    out_ref[rows] = ids.astype(F32)


def select_kernel(layout, lists_ref, *refs):
    shared_rows, rows, pieces = layout
    got, (out_ref, short_ref, match_ref) = refs[:-3], refs[-3:]
    owners = len(got)
    tiles, slots = lists_ref.shape
    blocks = got[0].shape[1]
    wide = tiles * slots
    me = lax.axis_index("tile")

    def slot_ids(shape):
        line = lax.broadcasted_iota(jnp.int32, shape, 0)
        ids = jnp.zeros(shape, jnp.int32)
        for t in range(tiles):
            for s in range(slots):
                ids = jnp.where(line == t * slots + s, lists_ref[t, s], ids)
        return ids

    shape = (wide, owners * blocks)
    lane = lax.broadcasted_iota(jnp.int32, shape, 1)
    held = lax.rem(me - lane // blocks + owners, owners) * blocks + lane % blocks
    choose = (slot_ids(shape) == held).astype(F32)
    for p in range(rows):
        chosen = pick(choose, jnp.concatenate([ref[p] for ref in got], axis=0))
        out_ref[p] = chosen
        if p < shared_rows:
            short_ref[p] = chosen

    shape = (wide + blocks, owners * wide)
    line = lax.broadcasted_iota(jnp.int32, shape, 0)
    own = jnp.where(line < wide, slot_ids(shape), me * blocks + line - wide).astype(F32)
    sent = jnp.concatenate([ref[rows, :1, :wide] for ref in got], axis=1)
    match_ref[...] = (own == sent).astype(F32)


def put_together(layout, band, epoch, ins, half, other, shared, amps):
    shared_rows, rows, pieces = layout
    epochs = len(pieces)
    for k in range(epochs):
        q = lax.rem(epoch - k + epochs, epochs)
        half[q] = ins[k][...]
        other[q] = ins[epochs + k][...]
    for q, piece in enumerate(pieces):
        for p, entry in enumerate(piece):
            if entry is None:
                continue
            kind, i = entry
            if kind == "s":
                shared[band, i] = half[q, p]
                shared[1 - band, i] = other[q, p]
            else:
                amps[i] = half[q, p]


def step_kernel(layout, later, counts_ref, offsets_ref, psf_ref, data_ref, weight_ref, *refs):
    shared_rows, rows, pieces = layout
    epochs = len(pieces)
    taken = 2 * epochs * (2 if later else 1)
    ins, refs = refs[:taken], refs[taken:]
    outs, refs = refs[: 2 * epochs], refs[2 * epochs :]
    shared, amps, derived, image, sums, half, other = refs[:7]
    prof_y, pieces_x, pieces_y, by_x, by_y = (refs[7 + 2 * n : 9 + 2 * n] for n in range(5))
    band, epoch = lax.axis_index("band"), lax.axis_index("epoch")
    tiles = data_ref.shape[0]
    pixels = data_ref.shape[-1]
    wide = shared.shape[2]
    slots = wide // tiles
    spacing = pixels / 8.0

    put_together(layout, band, epoch, ins[: 2 * epochs], half, other, shared, amps)

    def row(k, c):
        r = k * COMPS + c
        return r // HALF, r % HALF

    if later:
        moved, moved_amps = refs[17:]
        put_together(layout, band, epoch, ins[2 * epochs :], half, other, moved, moved_amps)
        for k in range(4):
            shift = 0.0
            if k < 2:
                shift = functools.reduce(lambda a, b: a + b, [moved[row(k, c)] for c in range(COMPS)])
                shift = shift * (spacing * spacing * POSITION_RATE)
            for c in range(COMPS):
                shared[row(k, c)] = shared[row(k, c)] - STEP * (moved[row(k, c)] + shift)
        for c in range(COMPS):
            amps[c] = amps[c] - STEP * moved_amps[c]

    psf = psf_ref[0, 0]
    line_of = lax.broadcasted_iota(jnp.int32, (wide, 128), 0)
    live = jnp.zeros((wide, 128), jnp.bool_)
    for t in range(tiles):
        live = live | ((line_of >= t * slots) & (line_of < t * slots + counts_ref[t]))
    for c in range(COMPS):
        lw, an = shared[row(2, c)], shared[row(3, c)]
        derived[0, c] = shared[row(0, c)]
        derived[1, c] = shared[row(1, c)]
        derived[2, c] = (-0.5 * LOG2E) / (jnp.exp(2.0 * (lw + an)) + psf * psf)
        derived[3, c] = (-0.5 * LOG2E) / (jnp.exp(2.0 * (lw - an)) + psf * psf)
        derived[4, c] = jnp.where(live, amps[c], 0.0)
        derived[5, c] = derived[4, c] * SPLIT_SCALE
    sums[...] = jnp.zeros_like(sums)

    grid = lax.broadcasted_iota(jnp.int32, (pixels, 128), 0).astype(F32)

    def cut(x, large):
        hi = (x + large) - large
        return jnp.concatenate([hi, x - hi], axis=0)

    def stack(x):
        hi = x.astype(BF16).astype(F32)
        return jnp.concatenate([hi, hi], axis=1), x - hi

    def times(left, right):
        near = jnp.dot(left[0], right, preferred_element_type=F32)
        return near + jnp.dot(left[1], right[:pixels], preferred_element_type=F32)

    def total(x):
        return jnp.sum(x, axis=0, keepdims=True)

    def line(index, c, g):
        return derived[index, c, pl.ds(g, 1), :]

    def place(t, s):
        s = jnp.minimum(s, slots - 1)
        return t * slots + s, offsets_ref[t, 0, s].astype(F32), offsets_ref[t, 1, s].astype(F32)

    spans = [(first, min(2, COMPS - first)) for first in range(0, COMPS, 2)]

    for t in range(tiles):
        trips = (counts_ref[t] + 1) // 2

        def profiles(i, u):
            at = i + u // 2
            g, off_x, off_y = place(t, 2 * i + u)
            for c in range(COMPS):
                d = grid - (line(0, c, g) + off_x)
                e = jnp.exp2(d * d * line(2, c, g))
                pieces_x[u % 2][at, :, c * 128 : (c + 1) * 128] = cut(e, SPLIT_UNIT)
                d = grid - (line(1, c, g) + off_y)
                e = jnp.exp2(d * d * line(3, c, g))
                prof_y[u % 2][at, :, c * 128 : (c + 1) * 128] = e
                pieces_y[u % 2][at, :, c * 128 : (c + 1) * 128] = cut(e * line(4, c, g), line(5, c, g))

        def add_image(i, u):
            image[...] += lax.dot_general(
                pieces_x[u][i], pieces_y[u][i], (((1,), (1,)), ((), ())), preferred_element_type=F32
            )

        image[...] = jnp.zeros_like(image)
        profiles(0, 0)

        def render(i, carry):
            for u in range(2):
                add_image(i, u)
                profiles(i, u + 1)
            return carry

        lax.fori_loop(0, trips, render, 0)

        model = (image[:pixels, :pixels] + image[pixels:, pixels:]) + (
            image[:pixels, pixels:] + image[pixels:, :pixels]
        )
        cotangent = weight_ref[t, 0, 0] * (model - data_ref[t, 0, 0])
        left_x, left_y = stack(cotangent), stack(cotangent.T)

        def products(i, u, first, here):
            at = i + u // 2
            span = slice(first * 128, (first + here) * 128)
            by_x[u % 2][:, span] = times(left_x, pieces_y[u % 2][at, :, span])
            by_y[u % 2][:, span] = times(left_y, pieces_x[u % 2][at, :, span])

        def reduce(i, u, first, here):
            g, off_x, off_y = place(t, 2 * i + u)
            for c in range(first, first + here):
                at = slice(c * 128, (c + 1) * 128)
                d = grid - (line(0, c, g) + off_x)
                e = pieces_x[u][i, :pixels, at] + pieces_x[u][i, pixels:, at]
                e = e * by_x[u][:, at]
                e1 = e * d
                sums[0, c, pl.ds(g, 1), :] = total(e1)
                sums[1, c, pl.ds(g, 1), :] = total(e1 * d)
                d = grid - (line(1, c, g) + off_y)
                e = prof_y[u][i, :, at] * by_y[u][:, at]
                e1 = e * d
                sums[2, c, pl.ds(g, 1), :] = total(e1)
                sums[3, c, pl.ds(g, 1), :] = total(e1 * d)
                sums[4, c, pl.ds(g, 1), :] = total(e)

        for span in spans:
            products(0, 0, *span)

        def pull(i, carry):
            for u in range(2):
                for span in spans:
                    products(i, u + 1, *span)
                    reduce(i, u, *span)
            return carry

        lax.fori_loop(0, trips, pull, 0)

    def keep(x):
        return jnp.where(live, x, 0.0)

    for c in range(COMPS):
        lw, an = shared[row(2, c)], shared[row(3, c)]
        wide_x, wide_y = jnp.exp(2.0 * (lw + an)), jnp.exp(2.0 * (lw - an))
        inv_x, inv_y = 1.0 / (wide_x + psf * psf), 1.0 / (wide_y + psf * psf)
        amp = amps[c]
        var_x = keep(sums[1, c] * inv_x * (inv_x * wide_x))
        var_y = keep(amp * sums[3, c] * inv_y * (inv_y * wide_y))
        shared[row(0, c)] = keep(sums[0, c] * inv_x)
        shared[row(1, c)] = keep(amp * sums[2, c] * inv_y)
        shared[row(2, c)] = var_x + var_y
        shared[row(3, c)] = var_x - var_y
        amps[c] = keep(sums[4, c])
    none = jnp.zeros((wide, 128), F32)
    for q, piece in enumerate(pieces):
        for p, entry in enumerate(piece):
            is_shared = entry is not None and entry[0] == "s"
            if is_shared:
                half[q, p] = shared[band, entry[1]]
            else:
                half[q, p] = none if entry is None else amps[entry[1]]
            if p < shared_rows:
                other[q, p] = shared[1 - band, entry[1]] if is_shared else none
    for k in range(epochs):
        outs[k][...] = half[lax.rem(epoch + k, epochs)]
        outs[epochs + k][...] = other[lax.rem(epoch + k, epochs)]


def step_gradient(layout, counts, offsets, psf, data, weight, slot_rows, moved):
    shared_rows, rows, pieces = layout
    epochs = len(pieces)
    later = moved is not None
    tiles, _, slots = offsets.shape
    pixels = data.shape[-1]
    wide = tiles * slots
    shapes = [(rows, wide, 128)] * epochs + [(shared_rows, wide, 128)] * epochs
    ins = slot_rows + (moved or [])
    together = [pltpu.VMEM((BANDS, HALF, wide, 128), F32), pltpu.VMEM((COMPS, wide, 128), F32)]
    return pl.pallas_call(
        functools.partial(step_kernel, layout, later),
        out_shape=[f32(*s) for s in shapes],
        in_specs=[smem()] * 3 + [vmem()] * (2 + len(ins)),
        out_specs=[vmem()] * len(shapes),
        scratch_shapes=together
        + [
            pltpu.VMEM((6, COMPS, wide, 128), F32),
            pltpu.VMEM((2 * pixels, 2 * pixels), F32),
            pltpu.VMEM((5, COMPS, wide, 128), F32),
            pltpu.VMEM((epochs, rows, wide, 128), F32),
            pltpu.VMEM((epochs, shared_rows, wide, 128), F32),
        ]
        + [pltpu.VMEM((slots // 2 + 1 - u, pixels, COMPS * 128), F32) for u in range(2)]
        + [pltpu.VMEM((slots // 2 + 1 - u, 2 * pixels, COMPS * 128), F32) for u in (0, 1, 0, 1)]
        + [pltpu.VMEM((pixels, COMPS * 128), F32)] * 4
        + (together if later else []),
        compiler_params=params(40),
        name="later_step" if later else "first_step",
    )(counts, offsets, psf, data, weight, *ins)


def combine_kernel(layout, match_ref, *refs):
    shared_rows, rows, pieces = layout
    got, (out_ref, short_ref, own_ref) = refs[:-3], refs[-3:]
    wide = out_ref.shape[1]
    match = match_ref[...]
    for p in range(rows):
        both = pick(match, jnp.concatenate([ref[p] for ref in got], axis=0))
        out_ref[p] = both[:wide]
        if p < shared_rows:
            short_ref[p] = both[:wide]
        own_ref[p] = both[wide:]


def dense_kernel(rows, lists_ref, grads, *outs):
    tiles, slots = lists_ref.shape
    owners, blocks = len(outs), outs[0].shape[1]
    shape = (owners * blocks, tiles * slots)
    line = lax.broadcasted_iota(jnp.int32, shape, 0)
    lane = lax.broadcasted_iota(jnp.int32, shape, 1)
    me = lax.axis_index("tile")
    target = lax.rem(me + line // blocks, owners) * blocks + line % blocks
    ids = jnp.zeros(shape, jnp.int32)
    for t in range(tiles):
        for s in range(slots):
            ids = jnp.where(lane == t * slots + s, lists_ref[t, s], ids)
    match = (ids == target).astype(F32)
    for p in range(rows):
        dense = pick(match, grads[p])
        for k, out in enumerate(outs):
            out[p] = dense[k * blocks : (k + 1) * blocks]


def final_kernel(layout, spacing, params_ref, *refs):
    shared_rows, rows, pieces = layout
    epochs = len(pieces)
    ins, (out_ref, held) = refs[: 2 * epochs], refs[2 * epochs :]
    band, epoch = lax.axis_index("band"), lax.axis_index("epoch")
    for k in range(epochs):
        q = lax.rem(epoch - k + epochs, epochs)
        held[band, q] = ins[k][...]
        held[1 - band, q] = ins[epochs + k][...]
    shift = [0.0, 0.0]
    for b in range(BANDS):
        for q, piece in enumerate(pieces):
            for p, entry in enumerate(piece):
                if entry is None:
                    continue
                row, position = row_of(b, entry)
                grad = held[b, q, p]
                out_ref[row] = params_ref[row] - STEP * grad
                if position is not None:
                    shift[position] = shift[position] + grad
    for k in range(2):
        out_ref[k] = params_ref[k] - (STEP * POSITION_RATE * spacing) * shift[k]


def shards(source_params, pixel_data, pixel_weight, psf_width, block_lists, block_counts, block_offsets):
    owners, epochs = lax.axis_size("tile"), lax.axis_size("epoch")
    blocks, param_rows, sources = source_params.shape
    tiles, slots = block_lists.shape
    wide = tiles * slots
    spacing = pixel_data.shape[-1] / 8.0
    layout = quarter_layout(epochs)
    shared_rows, rows, pieces = layout

    def to_peers(same, other):
        kept = [same[0]]
        for k in range(1, epochs):
            kept.append(lax.ppermute(same[k], "epoch", [(i, (i + k) % epochs) for i in range(epochs)]))
        for k in range(epochs):
            pairs = [
                (i * BANDS + b, (i + k) % epochs * BANDS + 1 - b)
                for i in range(epochs)
                for b in range(BANDS)
            ]
            kept.append(lax.ppermute(other[k], ("epoch", "band"), pairs))
        return kept

    def round_tiles(arrays):
        return [arrays[0]] + [
            lax.ppermute(arrays[k], "tile", [(i, (i + k) % owners) for i in range(owners)])
            for k in range(1, owners)
        ]

    def spread(piece, other):
        return to_peers([piece] * epochs, [other] * epochs)

    def summed(parts):
        near = functools.reduce(lambda a, b: a + b, parts[:epochs])
        far = functools.reduce(lambda a, b: a + b, parts[epochs:])
        return near + jnp.pad(far, ((0, rows - shared_rows), (0, 0), (0, 0)))

    by_row = jnp.transpose(source_params, (1, 0, 2))
    offsets = jnp.transpose(block_offsets, (0, 2, 1))
    packed = pl.pallas_call(
        functools.partial(pack_kernel, layout, spacing),
        out_shape=f32(rows + 1, blocks, sources),
        in_specs=[smem(), vmem()],
        out_specs=vmem(),
        compiler_params=params(),
        name="pack",
    )(block_lists, by_row)
    got = round_tiles([packed] * owners)
    slot_piece, slot_short, match = pl.pallas_call(
        functools.partial(select_kernel, layout),
        out_shape=[
            f32(rows, wide, sources),
            f32(shared_rows, wide, sources),
            f32(wide + blocks, owners * wide),
        ],
        in_specs=[smem()] + [vmem()] * owners,
        out_specs=[vmem()] * 3,
        compiler_params=params(),
        name="select",
    )(block_lists, *got)
    slot_rows = spread(slot_piece, slot_short)

    def gradient(moved):
        parts = step_gradient(
            layout, block_counts, offsets, psf_width, pixel_data, pixel_weight, slot_rows, moved
        )
        return summed(to_peers(parts[:epochs], parts[epochs:]))

    got = round_tiles([gradient(None)] * owners)
    slot_piece, slot_short, own_first = pl.pallas_call(
        functools.partial(combine_kernel, layout),
        out_shape=[
            f32(rows, wide, sources),
            f32(shared_rows, wide, sources),
            f32(rows, blocks, sources),
        ],
        in_specs=[vmem()] * (1 + owners),
        out_specs=[vmem()] * 3,
        compiler_params=params(),
        name="combine",
    )(match, *got)

    dense = pl.pallas_call(
        functools.partial(dense_kernel, rows),
        out_shape=[f32(rows, blocks, sources)] * owners,
        in_specs=[smem(), vmem()],
        out_specs=[vmem()] * owners,
        compiler_params=params(),
        name="dense",
    )(block_lists, gradient(spread(slot_piece, slot_short)))
    own = functools.reduce(lambda a, b: a + b, round_tiles(dense), own_first)
    whole = pl.pallas_call(
        functools.partial(final_kernel, layout, spacing),
        out_shape=f32(param_rows, blocks, sources),
        in_specs=[vmem()] * (1 + 2 * epochs),
        out_specs=vmem(),
        scratch_shapes=[pltpu.VMEM((BANDS, epochs, rows, blocks, sources), F32)],
        compiler_params=params(),
        name="final",
    )(by_row, *spread(own, own))
    return jnp.transpose(whole, (1, 0, 2))


def solution(mesh):
    return jax.shard_map(
        shards,
        mesh=mesh,
        in_specs=(
            P(("region", "tile"), None, None),
            P(("region", "tile"), "epoch", "band", None, None),
            P(("region", "tile"), "epoch", "band", None, None),
            P(("region", "epoch"), "band"),
            P(("region", "tile"), None),
            P(("region", "tile")),
            P(("region", "tile"), None, None),
        ),
        out_specs=P(("region", "tile"), None, None),
        check_vma=False,
    )
```

```python
import functools
import math

import jax
import jax.numpy as jnp
from jax import lax
from jax.experimental import pallas as pl
from jax.experimental.pallas import tpu as pltpu
from jax.sharding import PartitionSpec as P

ITERS = 2
STEP = 0.005
POSITION_RATE = 1.0 / 64.0
COMPS = 7
BANDS = 2
SHARED = 4 * COMPS
HALF = SHARED // BANDS
SPLIT_UNIT = 49152.0
SPLIT_SCALE = 65536.0
LOG2E = math.log2(math.e)
F32 = jnp.float32
BF16 = jnp.bfloat16
MIB = 1024 * 1024


def quarter_layout(epochs):
    shared_rows = -(-HALF // epochs)
    rows = -(-(HALF + COMPS) // epochs)
    pieces, amp = [], 0
    for q in range(epochs):
        piece = [("s", i) for i in range(q * shared_rows, min((q + 1) * shared_rows, HALF))]
        while len(piece) < rows and amp < COMPS:
            piece.append(("a", amp))
            amp += 1
        pieces.append(piece + [None] * (rows - len(piece)))
    return shared_rows, rows, pieces


def row_of(band, entry):
    kind, i = entry
    if kind == "a":
        return 2 + 6 * i + 4 + band, None
    k, c = divmod(HALF * band + i, COMPS)
    return 2 + 6 * c + k, (k if k < 2 else None)


def split3(x):
    hi = x.astype(BF16)
    rest = x - hi.astype(F32)
    mid = rest.astype(BF16)
    low = (rest - mid.astype(F32)).astype(BF16)
    return jnp.concatenate([hi, mid, low], axis=0)


def pick(matrix, rows):
    wide = jnp.concatenate([matrix, matrix, matrix], axis=1).astype(BF16)
    return jnp.dot(wide, split3(rows), preferred_element_type=F32)


def vmem():
    return pl.BlockSpec(memory_space=pltpu.VMEM)


def smem():
    return pl.BlockSpec(memory_space=pltpu.SMEM)


def f32(*shape):
    return jax.ShapeDtypeStruct(shape, F32)


def params(mib=4):
    return pltpu.CompilerParams(vmem_limit_bytes=mib * MIB)


def pack_kernel(layout, spacing, lists_ref, params_ref, out_ref):
    shared_rows, rows, pieces = layout
    band, epoch = lax.axis_index("band"), lax.axis_index("epoch")
    for b in range(BANDS):
        for q in range(len(pieces)):

            @pl.when((band == b) & (epoch == q))
            def _():
                for p, entry in enumerate(pieces[q]):
                    if entry is None:
                        out_ref[p] = jnp.zeros(out_ref.shape[1:], F32)
                        continue
                    row, position = row_of(b, entry)
                    value = params_ref[row]
                    if position is not None:
                        value = spacing * params_ref[position] + value
                    out_ref[p] = value

    tiles, slots = lists_ref.shape
    lane = lax.broadcasted_iota(jnp.int32, (8, 128), 1)
    ids = jnp.zeros((8, 128), jnp.int32)
    for t in range(tiles):
        for s in range(slots):
            ids = jnp.where(lane == t * slots + s, lists_ref[t, s], ids)
    out_ref[rows] = ids.astype(F32)


def select_kernel(layout, lists_ref, *refs):
    shared_rows, rows, pieces = layout
    got, (out_ref, short_ref, match_ref) = refs[:-3], refs[-3:]
    owners = len(got)
    tiles, slots = lists_ref.shape
    blocks = got[0].shape[1]
    wide = tiles * slots
    me = lax.axis_index("tile")

    def slot_ids(shape):
        line = lax.broadcasted_iota(jnp.int32, shape, 0)
        ids = jnp.zeros(shape, jnp.int32)
        for t in range(tiles):
            for s in range(slots):
                ids = jnp.where(line == t * slots + s, lists_ref[t, s], ids)
        return ids

    shape = (wide, owners * blocks)
    lane = lax.broadcasted_iota(jnp.int32, shape, 1)
    held = lax.rem(me - lane // blocks + owners, owners) * blocks + lane % blocks
    choose = (slot_ids(shape) == held).astype(F32)
    for p in range(rows):
        chosen = pick(choose, jnp.concatenate([ref[p] for ref in got], axis=0))
        out_ref[p] = chosen
        if p < shared_rows:
            short_ref[p] = chosen

    shape = (wide + blocks, owners * wide)
    line = lax.broadcasted_iota(jnp.int32, shape, 0)
    own = jnp.where(line < wide, slot_ids(shape), me * blocks + line - wide).astype(F32)
    sent = jnp.concatenate([ref[rows, :1, :wide] for ref in got], axis=1)
    match_ref[...] = (own == sent).astype(F32)


def put_together(layout, band, epoch, ins, half, other, shared, amps):
    shared_rows, rows, pieces = layout
    epochs = len(pieces)
    for k in range(epochs):
        q = lax.rem(epoch - k + epochs, epochs)
        half[q] = ins[k][...]
        other[q] = ins[epochs + k][...]
    for q, piece in enumerate(pieces):
        for p, entry in enumerate(piece):
            if entry is None:
                continue
            kind, i = entry
            if kind == "s":
                shared[band, i] = half[q, p]
                shared[1 - band, i] = other[q, p]
            else:
                amps[i] = half[q, p]


def step_kernel(layout, later, counts_ref, offsets_ref, psf_ref, data_ref, weight_ref, *refs):
    shared_rows, rows, pieces = layout
    epochs = len(pieces)
    taken = 2 * epochs * (2 if later else 1)
    ins, refs = refs[:taken], refs[taken:]
    outs, refs = refs[: 2 * epochs], refs[2 * epochs :]
    shared, amps, derived, prof_y, pieces_x, pieces_y, image, sums, half, other = refs[:10]
    right = refs[10:12]
    band, epoch = lax.axis_index("band"), lax.axis_index("epoch")
    tiles = data_ref.shape[0]
    pixels = data_ref.shape[-1]
    wide = shared.shape[2]
    slots = wide // tiles
    spacing = pixels / 8.0

    put_together(layout, band, epoch, ins[: 2 * epochs], half, other, shared, amps)

    def row(k, c):
        r = k * COMPS + c
        return r // HALF, r % HALF

    if later:
        moved, moved_amps = refs[12:]
        put_together(layout, band, epoch, ins[2 * epochs :], half, other, moved, moved_amps)
        for k in range(4):
            shift = 0.0
            if k < 2:
                shift = functools.reduce(lambda a, b: a + b, [moved[row(k, c)] for c in range(COMPS)])
                shift = shift * (spacing * spacing * POSITION_RATE)
            for c in range(COMPS):
                shared[row(k, c)] = shared[row(k, c)] - STEP * (moved[row(k, c)] + shift)
        for c in range(COMPS):
            amps[c] = amps[c] - STEP * moved_amps[c]

    psf = psf_ref[0, 0]
    line_of = lax.broadcasted_iota(jnp.int32, (wide, 128), 0)
    live = jnp.zeros((wide, 128), jnp.bool_)
    for t in range(tiles):
        live = live | ((line_of >= t * slots) & (line_of < t * slots + counts_ref[t]))
    for c in range(COMPS):
        lw, an = shared[row(2, c)], shared[row(3, c)]
        derived[0, c] = shared[row(0, c)]
        derived[1, c] = shared[row(1, c)]
        derived[2, c] = (-0.5 * LOG2E) / (jnp.exp(2.0 * (lw + an)) + psf * psf)
        derived[3, c] = (-0.5 * LOG2E) / (jnp.exp(2.0 * (lw - an)) + psf * psf)
        derived[4, c] = jnp.where(live, amps[c], 0.0)
        derived[5, c] = derived[4, c] * SPLIT_SCALE
    sums[...] = jnp.zeros_like(sums)

    grid = lax.broadcasted_iota(jnp.int32, (pixels, 128), 0).astype(F32)

    def cut(x, large):
        hi = (x + large) - large
        return jnp.concatenate([hi, x - hi], axis=0)

    def stack(x):
        hi = x.astype(BF16).astype(F32)
        return jnp.concatenate([hi, hi], axis=1), x - hi

    def times(left, right):
        near = jnp.dot(left[0], right, preferred_element_type=F32)
        return near + jnp.dot(left[1], right[:pixels], preferred_element_type=F32)

    def total(x):
        return jnp.sum(x, axis=0, keepdims=True)

    def line(index, c, s):
        return derived[index, c, pl.ds(s, 1), :]

    together = 2
    for t in range(tiles):
        trips = (counts_ref[t] + together - 1) // together
        image[...] = jnp.zeros_like(image)

        def render(i, carry):
            for u in range(together):
                s = i * together + u
                g = t * slots + s
                off_x = offsets_ref[t, 0, s].astype(F32)
                off_y = offsets_ref[t, 1, s].astype(F32)
                for c in range(COMPS):
                    d = grid - (line(0, c, g) + off_x)
                    e = jnp.exp2(d * d * line(2, c, g))
                    pieces_x[s, :, c * 128 : (c + 1) * 128] = cut(e, SPLIT_UNIT)
                    d = grid - (line(1, c, g) + off_y)
                    e = jnp.exp2(d * d * line(3, c, g))
                    prof_y[s * COMPS + c] = e
                    e = e * line(4, c, g)
                    pieces_y[s, :, c * 128 : (c + 1) * 128] = cut(e, line(5, c, g))
                    turned = e.T
                    hi = turned.astype(BF16).astype(F32)
                    right[u][c * 128 : (c + 1) * 128] = jnp.concatenate([hi, turned - hi], axis=1)
                image[...] += jnp.dot(pieces_x[s], right[u][...], preferred_element_type=F32)
            return carry

        lax.fori_loop(0, trips, render, 0)

        model = (image[:pixels, :pixels] + image[pixels:, pixels:]) + (
            image[:pixels, pixels:] + image[pixels:, :pixels]
        )
        cotangent = weight_ref[t, 0, 0] * (model - data_ref[t, 0, 0])
        left_x, left_y = stack(cotangent), stack(cotangent.T)

        def pull(i, carry):
            for u in range(together):
                s = i * together + u
                g = t * slots + s
                off_x = offsets_ref[t, 0, s].astype(F32)
                off_y = offsets_ref[t, 1, s].astype(F32)
                for first in range(0, COMPS, 2):
                    here = min(2, COMPS - first)
                    span = pl.ds(first * 128, 128 * here)
                    by_x = times(left_x, pieces_y[s, :, span])
                    by_y = times(left_y, pieces_x[s, :, span])
                    for n in range(here):
                        c = first + n
                        d = grid - (line(0, c, g) + off_x)
                        at = slice(c * 128, (c + 1) * 128)
                        e = pieces_x[s, :pixels, at] + pieces_x[s, pixels:, at]
                        e = e * by_x[:, n * 128 : (n + 1) * 128]
                        e1 = e * d
                        sums[0, c, pl.ds(g, 1), :] = total(e1)
                        sums[1, c, pl.ds(g, 1), :] = total(e1 * d)
                        d = grid - (line(1, c, g) + off_y)
                        e = prof_y[s * COMPS + c] * by_y[:, n * 128 : (n + 1) * 128]
                        e1 = e * d
                        sums[2, c, pl.ds(g, 1), :] = total(e1)
                        sums[3, c, pl.ds(g, 1), :] = total(e1 * d)
                        sums[4, c, pl.ds(g, 1), :] = total(e)
            return carry

        lax.fori_loop(0, trips, pull, 0)

    def keep(x):
        return jnp.where(live, x, 0.0)

    for c in range(COMPS):
        lw, an = shared[row(2, c)], shared[row(3, c)]
        wide_x, wide_y = jnp.exp(2.0 * (lw + an)), jnp.exp(2.0 * (lw - an))
        inv_x, inv_y = 1.0 / (wide_x + psf * psf), 1.0 / (wide_y + psf * psf)
        amp = amps[c]
        var_x = keep(sums[1, c] * inv_x * (inv_x * wide_x))
        var_y = keep(amp * sums[3, c] * inv_y * (inv_y * wide_y))
        shared[row(0, c)] = keep(sums[0, c] * inv_x)
        shared[row(1, c)] = keep(amp * sums[2, c] * inv_y)
        shared[row(2, c)] = var_x + var_y
        shared[row(3, c)] = var_x - var_y
        amps[c] = keep(sums[4, c])
    none = jnp.zeros((wide, 128), F32)
    for q, piece in enumerate(pieces):
        for p, entry in enumerate(piece):
            is_shared = entry is not None and entry[0] == "s"
            if is_shared:
                half[q, p] = shared[band, entry[1]]
            else:
                half[q, p] = none if entry is None else amps[entry[1]]
            if p < shared_rows:
                other[q, p] = shared[1 - band, entry[1]] if is_shared else none
    for k in range(epochs):
        outs[k][...] = half[lax.rem(epoch + k, epochs)]
        outs[epochs + k][...] = other[lax.rem(epoch + k, epochs)]


def step_gradient(layout, counts, offsets, psf, data, weight, slot_rows, moved):
    shared_rows, rows, pieces = layout
    epochs = len(pieces)
    later = moved is not None
    tiles, _, slots = offsets.shape
    pixels = data.shape[-1]
    wide = tiles * slots
    shapes = [(rows, wide, 128)] * epochs + [(shared_rows, wide, 128)] * epochs
    ins = slot_rows + (moved or [])
    together = [pltpu.VMEM((BANDS, HALF, wide, 128), F32), pltpu.VMEM((COMPS, wide, 128), F32)]
    return pl.pallas_call(
        functools.partial(step_kernel, layout, later),
        out_shape=[f32(*s) for s in shapes],
        in_specs=[smem()] * 3 + [vmem()] * (2 + len(ins)),
        out_specs=[vmem()] * len(shapes),
        scratch_shapes=together
        + [
            pltpu.VMEM((6, COMPS, wide, 128), F32),
            pltpu.VMEM((slots * COMPS, pixels, 128), F32),
            pltpu.VMEM((slots, 2 * pixels, COMPS * 128), F32),
            pltpu.VMEM((slots, 2 * pixels, COMPS * 128), F32),
            pltpu.VMEM((2 * pixels, 2 * pixels), F32),
            pltpu.VMEM((5, COMPS, wide, 128), F32),
            pltpu.VMEM((epochs, rows, wide, 128), F32),
            pltpu.VMEM((epochs, shared_rows, wide, 128), F32),
        ]
        + [pltpu.VMEM((COMPS * 128, 2 * pixels), F32)] * 2
        + (together if later else []),
        compiler_params=params(40),
        name="later_step" if later else "first_step",
    )(counts, offsets, psf, data, weight, *ins)


def combine_kernel(layout, match_ref, *refs):
    shared_rows, rows, pieces = layout
    got, (out_ref, short_ref, own_ref) = refs[:-3], refs[-3:]
    wide = out_ref.shape[1]
    match = match_ref[...]
    for p in range(rows):
        both = pick(match, jnp.concatenate([ref[p] for ref in got], axis=0))
        out_ref[p] = both[:wide]
        if p < shared_rows:
            short_ref[p] = both[:wide]
        own_ref[p] = both[wide:]


def dense_kernel(rows, lists_ref, grads, *outs):
    tiles, slots = lists_ref.shape
    owners, blocks = len(outs), outs[0].shape[1]
    shape = (owners * blocks, tiles * slots)
    line = lax.broadcasted_iota(jnp.int32, shape, 0)
    lane = lax.broadcasted_iota(jnp.int32, shape, 1)
    me = lax.axis_index("tile")
    target = lax.rem(me + line // blocks, owners) * blocks + line % blocks
    ids = jnp.zeros(shape, jnp.int32)
    for t in range(tiles):
        for s in range(slots):
            ids = jnp.where(lane == t * slots + s, lists_ref[t, s], ids)
    match = (ids == target).astype(F32)
    for p in range(rows):
        dense = pick(match, grads[p])
        for k, out in enumerate(outs):
            out[p] = dense[k * blocks : (k + 1) * blocks]


def final_kernel(layout, spacing, params_ref, *refs):
    shared_rows, rows, pieces = layout
    epochs = len(pieces)
    ins, (out_ref, held) = refs[: 2 * epochs], refs[2 * epochs :]
    band, epoch = lax.axis_index("band"), lax.axis_index("epoch")
    for k in range(epochs):
        q = lax.rem(epoch - k + epochs, epochs)
        held[band, q] = ins[k][...]
        held[1 - band, q] = ins[epochs + k][...]
    shift = [0.0, 0.0]
    for b in range(BANDS):
        for q, piece in enumerate(pieces):
            for p, entry in enumerate(piece):
                if entry is None:
                    continue
                row, position = row_of(b, entry)
                grad = held[b, q, p]
                out_ref[row] = params_ref[row] - STEP * grad
                if position is not None:
                    shift[position] = shift[position] + grad
    for k in range(2):
        out_ref[k] = params_ref[k] - (STEP * POSITION_RATE * spacing) * shift[k]


def shards(source_params, pixel_data, pixel_weight, psf_width, block_lists, block_counts, block_offsets):
    owners, epochs = lax.axis_size("tile"), lax.axis_size("epoch")
    blocks, param_rows, sources = source_params.shape
    tiles, slots = block_lists.shape
    wide = tiles * slots
    spacing = pixel_data.shape[-1] / 8.0
    layout = quarter_layout(epochs)
    shared_rows, rows, pieces = layout

    def to_peers(same, other):
        kept = [same[0]]
        for k in range(1, epochs):
            kept.append(lax.ppermute(same[k], "epoch", [(i, (i + k) % epochs) for i in range(epochs)]))
        for k in range(epochs):
            pairs = [
                (i * BANDS + b, (i + k) % epochs * BANDS + 1 - b)
                for i in range(epochs)
                for b in range(BANDS)
            ]
            kept.append(lax.ppermute(other[k], ("epoch", "band"), pairs))
        return kept

    def round_tiles(arrays):
        return [arrays[0]] + [
            lax.ppermute(arrays[k], "tile", [(i, (i + k) % owners) for i in range(owners)])
            for k in range(1, owners)
        ]

    def spread(piece, other):
        return to_peers([piece] * epochs, [other] * epochs)

    def summed(parts):
        near = functools.reduce(lambda a, b: a + b, parts[:epochs])
        far = functools.reduce(lambda a, b: a + b, parts[epochs:])
        return near + jnp.pad(far, ((0, rows - shared_rows), (0, 0), (0, 0)))

    by_row = jnp.transpose(source_params, (1, 0, 2))
    offsets = jnp.transpose(block_offsets, (0, 2, 1))
    packed = pl.pallas_call(
        functools.partial(pack_kernel, layout, spacing),
        out_shape=f32(rows + 1, blocks, sources),
        in_specs=[smem(), vmem()],
        out_specs=vmem(),
        compiler_params=params(),
        name="pack",
    )(block_lists, by_row)
    got = round_tiles([packed] * owners)
    slot_piece, slot_short, match = pl.pallas_call(
        functools.partial(select_kernel, layout),
        out_shape=[
            f32(rows, wide, sources),
            f32(shared_rows, wide, sources),
            f32(wide + blocks, owners * wide),
        ],
        in_specs=[smem()] + [vmem()] * owners,
        out_specs=[vmem()] * 3,
        compiler_params=params(),
        name="select",
    )(block_lists, *got)
    slot_rows = spread(slot_piece, slot_short)

    def gradient(moved):
        parts = step_gradient(
            layout, block_counts, offsets, psf_width, pixel_data, pixel_weight, slot_rows, moved
        )
        return summed(to_peers(parts[:epochs], parts[epochs:]))

    got = round_tiles([gradient(None)] * owners)
    slot_piece, slot_short, own_first = pl.pallas_call(
        functools.partial(combine_kernel, layout),
        out_shape=[
            f32(rows, wide, sources),
            f32(shared_rows, wide, sources),
            f32(rows, blocks, sources),
        ],
        in_specs=[vmem()] * (1 + owners),
        out_specs=[vmem()] * 3,
        compiler_params=params(),
        name="combine",
    )(match, *got)

    dense = pl.pallas_call(
        functools.partial(dense_kernel, rows),
        out_shape=[f32(rows, blocks, sources)] * owners,
        in_specs=[smem(), vmem()],
        out_specs=[vmem()] * owners,
        compiler_params=params(),
        name="dense",
    )(block_lists, gradient(spread(slot_piece, slot_short)))
    own = functools.reduce(lambda a, b: a + b, round_tiles(dense), own_first)
    whole = pl.pallas_call(
        functools.partial(final_kernel, layout, spacing),
        out_shape=f32(param_rows, blocks, sources),
        in_specs=[vmem()] * (1 + 2 * epochs),
        out_specs=vmem(),
        scratch_shapes=[pltpu.VMEM((BANDS, epochs, rows, blocks, sources), F32)],
        compiler_params=params(),
        name="final",
    )(by_row, *spread(own, own))
    return jnp.transpose(whole, (1, 0, 2))


def solution(mesh):
    return jax.shard_map(
        shards,
        mesh=mesh,
        in_specs=(
            P(("region", "tile"), None, None),
            P(("region", "tile"), "epoch", "band", None, None),
            P(("region", "tile"), "epoch", "band", None, None),
            P(("region", "epoch"), "band"),
            P(("region", "tile"), None),
            P(("region", "tile")),
            P(("region", "tile"), None, None),
        ),
        out_specs=P(("region", "tile"), None, None),
        check_vma=False,
    )
```

```python
import functools
import math

import jax
import jax.numpy as jnp
from jax import lax
from jax.experimental import pallas as pl
from jax.experimental.pallas import tpu as pltpu
from jax.sharding import PartitionSpec as P

ITERS = 2
STEP = 0.005
POSITION_RATE = 1.0 / 64.0
COMPS = 7
BANDS = 2
SHARED = 4 * COMPS
HALF = SHARED // BANDS
SPLIT_UNIT = 49152.0
SPLIT_SCALE = 65536.0
LOG2E = math.log2(math.e)
F32 = jnp.float32
BF16 = jnp.bfloat16
MIB = 1024 * 1024


def quarter_layout(epochs):
    shared_rows = -(-HALF // epochs)
    rows = -(-(HALF + COMPS) // epochs)
    pieces, amp = [], 0
    for q in range(epochs):
        piece = [("s", i) for i in range(q * shared_rows, min((q + 1) * shared_rows, HALF))]
        while len(piece) < rows and amp < COMPS:
            piece.append(("a", amp))
            amp += 1
        pieces.append(piece + [None] * (rows - len(piece)))
    return shared_rows, rows, pieces


def row_of(band, entry):
    kind, i = entry
    if kind == "a":
        return 2 + 6 * i + 4 + band, None
    k, c = divmod(HALF * band + i, COMPS)
    return 2 + 6 * c + k, (k if k < 2 else None)


def split3(x):
    hi = x.astype(BF16)
    rest = x - hi.astype(F32)
    mid = rest.astype(BF16)
    low = (rest - mid.astype(F32)).astype(BF16)
    return jnp.concatenate([hi, mid, low], axis=0)


def pick(matrix, rows):
    wide = jnp.concatenate([matrix, matrix, matrix], axis=1).astype(BF16)
    return jnp.dot(wide, split3(rows), preferred_element_type=F32)


def vmem():
    return pl.BlockSpec(memory_space=pltpu.VMEM)


def smem():
    return pl.BlockSpec(memory_space=pltpu.SMEM)


def f32(*shape):
    return jax.ShapeDtypeStruct(shape, F32)


def params(mib=4):
    return pltpu.CompilerParams(vmem_limit_bytes=mib * MIB)


def pack_kernel(layout, spacing, lists_ref, params_ref, out_ref):
    shared_rows, rows, pieces = layout
    band, epoch = lax.axis_index("band"), lax.axis_index("epoch")
    for b in range(BANDS):
        for q in range(len(pieces)):

            @pl.when((band == b) & (epoch == q))
            def _():
                for p, entry in enumerate(pieces[q]):
                    if entry is None:
                        out_ref[p] = jnp.zeros(out_ref.shape[1:], F32)
                        continue
                    row, position = row_of(b, entry)
                    value = params_ref[row]
                    if position is not None:
                        value = spacing * params_ref[position] + value
                    out_ref[p] = value

    tiles, slots = lists_ref.shape
    lane = lax.broadcasted_iota(jnp.int32, (8, 128), 1)
    ids = jnp.zeros((8, 128), jnp.int32)
    for t in range(tiles):
        for s in range(slots):
            ids = jnp.where(lane == t * slots + s, lists_ref[t, s], ids)
    out_ref[rows] = ids.astype(F32)


def select_kernel(layout, wide, *refs):
    shared_rows, rows, pieces = layout
    got, (out_ref, short_ref, match_ref, place_ref) = refs[:-4], refs[-4:]
    owners = len(got)
    blocks = got[0].shape[1]
    me = lax.axis_index("tile")
    own_line = got[0][rows, :1, :]
    own_column = jnp.broadcast_to(own_line, (128, 128)).T[:wide]

    shape = (wide, owners * blocks)
    lane = lax.broadcasted_iota(jnp.int32, shape, 1)
    held = lax.rem(me - lane // blocks + owners, owners) * blocks + lane % blocks
    choose = (own_column[:, : owners * blocks] == held.astype(F32)).astype(F32)
    for p in range(rows):
        chosen = pick(choose, jnp.concatenate([ref[p] for ref in got], axis=0))
        out_ref[p] = chosen
        if p < shared_rows:
            short_ref[p] = chosen

    lists = jnp.concatenate([ref[rows, :1, :wide] for ref in got], axis=1)
    match_ref[:wide] = (own_column[:, :1] == lists).astype(F32)
    own_blocks = me * blocks + lax.broadcasted_iota(jnp.int32, (blocks, owners * wide), 0)
    match_ref[wide:] = (own_blocks.astype(F32) == lists).astype(F32)
    line = lax.broadcasted_iota(jnp.int32, (owners * blocks, wide), 0)
    target = lax.rem(me + line // blocks, owners) * blocks + line % blocks
    place_ref[...] = (own_line[:, :wide] == target.astype(F32)).astype(F32)


def put_together(layout, band, epoch, ins, half, other, shared, amps):
    shared_rows, rows, pieces = layout
    epochs = len(pieces)
    for k in range(epochs):
        q = lax.rem(epoch - k + epochs, epochs)
        half[q] = ins[k][...]
        other[q] = ins[epochs + k][...]
    for q, piece in enumerate(pieces):
        for p, entry in enumerate(piece):
            if entry is None:
                continue
            kind, i = entry
            if kind == "s":
                shared[band, i] = half[q, p]
                shared[1 - band, i] = other[q, p]
            else:
                amps[i] = half[q, p]


def step_kernel(layout, later, counts_ref, offsets_ref, psf_ref, data_ref, weight_ref, *refs):
    shared_rows, rows, pieces = layout
    epochs = len(pieces)
    taken = 2 * epochs * (2 if later else 1)
    ins, refs = refs[:taken], refs[taken:]
    outs, refs = refs[: 2 * epochs], refs[2 * epochs :]
    shared, amps, derived, prof_x, prof_y, pieces_x, pieces_y, image, sums, half, other = refs[:11]
    band, epoch = lax.axis_index("band"), lax.axis_index("epoch")
    tiles = data_ref.shape[0]
    pixels = data_ref.shape[-1]
    wide = shared.shape[2]
    slots = wide // tiles
    spacing = pixels / 8.0

    put_together(layout, band, epoch, ins[: 2 * epochs], half, other, shared, amps)

    def row(k, c):
        r = k * COMPS + c
        return r // HALF, r % HALF

    if later:
        moved, moved_amps = refs[11:]
        put_together(layout, band, epoch, ins[2 * epochs :], half, other, moved, moved_amps)
        for k in range(4):
            shift = 0.0
            if k < 2:
                shift = functools.reduce(lambda a, b: a + b, [moved[row(k, c)] for c in range(COMPS)])
                shift = shift * (spacing * spacing * POSITION_RATE)
            for c in range(COMPS):
                shared[row(k, c)] = shared[row(k, c)] - STEP * (moved[row(k, c)] + shift)
        for c in range(COMPS):
            amps[c] = amps[c] - STEP * moved_amps[c]

    psf = psf_ref[0, 0]
    line_of = lax.broadcasted_iota(jnp.int32, (wide, 128), 0)
    live = jnp.zeros((wide, 128), jnp.bool_)
    for t in range(tiles):
        live = live | ((line_of >= t * slots) & (line_of < t * slots + counts_ref[t]))
    off_x = off_y = jnp.zeros((wide, 128), jnp.int32)
    for t in range(tiles):
        for s in range(slots):
            at = line_of == t * slots + s
            off_x = jnp.where(at, offsets_ref[t, 0, s], off_x)
            off_y = jnp.where(at, offsets_ref[t, 1, s], off_y)
    off_x, off_y = off_x.astype(F32), off_y.astype(F32)
    for c in range(COMPS):
        lw, an = shared[row(2, c)], shared[row(3, c)]
        derived[0, c] = shared[row(0, c)] + off_x
        derived[1, c] = shared[row(1, c)] + off_y
        derived[2, c] = (-0.5 * LOG2E) / (jnp.exp(2.0 * (lw + an)) + psf * psf)
        derived[3, c] = (-0.5 * LOG2E) / (jnp.exp(2.0 * (lw - an)) + psf * psf)
        derived[4, c] = jnp.where(live, amps[c], 0.0)
        derived[5, c] = derived[4, c] * SPLIT_SCALE
    sums[...] = jnp.zeros_like(sums)

    grid = lax.broadcasted_iota(jnp.int32, (pixels, 128), 0).astype(F32)

    def cut(x, large):
        hi = (x + large) - large
        return jnp.concatenate([hi, x - hi], axis=0)

    def stack(x):
        hi = x.astype(BF16).astype(F32)
        return jnp.concatenate([hi, hi, x - hi], axis=1)

    def times(left, right):
        return jnp.dot(left, jnp.concatenate([right, right[:pixels]], axis=0), preferred_element_type=F32)

    middle = pixels // 2
    inner = lax.broadcasted_iota(jnp.int32, (8, 128), 0).astype(F32)

    def running(groups):
        sum_0 = sum_1 = sum_2 = groups[0]
        for group in groups[1:]:
            sum_0 = sum_0 + group
            sum_1 = sum_1 + sum_0
            sum_2 = sum_2 + sum_1
        return sum_0, sum_1, sum_2

    def moments(x):
        groups = [x[r : r + 8] for r in range(0, pixels, 8)]
        high = running(groups[len(groups) // 2 :][::-1])
        low = running(groups[: len(groups) // 2])
        m0 = high[0] + low[0]
        m1 = high[1] - high[0] - low[1]
        m2 = 2.0 * (high[2] + low[2]) - 2.0 * high[1] - (high[1] - high[0]) - low[1]
        first = inner * m0 + 8.0 * m1
        second = inner * (first + 8.0 * m1) + 64.0 * m2
        return [jnp.sum(m, axis=0, keepdims=True) for m in (m0, first, second)]

    def line(index, c, s):
        return derived[index, c, pl.ds(s, 1), :]

    together = 2
    for t in range(tiles):
        trips = (counts_ref[t] + together - 1) // together
        image[...] = jnp.zeros_like(image)

        def render(i, carry):
            for u in range(together):
                s = i * together + u
                g = t * slots + s
                for c in range(COMPS):
                    d = grid - line(0, c, g)
                    e = jnp.exp2(d * d * line(2, c, g))
                    prof_x[s * COMPS + c] = e
                    pieces_x[s, :, c * 128 : (c + 1) * 128] = cut(e, SPLIT_UNIT)
                    d = grid - line(1, c, g)
                    e = jnp.exp2(d * d * line(3, c, g))
                    prof_y[s * COMPS + c] = e
                    pieces_y[s, :, c * 128 : (c + 1) * 128] = cut(e * line(4, c, g), line(5, c, g))
                image[...] += lax.dot_general(
                    pieces_x[s], pieces_y[s], (((1,), (1,)), ((), ())), preferred_element_type=F32
                )
            return carry

        lax.fori_loop(0, trips, render, 0)

        model = (image[:pixels, :pixels] + image[pixels:, pixels:]) + (
            image[:pixels, pixels:] + image[pixels:, :pixels]
        )
        cotangent = weight_ref[t, 0, 0] * (model - data_ref[t, 0, 0])
        left_x, left_y = stack(cotangent), stack(cotangent.T)

        def pull(i, carry):
            for u in range(together):
                s = i * together + u
                g = t * slots + s
                for first in range(0, COMPS, 2):
                    here = min(2, COMPS - first)
                    span = pl.ds(first * 128, 128 * here)
                    by_x = times(left_x, pieces_y[s, :, span])
                    by_y = times(left_y, pieces_x[s, :, span])
                    for n in range(here):
                        c = first + n
                        at = slice(n * 128, (n + 1) * 128)
                        for k, value in enumerate(moments(prof_x[s * COMPS + c] * by_x[:, at])):
                            sums[k, c, pl.ds(g, 1), :] = value
                        for k, value in enumerate(moments(prof_y[s * COMPS + c] * by_y[:, at])):
                            sums[3 + k, c, pl.ds(g, 1), :] = value
            return carry

        lax.fori_loop(0, trips, pull, 0)

    def keep(x):
        return jnp.where(live, x, 0.0)

    for c in range(COMPS):
        lw, an = shared[row(2, c)], shared[row(3, c)]
        wide_x, wide_y = jnp.exp(2.0 * (lw + an)), jnp.exp(2.0 * (lw - an))
        inv_x, inv_y = 1.0 / (wide_x + psf * psf), 1.0 / (wide_y + psf * psf)
        amp = amps[c]
        shift_x, shift_y = middle - derived[0, c], middle - derived[1, c]
        first_x = sums[1, c] + shift_x * sums[0, c]
        first_y = sums[4, c] + shift_y * sums[3, c]
        second_x = sums[2, c] + shift_x * (sums[1, c] + first_x)
        second_y = sums[5, c] + shift_y * (sums[4, c] + first_y)
        var_x = keep(second_x * inv_x * (inv_x * wide_x))
        var_y = keep(amp * second_y * inv_y * (inv_y * wide_y))
        shared[row(0, c)] = keep(first_x * inv_x)
        shared[row(1, c)] = keep(amp * first_y * inv_y)
        shared[row(2, c)] = var_x + var_y
        shared[row(3, c)] = var_x - var_y
        amps[c] = keep(sums[3, c])
    none = jnp.zeros((wide, 128), F32)
    for q, piece in enumerate(pieces):
        for p, entry in enumerate(piece):
            is_shared = entry is not None and entry[0] == "s"
            if is_shared:
                half[q, p] = shared[band, entry[1]]
            else:
                half[q, p] = none if entry is None else amps[entry[1]]
            if p < shared_rows:
                other[q, p] = shared[1 - band, entry[1]] if is_shared else none
    for k in range(epochs):
        outs[k][...] = half[lax.rem(epoch + k, epochs)]
        outs[epochs + k][...] = other[lax.rem(epoch + k, epochs)]


def step_gradient(layout, counts, offsets, psf, data, weight, slot_rows, moved):
    shared_rows, rows, pieces = layout
    epochs = len(pieces)
    later = moved is not None
    tiles, _, slots = offsets.shape
    pixels = data.shape[-1]
    wide = tiles * slots
    shapes = [(rows, wide, 128)] * epochs + [(shared_rows, wide, 128)] * epochs
    ins = slot_rows + (moved or [])
    together = [pltpu.VMEM((BANDS, HALF, wide, 128), F32), pltpu.VMEM((COMPS, wide, 128), F32)]
    return pl.pallas_call(
        functools.partial(step_kernel, layout, later),
        out_shape=[f32(*s) for s in shapes],
        in_specs=[smem()] * 3 + [vmem()] * (2 + len(ins)),
        out_specs=[vmem()] * len(shapes),
        scratch_shapes=together
        + [
            pltpu.VMEM((6, COMPS, wide, 128), F32),
            pltpu.VMEM((slots * COMPS, pixels, 128), F32),
            pltpu.VMEM((slots * COMPS, pixels, 128), F32),
            pltpu.VMEM((slots, 2 * pixels, COMPS * 128), F32),
            pltpu.VMEM((slots, 2 * pixels, COMPS * 128), F32),
            pltpu.VMEM((2 * pixels, 2 * pixels), F32),
            pltpu.VMEM((6, COMPS, wide, 128), F32),
            pltpu.VMEM((epochs, rows, wide, 128), F32),
            pltpu.VMEM((epochs, shared_rows, wide, 128), F32),
        ]
        + (together if later else []),
        compiler_params=params(40),
        name="later_step" if later else "first_step",
    )(counts, offsets, psf, data, weight, *ins)


def combine_kernel(layout, match_ref, *refs):
    shared_rows, rows, pieces = layout
    got, (out_ref, short_ref, own_ref) = refs[:-3], refs[-3:]
    wide = out_ref.shape[1]
    match = match_ref[...]
    for p in range(rows):
        both = pick(match, jnp.concatenate([ref[p] for ref in got], axis=0))
        out_ref[p] = both[:wide]
        if p < shared_rows:
            short_ref[p] = both[:wide]
        own_ref[p] = both[wide:]


def dense_kernel(rows, place_ref, grads, *outs):
    blocks = outs[0].shape[1]
    place = place_ref[...]
    for p in range(rows):
        dense = pick(place, grads[p])
        for k, out in enumerate(outs):
            out[p] = dense[k * blocks : (k + 1) * blocks]


def final_kernel(layout, spacing, params_ref, *refs):
    shared_rows, rows, pieces = layout
    epochs = len(pieces)
    ins, (out_ref, held) = refs[: 2 * epochs], refs[2 * epochs :]
    band, epoch = lax.axis_index("band"), lax.axis_index("epoch")
    for k in range(epochs):
        q = lax.rem(epoch - k + epochs, epochs)
        held[band, q] = ins[k][...]
        held[1 - band, q] = ins[epochs + k][...]
    shift = [0.0, 0.0]
    for b in range(BANDS):
        for q, piece in enumerate(pieces):
            for p, entry in enumerate(piece):
                if entry is None:
                    continue
                row, position = row_of(b, entry)
                grad = held[b, q, p]
                out_ref[row] = params_ref[row] - STEP * grad
                if position is not None:
                    shift[position] = shift[position] + grad
    for k in range(2):
        out_ref[k] = params_ref[k] - (STEP * POSITION_RATE * spacing) * shift[k]


def shards(source_params, pixel_data, pixel_weight, psf_width, block_lists, block_counts, block_offsets):
    owners, epochs = lax.axis_size("tile"), lax.axis_size("epoch")
    blocks, param_rows, sources = source_params.shape
    tiles, slots = block_lists.shape
    wide = tiles * slots
    spacing = pixel_data.shape[-1] / 8.0
    layout = quarter_layout(epochs)
    shared_rows, rows, pieces = layout

    def to_peers(same, other):
        kept = [same[0]]
        for k in range(1, epochs):
            kept.append(lax.ppermute(same[k], "epoch", [(i, (i + k) % epochs) for i in range(epochs)]))
        for k in range(epochs):
            pairs = [
                (i * BANDS + b, (i + k) % epochs * BANDS + 1 - b)
                for i in range(epochs)
                for b in range(BANDS)
            ]
            kept.append(lax.ppermute(other[k], ("epoch", "band"), pairs))
        return kept

    def round_tiles(arrays):
        return [arrays[0]] + [
            lax.ppermute(arrays[k], "tile", [(i, (i + k) % owners) for i in range(owners)])
            for k in range(1, owners)
        ]

    def spread(piece, other):
        return to_peers([piece] * epochs, [other] * epochs)

    def summed(parts):
        near = functools.reduce(lambda a, b: a + b, parts[:epochs])
        far = functools.reduce(lambda a, b: a + b, parts[epochs:])
        return near + jnp.pad(far, ((0, rows - shared_rows), (0, 0), (0, 0)))

    by_row = jnp.transpose(source_params, (1, 0, 2))
    offsets = jnp.transpose(block_offsets, (0, 2, 1))
    packed = pl.pallas_call(
        functools.partial(pack_kernel, layout, spacing),
        out_shape=f32(rows + 1, blocks, sources),
        in_specs=[smem(), vmem()],
        out_specs=vmem(),
        compiler_params=params(),
        name="pack",
    )(block_lists, by_row)
    got = round_tiles([packed] * owners)
    slot_piece, slot_short, match, place = pl.pallas_call(
        functools.partial(select_kernel, layout, wide),
        out_shape=[
            f32(rows, wide, sources),
            f32(shared_rows, wide, sources),
            f32(wide + blocks, owners * wide),
            f32(owners * blocks, wide),
        ],
        in_specs=[vmem()] * owners,
        out_specs=[vmem()] * 4,
        compiler_params=params(),
        name="select",
    )(*got)
    slot_rows = spread(slot_piece, slot_short)

    def gradient(moved):
        parts = step_gradient(
            layout, block_counts, offsets, psf_width, pixel_data, pixel_weight, slot_rows, moved
        )
        return summed(to_peers(parts[:epochs], parts[epochs:]))

    got = round_tiles([gradient(None)] * owners)
    slot_piece, slot_short, own_first = pl.pallas_call(
        functools.partial(combine_kernel, layout),
        out_shape=[
            f32(rows, wide, sources),
            f32(shared_rows, wide, sources),
            f32(rows, blocks, sources),
        ],
        in_specs=[vmem()] * (1 + owners),
        out_specs=[vmem()] * 3,
        compiler_params=params(),
        name="combine",
    )(match, *got)

    dense = pl.pallas_call(
        functools.partial(dense_kernel, rows),
        out_shape=[f32(rows, blocks, sources)] * owners,
        in_specs=[vmem()] * 2,
        out_specs=[vmem()] * owners,
        compiler_params=params(),
        name="dense",
    )(place, gradient(spread(slot_piece, slot_short)))
    own = functools.reduce(lambda a, b: a + b, round_tiles(dense), own_first)
    whole = pl.pallas_call(
        functools.partial(final_kernel, layout, spacing),
        out_shape=f32(param_rows, blocks, sources),
        in_specs=[vmem()] * (1 + 2 * epochs),
        out_specs=vmem(),
        scratch_shapes=[pltpu.VMEM((BANDS, epochs, rows, blocks, sources), F32)],
        compiler_params=params(),
        name="final",
    )(by_row, *spread(own, own))
    return jnp.transpose(whole, (1, 0, 2))


def solution(mesh):
    return jax.shard_map(
        shards,
        mesh=mesh,
        in_specs=(
            P(("region", "tile"), None, None),
            P(("region", "tile"), "epoch", "band", None, None),
            P(("region", "tile"), "epoch", "band", None, None),
            P(("region", "epoch"), "band"),
            P(("region", "tile"), None),
            P(("region", "tile")),
            P(("region", "tile"), None, None),
        ),
        out_specs=P(("region", "tile"), None, None),
        check_vma=False,
    )
```

```python
import functools
import math

import jax
import jax.numpy as jnp
from jax import lax
from jax.experimental import pallas as pl
from jax.experimental.pallas import tpu as pltpu
from jax.sharding import PartitionSpec as P

ITERS = 2
STEP = 0.005
POSITION_RATE = 1.0 / 64.0
COMPS = 7
BANDS = 2
SHARED = 4 * COMPS
HALF = SHARED // BANDS
SPLIT_UNIT = 49152.0
SPLIT_SCALE = 65536.0
LOG2E = math.log2(math.e)
F32 = jnp.float32
BF16 = jnp.bfloat16
BLOCK = 32
MIB = 1024 * 1024


def quarter_layout(epochs):
    shared_rows = -(-HALF // epochs)
    rows = -(-(HALF + COMPS) // epochs)
    pieces, amp = [], 0
    for q in range(epochs):
        piece = [("s", i) for i in range(q * shared_rows, min((q + 1) * shared_rows, HALF))]
        while len(piece) < rows and amp < COMPS:
            piece.append(("a", amp))
            amp += 1
        pieces.append(piece + [None] * (rows - len(piece)))
    return shared_rows, rows, pieces


def row_of(band, entry):
    kind, i = entry
    if kind == "a":
        return 2 + 6 * i + 4 + band, None
    k, c = divmod(HALF * band + i, COMPS)
    return 2 + 6 * c + k, (k if k < 2 else None)


def split3(x):
    hi = x.astype(BF16)
    rest = x - hi.astype(F32)
    mid = rest.astype(BF16)
    low = (rest - mid.astype(F32)).astype(BF16)
    return jnp.concatenate([hi, mid, low], axis=0)


def pick(matrix, rows):
    wide = jnp.concatenate([matrix, matrix, matrix], axis=1).astype(BF16)
    return jnp.dot(wide, split3(rows), preferred_element_type=F32)


def vmem():
    return pl.BlockSpec(memory_space=pltpu.VMEM)


def smem():
    return pl.BlockSpec(memory_space=pltpu.SMEM)


def f32(*shape):
    return jax.ShapeDtypeStruct(shape, F32)


def params(mib=4):
    return pltpu.CompilerParams(vmem_limit_bytes=mib * MIB)


def pack_kernel(layout, spacing, lists_ref, params_ref, out_ref):
    shared_rows, rows, pieces = layout
    band, epoch = lax.axis_index("band"), lax.axis_index("epoch")
    for b in range(BANDS):
        for q in range(len(pieces)):

            @pl.when((band == b) & (epoch == q))
            def _():
                for p, entry in enumerate(pieces[q]):
                    if entry is None:
                        out_ref[p] = jnp.zeros(out_ref.shape[1:], F32)
                        continue
                    row, position = row_of(b, entry)
                    value = params_ref[row]
                    if position is not None:
                        value = spacing * params_ref[position] + value
                    out_ref[p] = value

    tiles, slots = lists_ref.shape
    lane = lax.broadcasted_iota(jnp.int32, (8, 128), 1)
    ids = jnp.zeros((8, 128), jnp.int32)
    for t in range(tiles):
        for s in range(slots):
            ids = jnp.where(lane == t * slots + s, lists_ref[t, s], ids)
    out_ref[rows] = ids.astype(F32)


def select_kernel(layout, wide, *refs):
    shared_rows, rows, pieces = layout
    got, (out_ref, short_ref, match_ref, place_ref) = refs[:-4], refs[-4:]
    owners = len(got)
    blocks = got[0].shape[1]
    me = lax.axis_index("tile")
    own_line = got[0][rows, :1, :]
    own_column = jnp.broadcast_to(own_line, (128, 128)).T[:wide]

    shape = (wide, owners * blocks)
    lane = lax.broadcasted_iota(jnp.int32, shape, 1)
    held = lax.rem(me - lane // blocks + owners, owners) * blocks + lane % blocks
    choose = (own_column[:, : owners * blocks] == held.astype(F32)).astype(F32)
    for p in range(rows):
        chosen = pick(choose, jnp.concatenate([ref[p] for ref in got], axis=0))
        out_ref[p] = chosen
        if p < shared_rows:
            short_ref[p] = chosen

    lists = jnp.concatenate([ref[rows, :1, :wide] for ref in got], axis=1)
    match_ref[:wide] = (own_column[:, :1] == lists).astype(F32)
    own_blocks = me * blocks + lax.broadcasted_iota(jnp.int32, (blocks, owners * wide), 0)
    match_ref[wide:] = (own_blocks.astype(F32) == lists).astype(F32)
    line = lax.broadcasted_iota(jnp.int32, (owners * blocks, wide), 0)
    target = lax.rem(me + line // blocks, owners) * blocks + line % blocks
    place_ref[...] = (own_line[:, :wide] == target.astype(F32)).astype(F32)


def put_together(layout, band, epoch, ins, half, other, shared, amps):
    shared_rows, rows, pieces = layout
    epochs = len(pieces)
    for k in range(epochs):
        q = lax.rem(epoch - k + epochs, epochs)
        half[q] = ins[k][...]
        other[q] = ins[epochs + k][...]
    for q, piece in enumerate(pieces):
        for p, entry in enumerate(piece):
            if entry is None:
                continue
            kind, i = entry
            if kind == "s":
                shared[band, i] = half[q, p]
                shared[1 - band, i] = other[q, p]
            else:
                amps[i] = half[q, p]


def step_kernel(layout, later, counts_ref, offsets_ref, psf_ref, data_ref, weight_ref, *refs):
    shared_rows, rows, pieces = layout
    epochs = len(pieces)
    taken = 2 * epochs * (2 if later else 1)
    ins, refs = refs[:taken], refs[taken:]
    outs, refs = refs[: 2 * epochs], refs[2 * epochs :]
    shared, amps, derived, prof_x, prof_y, pieces_x, pieces_y, image, sums, half, other = refs[:11]
    band, epoch = lax.axis_index("band"), lax.axis_index("epoch")
    tiles = data_ref.shape[0]
    pixels = data_ref.shape[-1]
    wide = shared.shape[2]
    slots = wide // tiles
    spacing = pixels / 8.0

    put_together(layout, band, epoch, ins[: 2 * epochs], half, other, shared, amps)

    def row(k, c):
        r = k * COMPS + c
        return r // HALF, r % HALF

    if later:
        moved, moved_amps = refs[11:]
        put_together(layout, band, epoch, ins[2 * epochs :], half, other, moved, moved_amps)
        for k in range(4):
            shift = 0.0
            if k < 2:
                shift = functools.reduce(lambda a, b: a + b, [moved[row(k, c)] for c in range(COMPS)])
                shift = shift * (spacing * spacing * POSITION_RATE)
            for c in range(COMPS):
                shared[row(k, c)] = shared[row(k, c)] - STEP * (moved[row(k, c)] + shift)
        for c in range(COMPS):
            amps[c] = amps[c] - STEP * moved_amps[c]

    psf = psf_ref[0, 0]
    line_of = lax.broadcasted_iota(jnp.int32, (wide, 128), 0)
    live = jnp.zeros((wide, 128), jnp.bool_)
    for t in range(tiles):
        live = live | ((line_of >= t * slots) & (line_of < t * slots + counts_ref[t]))
    off_x = off_y = jnp.zeros((wide, 128), jnp.int32)
    for t in range(tiles):
        for s in range(slots):
            at = line_of == t * slots + s
            off_x = jnp.where(at, offsets_ref[t, 0, s], off_x)
            off_y = jnp.where(at, offsets_ref[t, 1, s], off_y)
    off_x, off_y = off_x.astype(F32), off_y.astype(F32)
    for c in range(COMPS):
        lw, an = shared[row(2, c)], shared[row(3, c)]
        derived[0, c] = shared[row(0, c)] + off_x
        derived[1, c] = shared[row(1, c)] + off_y
        derived[2, c] = (-0.5 * LOG2E) / (jnp.exp(2.0 * (lw + an)) + psf * psf)
        derived[3, c] = (-0.5 * LOG2E) / (jnp.exp(2.0 * (lw - an)) + psf * psf)
        derived[4, c] = jnp.where(live, amps[c], 0.0)
        derived[5, c] = derived[4, c] * SPLIT_SCALE
    sums[...] = jnp.zeros_like(sums)

    first_rows = lax.broadcasted_iota(jnp.int32, (BLOCK, 128), 0).astype(F32)

    def stack(x):
        hi = x.astype(BF16).astype(F32)
        return jnp.concatenate([hi, hi, x - hi], axis=1)

    def times(left, right):
        return jnp.dot(left, jnp.concatenate([right, right[:pixels]], axis=0), preferred_element_type=F32)

    middle = pixels // 2
    inner = lax.broadcasted_iota(jnp.int32, (8, 128), 0).astype(F32)

    def running(groups):
        sum_0 = sum_1 = sum_2 = groups[0]
        for group in groups[1:]:
            sum_0 = sum_0 + group
            sum_1 = sum_1 + sum_0
            sum_2 = sum_2 + sum_1
        return sum_0, sum_1, sum_2

    def moments(x):
        groups = [x[r : r + 8] for r in range(0, pixels, 8)]
        high = running(groups[len(groups) // 2 :][::-1])
        low = running(groups[: len(groups) // 2])
        m0 = high[0] + low[0]
        m1 = high[1] - high[0] - low[1]
        m2 = 2.0 * (high[2] + low[2]) - 2.0 * high[1] - (high[1] - high[0]) - low[1]
        first = inner * m0 + 8.0 * m1
        second = inner * (first + 8.0 * m1) + 64.0 * m2
        return [jnp.sum(m, axis=0, keepdims=True) for m in (m0, first, second)]

    def line(index, c, s):
        return derived[index, c, pl.ds(s, 1), :]

    together = 2
    for t in range(tiles):
        trips = (counts_ref[t] + together - 1) // together
        image[...] = jnp.zeros_like(image)

        def render(i, carry):
            for u in range(together):
                s = i * together + u
                g = t * slots + s
                for c in range(COMPS):
                    at = slice(c * 128, (c + 1) * 128)
                    centre_x, centre_y = line(0, c, g), line(1, c, g)
                    scale_x, scale_y = line(2, c, g), line(3, c, g)
                    amp, large = line(4, c, g), line(5, c, g)
                    for r in range(0, pixels, BLOCK):
                        d = (first_rows - centre_x) + F32(r)
                        e = jnp.exp2(d * d * scale_x)
                        prof_x[s * COMPS + c, r : r + BLOCK] = e
                        hi = (e + SPLIT_UNIT) - SPLIT_UNIT
                        pieces_x[s, r : r + BLOCK, at] = hi
                        pieces_x[s, pixels + r : pixels + r + BLOCK, at] = e - hi
                        d = (first_rows - centre_y) + F32(r)
                        e = jnp.exp2(d * d * scale_y)
                        prof_y[s * COMPS + c, r : r + BLOCK] = e
                        e = e * amp
                        hi = (e + large) - large
                        pieces_y[s, r : r + BLOCK, at] = hi
                        pieces_y[s, pixels + r : pixels + r + BLOCK, at] = e - hi
                image[...] += lax.dot_general(
                    pieces_x[s], pieces_y[s], (((1,), (1,)), ((), ())), preferred_element_type=F32
                )
            return carry

        lax.fori_loop(0, trips, render, 0)

        model = (image[:pixels, :pixels] + image[pixels:, pixels:]) + (
            image[:pixels, pixels:] + image[pixels:, :pixels]
        )
        cotangent = weight_ref[t, 0, 0] * (model - data_ref[t, 0, 0])
        left_x, left_y = stack(cotangent), stack(cotangent.T)

        def pull(i, carry):
            for u in range(together):
                s = i * together + u
                g = t * slots + s
                for first in range(0, COMPS, 2):
                    here = min(2, COMPS - first)
                    span = pl.ds(first * 128, 128 * here)
                    for left, pieces, prof, k0 in (
                        (left_x, pieces_y, prof_x, 0),
                        (left_y, pieces_x, prof_y, 3),
                    ):
                        by = times(left, pieces[s, :, span])
                        for n in range(here):
                            c = first + n
                            found = moments(prof[s * COMPS + c] * by[:, n * 128 : (n + 1) * 128])
                            for k, value in enumerate(found):
                                sums[k0 + k, c, pl.ds(g, 1), :] = value
            return carry

        lax.fori_loop(0, trips, pull, 0)

    def keep(x):
        return jnp.where(live, x, 0.0)

    for c in range(COMPS):
        lw, an = shared[row(2, c)], shared[row(3, c)]
        wide_x, wide_y = jnp.exp(2.0 * (lw + an)), jnp.exp(2.0 * (lw - an))
        inv_x, inv_y = 1.0 / (wide_x + psf * psf), 1.0 / (wide_y + psf * psf)
        amp = amps[c]
        shift_x, shift_y = middle - derived[0, c], middle - derived[1, c]
        first_x = sums[1, c] + shift_x * sums[0, c]
        first_y = sums[4, c] + shift_y * sums[3, c]
        second_x = sums[2, c] + shift_x * (sums[1, c] + first_x)
        second_y = sums[5, c] + shift_y * (sums[4, c] + first_y)
        var_x = keep(second_x * inv_x * (inv_x * wide_x))
        var_y = keep(amp * second_y * inv_y * (inv_y * wide_y))
        shared[row(0, c)] = keep(first_x * inv_x)
        shared[row(1, c)] = keep(amp * first_y * inv_y)
        shared[row(2, c)] = var_x + var_y
        shared[row(3, c)] = var_x - var_y
        amps[c] = keep(sums[3, c])
    none = jnp.zeros((wide, 128), F32)
    for q, piece in enumerate(pieces):
        for p, entry in enumerate(piece):
            is_shared = entry is not None and entry[0] == "s"
            if is_shared:
                half[q, p] = shared[band, entry[1]]
            else:
                half[q, p] = none if entry is None else amps[entry[1]]
            if p < shared_rows:
                other[q, p] = shared[1 - band, entry[1]] if is_shared else none
    for k in range(epochs):
        outs[k][...] = half[lax.rem(epoch + k, epochs)]
        outs[epochs + k][...] = other[lax.rem(epoch + k, epochs)]


def step_gradient(layout, counts, offsets, psf, data, weight, slot_rows, moved):
    shared_rows, rows, pieces = layout
    epochs = len(pieces)
    later = moved is not None
    tiles, _, slots = offsets.shape
    pixels = data.shape[-1]
    wide = tiles * slots
    shapes = [(rows, wide, 128)] * epochs + [(shared_rows, wide, 128)] * epochs
    ins = slot_rows + (moved or [])
    together = [pltpu.VMEM((BANDS, HALF, wide, 128), F32), pltpu.VMEM((COMPS, wide, 128), F32)]
    return pl.pallas_call(
        functools.partial(step_kernel, layout, later),
        out_shape=[f32(*s) for s in shapes],
        in_specs=[smem()] * 3 + [vmem()] * (2 + len(ins)),
        out_specs=[vmem()] * len(shapes),
        scratch_shapes=together
        + [
            pltpu.VMEM((6, COMPS, wide, 128), F32),
            pltpu.VMEM((slots * COMPS, pixels, 128), F32),
            pltpu.VMEM((slots * COMPS, pixels, 128), F32),
            pltpu.VMEM((slots, 2 * pixels, COMPS * 128), F32),
            pltpu.VMEM((slots, 2 * pixels, COMPS * 128), F32),
            pltpu.VMEM((2 * pixels, 2 * pixels), F32),
            pltpu.VMEM((6, COMPS, wide, 128), F32),
            pltpu.VMEM((epochs, rows, wide, 128), F32),
            pltpu.VMEM((epochs, shared_rows, wide, 128), F32),
        ]
        + (together if later else []),
        compiler_params=params(40),
        name="later_step" if later else "first_step",
    )(counts, offsets, psf, data, weight, *ins)


def combine_kernel(layout, match_ref, *refs):
    shared_rows, rows, pieces = layout
    got, (out_ref, short_ref, own_ref) = refs[:-3], refs[-3:]
    wide = out_ref.shape[1]
    match = match_ref[...]
    for p in range(rows):
        both = pick(match, jnp.concatenate([ref[p] for ref in got], axis=0))
        out_ref[p] = both[:wide]
        if p < shared_rows:
            short_ref[p] = both[:wide]
        own_ref[p] = both[wide:]


def dense_kernel(rows, place_ref, grads, *outs):
    blocks = outs[0].shape[1]
    place = place_ref[...]
    for p in range(rows):
        dense = pick(place, grads[p])
        for k, out in enumerate(outs):
            out[p] = dense[k * blocks : (k + 1) * blocks]


def final_kernel(layout, spacing, params_ref, *refs):
    shared_rows, rows, pieces = layout
    epochs = len(pieces)
    ins, (out_ref, held) = refs[: 2 * epochs], refs[2 * epochs :]
    band, epoch = lax.axis_index("band"), lax.axis_index("epoch")
    for k in range(epochs):
        q = lax.rem(epoch - k + epochs, epochs)
        held[band, q] = ins[k][...]
        held[1 - band, q] = ins[epochs + k][...]
    shift = [0.0, 0.0]
    for b in range(BANDS):
        for q, piece in enumerate(pieces):
            for p, entry in enumerate(piece):
                if entry is None:
                    continue
                row, position = row_of(b, entry)
                grad = held[b, q, p]
                out_ref[row] = params_ref[row] - STEP * grad
                if position is not None:
                    shift[position] = shift[position] + grad
    for k in range(2):
        out_ref[k] = params_ref[k] - (STEP * POSITION_RATE * spacing) * shift[k]


def shards(source_params, pixel_data, pixel_weight, psf_width, block_lists, block_counts, block_offsets):
    owners, epochs = lax.axis_size("tile"), lax.axis_size("epoch")
    blocks, param_rows, sources = source_params.shape
    tiles, slots = block_lists.shape
    wide = tiles * slots
    spacing = pixel_data.shape[-1] / 8.0
    layout = quarter_layout(epochs)
    shared_rows, rows, pieces = layout

    def to_peers(same, other):
        kept = [same[0]]
        for k in range(1, epochs):
            kept.append(lax.ppermute(same[k], "epoch", [(i, (i + k) % epochs) for i in range(epochs)]))
        for k in range(epochs):
            pairs = [
                (i * BANDS + b, (i + k) % epochs * BANDS + 1 - b)
                for i in range(epochs)
                for b in range(BANDS)
            ]
            kept.append(lax.ppermute(other[k], ("epoch", "band"), pairs))
        return kept

    def round_tiles(arrays):
        return [arrays[0]] + [
            lax.ppermute(arrays[k], "tile", [(i, (i + k) % owners) for i in range(owners)])
            for k in range(1, owners)
        ]

    def spread(piece, other):
        return to_peers([piece] * epochs, [other] * epochs)

    def summed(parts):
        near = functools.reduce(lambda a, b: a + b, parts[:epochs])
        far = functools.reduce(lambda a, b: a + b, parts[epochs:])
        return near + jnp.pad(far, ((0, rows - shared_rows), (0, 0), (0, 0)))

    by_row = jnp.transpose(source_params, (1, 0, 2))
    offsets = jnp.transpose(block_offsets, (0, 2, 1))
    packed = pl.pallas_call(
        functools.partial(pack_kernel, layout, spacing),
        out_shape=f32(rows + 1, blocks, sources),
        in_specs=[smem(), vmem()],
        out_specs=vmem(),
        compiler_params=params(),
        name="pack",
    )(block_lists, by_row)
    got = round_tiles([packed] * owners)
    slot_piece, slot_short, match, place = pl.pallas_call(
        functools.partial(select_kernel, layout, wide),
        out_shape=[
            f32(rows, wide, sources),
            f32(shared_rows, wide, sources),
            f32(wide + blocks, owners * wide),
            f32(owners * blocks, wide),
        ],
        in_specs=[vmem()] * owners,
        out_specs=[vmem()] * 4,
        compiler_params=params(),
        name="select",
    )(*got)
    slot_rows = spread(slot_piece, slot_short)

    def gradient(moved):
        parts = step_gradient(
            layout, block_counts, offsets, psf_width, pixel_data, pixel_weight, slot_rows, moved
        )
        return summed(to_peers(parts[:epochs], parts[epochs:]))

    got = round_tiles([gradient(None)] * owners)
    slot_piece, slot_short, own_first = pl.pallas_call(
        functools.partial(combine_kernel, layout),
        out_shape=[
            f32(rows, wide, sources),
            f32(shared_rows, wide, sources),
            f32(rows, blocks, sources),
        ],
        in_specs=[vmem()] * (1 + owners),
        out_specs=[vmem()] * 3,
        compiler_params=params(),
        name="combine",
    )(match, *got)

    dense = pl.pallas_call(
        functools.partial(dense_kernel, rows),
        out_shape=[f32(rows, blocks, sources)] * owners,
        in_specs=[vmem()] * 2,
        out_specs=[vmem()] * owners,
        compiler_params=params(),
        name="dense",
    )(place, gradient(spread(slot_piece, slot_short)))
    own = functools.reduce(lambda a, b: a + b, round_tiles(dense), own_first)
    whole = pl.pallas_call(
        functools.partial(final_kernel, layout, spacing),
        out_shape=f32(param_rows, blocks, sources),
        in_specs=[vmem()] * (1 + 2 * epochs),
        out_specs=vmem(),
        scratch_shapes=[pltpu.VMEM((BANDS, epochs, rows, blocks, sources), F32)],
        compiler_params=params(),
        name="final",
    )(by_row, *spread(own, own))
    return jnp.transpose(whole, (1, 0, 2))


def solution(mesh):
    return jax.shard_map(
        shards,
        mesh=mesh,
        in_specs=(
            P(("region", "tile"), None, None),
            P(("region", "tile"), "epoch", "band", None, None),
            P(("region", "tile"), "epoch", "band", None, None),
            P(("region", "epoch"), "band"),
            P(("region", "tile"), None),
            P(("region", "tile")),
            P(("region", "tile"), None, None),
        ),
        out_specs=P(("region", "tile"), None, None),
        check_vma=False,
    )
```

```python
import functools
import math

import jax
import jax.numpy as jnp
from jax import lax
from jax.experimental import pallas as pl
from jax.experimental.pallas import tpu as pltpu
from jax.sharding import PartitionSpec as P

ITERS = 2
STEP = 0.005
POSITION_RATE = 1.0 / 64.0
COMPS = 7
BANDS = 2
SHARED = 4 * COMPS
HALF = SHARED // BANDS
SPLIT_UNIT = 49152.0
SPLIT_SCALE = 65536.0
LOG2E = math.log2(math.e)
F32 = jnp.float32
BF16 = jnp.bfloat16
MIB = 1024 * 1024


def quarter_layout(epochs):
    shared_rows = -(-HALF // epochs)
    rows = -(-(HALF + COMPS) // epochs)
    pieces, amp = [], 0
    for q in range(epochs):
        piece = [("s", i) for i in range(q * shared_rows, min((q + 1) * shared_rows, HALF))]
        while len(piece) < rows and amp < COMPS:
            piece.append(("a", amp))
            amp += 1
        pieces.append(piece + [None] * (rows - len(piece)))
    return shared_rows, rows, pieces


def row_of(band, entry):
    kind, i = entry
    if kind == "a":
        return 2 + 6 * i + 4 + band, None
    k, c = divmod(HALF * band + i, COMPS)
    return 2 + 6 * c + k, (k if k < 2 else None)


def split3(x):
    hi = x.astype(BF16)
    rest = x - hi.astype(F32)
    mid = rest.astype(BF16)
    low = (rest - mid.astype(F32)).astype(BF16)
    return jnp.concatenate([hi, mid, low], axis=0)


def pick(matrix, rows):
    wide = jnp.concatenate([matrix, matrix, matrix], axis=1).astype(BF16)
    return jnp.dot(wide, split3(rows), preferred_element_type=F32)


def vmem():
    return pl.BlockSpec(memory_space=pltpu.VMEM)


def smem():
    return pl.BlockSpec(memory_space=pltpu.SMEM)


def f32(*shape):
    return jax.ShapeDtypeStruct(shape, F32)


def params(mib=4):
    return pltpu.CompilerParams(vmem_limit_bytes=mib * MIB)


def pack_kernel(layout, spacing, lists_ref, params_ref, out_ref):
    shared_rows, rows, pieces = layout
    band, epoch = lax.axis_index("band"), lax.axis_index("epoch")
    for b in range(BANDS):
        for q in range(len(pieces)):

            @pl.when((band == b) & (epoch == q))
            def _():
                for p, entry in enumerate(pieces[q]):
                    if entry is None:
                        out_ref[p] = jnp.zeros(out_ref.shape[1:], F32)
                        continue
                    row, position = row_of(b, entry)
                    value = params_ref[row]
                    if position is not None:
                        value = spacing * params_ref[position] + value
                    out_ref[p] = value

    tiles, slots = lists_ref.shape
    lane = lax.broadcasted_iota(jnp.int32, (8, 128), 1)
    ids = jnp.zeros((8, 128), jnp.int32)
    for t in range(tiles):
        for s in range(slots):
            ids = jnp.where(lane == t * slots + s, lists_ref[t, s], ids)
    out_ref[rows] = ids.astype(F32)


def select_kernel(layout, wide, *refs):
    shared_rows, rows, pieces = layout
    got, (out_ref, match_ref, place_ref) = refs[:-3], refs[-3:]
    owners = len(got)
    blocks = got[0].shape[1]
    me = lax.axis_index("tile")
    own_line = got[0][rows, :1, :]
    own_column = jnp.broadcast_to(own_line, (128, 128)).T[:wide]

    shape = (wide, owners * blocks)
    lane = lax.broadcasted_iota(jnp.int32, shape, 1)
    held = lax.rem(me - lane // blocks + owners, owners) * blocks + lane % blocks
    choose = (own_column[:, : owners * blocks] == held.astype(F32)).astype(F32)
    for p in range(rows):
        out_ref[p] = pick(choose, jnp.concatenate([ref[p] for ref in got], axis=0))

    lists = jnp.concatenate([ref[rows, :1, :wide] for ref in got], axis=1)
    match_ref[:wide] = (own_column[:, :1] == lists).astype(F32)
    own_blocks = me * blocks + lax.broadcasted_iota(jnp.int32, (blocks, owners * wide), 0)
    match_ref[wide:] = (own_blocks.astype(F32) == lists).astype(F32)
    line = lax.broadcasted_iota(jnp.int32, (owners * blocks, wide), 0)
    target = lax.rem(me + line // blocks, owners) * blocks + line % blocks
    place_ref[...] = (own_line[:, :wide] == target.astype(F32)).astype(F32)


def put_together(layout, band, epoch, ins, half, other, shared, amps):
    shared_rows, rows, pieces = layout
    epochs = len(pieces)
    for k in range(epochs):
        q = lax.rem(epoch - k + epochs, epochs)
        half[q] = ins[k][...]
        other[q] = ins[epochs][k]
    for q, piece in enumerate(pieces):
        for p, entry in enumerate(piece):
            if entry is None:
                continue
            kind, i = entry
            if kind == "s":
                shared[band, i] = half[q, p]
                shared[1 - band, i] = other[q, p]
            else:
                amps[i] = half[q, p]


def step_kernel(layout, later, counts_ref, offsets_ref, psf_ref, data_ref, weight_ref, *refs):
    shared_rows, rows, pieces = layout
    epochs = len(pieces)
    arrays = epochs + 1
    taken = arrays * (2 if later else 1)
    ins, refs = refs[:taken], refs[taken:]
    outs, refs = refs[:arrays], refs[arrays:]
    shared, amps, derived, prof_x, prof_y, pieces_x, pieces_y, image, sums, half, other = refs[:11]
    band, epoch = lax.axis_index("band"), lax.axis_index("epoch")
    tiles = data_ref.shape[0]
    pixels = data_ref.shape[-1]
    wide = shared.shape[2]
    slots = wide // tiles
    spacing = pixels / 8.0

    put_together(layout, band, epoch, ins[:arrays], half, other, shared, amps)

    def row(k, c):
        r = k * COMPS + c
        return r // HALF, r % HALF

    if later:
        moved, moved_amps = refs[11:]
        put_together(layout, band, epoch, ins[arrays:], half, other, moved, moved_amps)
        for k in range(4):
            shift = 0.0
            if k < 2:
                shift = functools.reduce(lambda a, b: a + b, [moved[row(k, c)] for c in range(COMPS)])
                shift = shift * (spacing * spacing * POSITION_RATE)
            for c in range(COMPS):
                shared[row(k, c)] = shared[row(k, c)] - STEP * (moved[row(k, c)] + shift)
        for c in range(COMPS):
            amps[c] = amps[c] - STEP * moved_amps[c]

    psf = psf_ref[0, 0]
    line_of = lax.broadcasted_iota(jnp.int32, (wide, 128), 0)
    live = jnp.zeros((wide, 128), jnp.bool_)
    for t in range(tiles):
        live = live | ((line_of >= t * slots) & (line_of < t * slots + counts_ref[t]))
    off_x = off_y = jnp.zeros((wide, 128), jnp.int32)
    for t in range(tiles):
        for s in range(slots):
            at = line_of == t * slots + s
            off_x = jnp.where(at, offsets_ref[t, 0, s], off_x)
            off_y = jnp.where(at, offsets_ref[t, 1, s], off_y)
    off_x, off_y = off_x.astype(F32), off_y.astype(F32)
    for c in range(COMPS):
        lw, an = shared[row(2, c)], shared[row(3, c)]
        derived[0, c] = shared[row(0, c)] + off_x
        derived[1, c] = shared[row(1, c)] + off_y
        derived[2, c] = (-0.5 * LOG2E) / (jnp.exp(2.0 * (lw + an)) + psf * psf)
        derived[3, c] = (-0.5 * LOG2E) / (jnp.exp(2.0 * (lw - an)) + psf * psf)
        derived[4, c] = jnp.where(live, amps[c], 0.0)
        derived[5, c] = derived[4, c] * SPLIT_SCALE
    sums[...] = jnp.zeros_like(sums)

    grid = lax.broadcasted_iota(jnp.int32, (pixels, 128), 0).astype(F32)

    def cut(x, large):
        hi = (x + large) - large
        return jnp.concatenate([hi, x - hi], axis=0)

    def stack(x):
        hi = x.astype(BF16).astype(F32)
        return jnp.concatenate([hi, hi, x - hi], axis=1)

    def times(left, right):
        return jnp.dot(left, jnp.concatenate([right, right[:pixels]], axis=0), preferred_element_type=F32)

    middle = pixels // 2
    inner = lax.broadcasted_iota(jnp.int32, (8, 128), 0).astype(F32)

    def running(groups):
        sum_0 = sum_1 = sum_2 = groups[0]
        for group in groups[1:]:
            sum_0 = sum_0 + group
            sum_1 = sum_1 + sum_0
            sum_2 = sum_2 + sum_1
        return sum_0, sum_1, sum_2

    def moments(x):
        groups = [x[r : r + 8] for r in range(0, pixels, 8)]
        high = running(groups[len(groups) // 2 :][::-1])
        low = running(groups[: len(groups) // 2])
        m0 = high[0] + low[0]
        m1 = high[1] - high[0] - low[1]
        m2 = 2.0 * (high[2] + low[2]) - 2.0 * high[1] - (high[1] - high[0]) - low[1]
        first = inner * m0 + 8.0 * m1
        second = inner * (first + 8.0 * m1) + 64.0 * m2
        return [jnp.sum(m, axis=0, keepdims=True) for m in (m0, first, second)]

    def line(index, c, s):
        return derived[index, c, pl.ds(s, 1), :]

    together = 2
    for t in range(tiles):
        trips = (counts_ref[t] + together - 1) // together
        image[...] = jnp.zeros_like(image)

        def render(i, carry):
            for u in range(together):
                s = i * together + u
                g = t * slots + s
                for c in range(COMPS):
                    d = grid - line(0, c, g)
                    e = jnp.exp2(d * d * line(2, c, g))
                    prof_x[s * COMPS + c] = e
                    pieces_x[s, :, c * 128 : (c + 1) * 128] = cut(e, SPLIT_UNIT)
                    d = grid - line(1, c, g)
                    e = jnp.exp2(d * d * line(3, c, g))
                    prof_y[s * COMPS + c] = e
                    pieces_y[s, :, c * 128 : (c + 1) * 128] = cut(e * line(4, c, g), line(5, c, g))
                image[...] += lax.dot_general(
                    pieces_x[s], pieces_y[s], (((1,), (1,)), ((), ())), preferred_element_type=F32
                )
            return carry

        lax.fori_loop(0, trips, render, 0)

        model = (image[:pixels, :pixels] + image[pixels:, pixels:]) + (
            image[:pixels, pixels:] + image[pixels:, :pixels]
        )
        cotangent = weight_ref[t, 0, 0] * (model - data_ref[t, 0, 0])
        left_x, left_y = stack(cotangent), stack(cotangent.T)

        def pull(i, carry):
            for u in range(together):
                s = i * together + u
                g = t * slots + s
                for first in range(0, COMPS, 2):
                    here = min(2, COMPS - first)
                    span = pl.ds(first * 128, 128 * here)
                    by_x = times(left_x, pieces_y[s, :, span])
                    by_y = times(left_y, pieces_x[s, :, span])
                    for n in range(here):
                        c = first + n
                        at = slice(n * 128, (n + 1) * 128)
                        for k, value in enumerate(moments(prof_x[s * COMPS + c] * by_x[:, at])):
                            sums[k, c, pl.ds(g, 1), :] = value
                        for k, value in enumerate(moments(prof_y[s * COMPS + c] * by_y[:, at])):
                            sums[3 + k, c, pl.ds(g, 1), :] = value
            return carry

        lax.fori_loop(0, trips, pull, 0)

    def keep(x):
        return jnp.where(live, x, 0.0)

    for c in range(COMPS):
        lw, an = shared[row(2, c)], shared[row(3, c)]
        wide_x, wide_y = jnp.exp(2.0 * (lw + an)), jnp.exp(2.0 * (lw - an))
        inv_x, inv_y = 1.0 / (wide_x + psf * psf), 1.0 / (wide_y + psf * psf)
        amp = amps[c]
        shift_x, shift_y = middle - derived[0, c], middle - derived[1, c]
        first_x = sums[1, c] + shift_x * sums[0, c]
        first_y = sums[4, c] + shift_y * sums[3, c]
        second_x = sums[2, c] + shift_x * (sums[1, c] + first_x)
        second_y = sums[5, c] + shift_y * (sums[4, c] + first_y)
        var_x = keep(second_x * inv_x * (inv_x * wide_x))
        var_y = keep(amp * second_y * inv_y * (inv_y * wide_y))
        shared[row(0, c)] = keep(first_x * inv_x)
        shared[row(1, c)] = keep(amp * first_y * inv_y)
        shared[row(2, c)] = var_x + var_y
        shared[row(3, c)] = var_x - var_y
        amps[c] = keep(sums[3, c])
    none = jnp.zeros((wide, 128), F32)
    for q, piece in enumerate(pieces):
        for p, entry in enumerate(piece):
            is_shared = entry is not None and entry[0] == "s"
            if is_shared:
                half[q, p] = shared[band, entry[1]]
            else:
                half[q, p] = none if entry is None else amps[entry[1]]
            if p < shared_rows:
                other[q, p] = shared[1 - band, entry[1]] if is_shared else none
    for k in range(epochs):
        outs[k][...] = half[lax.rem(epoch + k, epochs)]
        outs[epochs][k] = other[lax.rem(epoch + k, epochs)]


def step_gradient(layout, counts, offsets, psf, data, weight, slot_rows, moved):
    shared_rows, rows, pieces = layout
    epochs = len(pieces)
    later = moved is not None
    tiles, _, slots = offsets.shape
    pixels = data.shape[-1]
    wide = tiles * slots
    shapes = [(rows, wide, 128)] * epochs + [(epochs, shared_rows, wide, 128)]
    ins = slot_rows + (moved or [])
    together = [pltpu.VMEM((BANDS, HALF, wide, 128), F32), pltpu.VMEM((COMPS, wide, 128), F32)]
    return pl.pallas_call(
        functools.partial(step_kernel, layout, later),
        out_shape=[f32(*s) for s in shapes],
        in_specs=[smem()] * 3 + [vmem()] * (2 + len(ins)),
        out_specs=[vmem()] * len(shapes),
        scratch_shapes=together
        + [
            pltpu.VMEM((6, COMPS, wide, 128), F32),
            pltpu.VMEM((slots * COMPS, pixels, 128), F32),
            pltpu.VMEM((slots * COMPS, pixels, 128), F32),
            pltpu.VMEM((slots, 2 * pixels, COMPS * 128), F32),
            pltpu.VMEM((slots, 2 * pixels, COMPS * 128), F32),
            pltpu.VMEM((2 * pixels, 2 * pixels), F32),
            pltpu.VMEM((6, COMPS, wide, 128), F32),
            pltpu.VMEM((epochs, rows, wide, 128), F32),
            pltpu.VMEM((epochs, shared_rows, wide, 128), F32),
        ]
        + (together if later else []),
        compiler_params=params(40),
        name="later_step" if later else "first_step",
    )(counts, offsets, psf, data, weight, *ins)


def combine_kernel(layout, match_ref, *refs):
    shared_rows, rows, pieces = layout
    got, (out_ref, own_ref) = refs[:-2], refs[-2:]
    wide = out_ref.shape[1]
    match = match_ref[...]
    for p in range(rows):
        both = pick(match, jnp.concatenate([ref[p] for ref in got], axis=0))
        out_ref[p] = both[:wide]
        own_ref[p] = both[wide:]


def dense_kernel(rows, place_ref, grads, *outs):
    blocks = outs[0].shape[1]
    place = place_ref[...]
    for p in range(rows):
        dense = pick(place, grads[p])
        for k, out in enumerate(outs):
            out[p] = dense[k * blocks : (k + 1) * blocks]


def final_kernel(layout, spacing, params_ref, *refs):
    shared_rows, rows, pieces = layout
    epochs = len(pieces)
    ins, (out_ref, held) = refs[: epochs + 1], refs[epochs + 1 :]
    band, epoch = lax.axis_index("band"), lax.axis_index("epoch")
    for k in range(epochs):
        q = lax.rem(epoch - k + epochs, epochs)
        held[band, q] = ins[k][...]
        held[1 - band, q] = ins[epochs][k]
    shift = [0.0, 0.0]
    for b in range(BANDS):
        for q, piece in enumerate(pieces):
            for p, entry in enumerate(piece):
                if entry is None:
                    continue
                row, position = row_of(b, entry)
                grad = held[b, q, p]
                out_ref[row] = params_ref[row] - STEP * grad
                if position is not None:
                    shift[position] = shift[position] + grad
    for k in range(2):
        out_ref[k] = params_ref[k] - (STEP * POSITION_RATE * spacing) * shift[k]


def shards(source_params, pixel_data, pixel_weight, psf_width, block_lists, block_counts, block_offsets):
    owners, epochs = lax.axis_size("tile"), lax.axis_size("epoch")
    blocks, param_rows, sources = source_params.shape
    tiles, slots = block_lists.shape
    wide = tiles * slots
    spacing = pixel_data.shape[-1] / 8.0
    layout = quarter_layout(epochs)
    shared_rows, rows, pieces = layout

    def to_epoch(x, k):
        return lax.ppermute(x, "epoch", [(i, (i + k) % epochs) for i in range(epochs)])

    def to_other_band(x):
        return lax.ppermute(x, "band", [(b, 1 - b) for b in range(BANDS)])

    def round_tiles(arrays):
        return [arrays[0]] + [
            lax.ppermute(arrays[k], "tile", [(i, (i + k) % owners) for i in range(owners)])
            for k in range(1, owners)
        ]

    def spread(piece, count):
        got = [piece] + [to_epoch(piece, k) for k in range(1, epochs)]
        return got + [to_other_band(jnp.stack([x[:count] for x in got]))]

    def summed(parts):
        far = to_other_band(parts[epochs])
        missing = ((0, rows - shared_rows), (0, 0), (0, 0))
        halves = [parts[k] + jnp.pad(far[k], missing) for k in range(epochs)]
        return functools.reduce(
            lambda a, b: a + b, [to_epoch(halves[k], k) for k in range(1, epochs)], halves[0]
        )

    by_row = jnp.transpose(source_params, (1, 0, 2))
    offsets = jnp.transpose(block_offsets, (0, 2, 1))
    packed = pl.pallas_call(
        functools.partial(pack_kernel, layout, spacing),
        out_shape=f32(rows + 1, blocks, sources),
        in_specs=[smem(), vmem()],
        out_specs=vmem(),
        compiler_params=params(),
        name="pack",
    )(block_lists, by_row)
    got = round_tiles([packed] * owners)
    slot_piece, match, place = pl.pallas_call(
        functools.partial(select_kernel, layout, wide),
        out_shape=[
            f32(rows, wide, sources),
            f32(wide + blocks, owners * wide),
            f32(owners * blocks, wide),
        ],
        in_specs=[vmem()] * owners,
        out_specs=[vmem()] * 3,
        compiler_params=params(),
        name="select",
    )(*got)
    slot_rows = spread(slot_piece, shared_rows)

    def gradient(moved):
        parts = step_gradient(
            layout, block_counts, offsets, psf_width, pixel_data, pixel_weight, slot_rows, moved
        )
        return summed(parts)

    got = round_tiles([gradient(None)] * owners)
    slot_piece, own_first = pl.pallas_call(
        functools.partial(combine_kernel, layout),
        out_shape=[
            f32(rows, wide, sources),
            f32(rows, blocks, sources),
        ],
        in_specs=[vmem()] * (1 + owners),
        out_specs=[vmem()] * 2,
        compiler_params=params(),
        name="combine",
    )(match, *got)

    dense = pl.pallas_call(
        functools.partial(dense_kernel, rows),
        out_shape=[f32(rows, blocks, sources)] * owners,
        in_specs=[vmem()] * 2,
        out_specs=[vmem()] * owners,
        compiler_params=params(),
        name="dense",
    )(place, gradient(spread(slot_piece, shared_rows)))
    own = functools.reduce(lambda a, b: a + b, round_tiles(dense), own_first)
    whole = pl.pallas_call(
        functools.partial(final_kernel, layout, spacing),
        out_shape=f32(param_rows, blocks, sources),
        in_specs=[vmem()] * (2 + epochs),
        out_specs=vmem(),
        scratch_shapes=[pltpu.VMEM((BANDS, epochs, rows, blocks, sources), F32)],
        compiler_params=params(),
        name="final",
    )(by_row, *spread(own, rows))
    return jnp.transpose(whole, (1, 0, 2))


def solution(mesh):
    return jax.shard_map(
        shards,
        mesh=mesh,
        in_specs=(
            P(("region", "tile"), None, None),
            P(("region", "tile"), "epoch", "band", None, None),
            P(("region", "tile"), "epoch", "band", None, None),
            P(("region", "epoch"), "band"),
            P(("region", "tile"), None),
            P(("region", "tile")),
            P(("region", "tile"), None, None),
        ),
        out_specs=P(("region", "tile"), None, None),
        check_vma=False,
    )
```

```python
import functools
import math

import jax
import jax.numpy as jnp
from jax import lax
from jax.experimental import pallas as pl
from jax.experimental.pallas import tpu as pltpu
from jax.sharding import PartitionSpec as P

ITERS = 2
STEP = 0.005
POSITION_RATE = 1.0 / 64.0
COMPS = 7
BANDS = 2
SHARED = 4 * COMPS
HALF = SHARED // BANDS
SPLIT_UNIT = 49152.0
SPLIT_SCALE = 65536.0
LOG2E = math.log2(math.e)
F32 = jnp.float32
BF16 = jnp.bfloat16
MIB = 1024 * 1024


def quarter_layout(epochs):
    shared_rows = -(-HALF // epochs)
    rows = -(-(HALF + COMPS) // epochs)
    pieces, amp = [], 0
    for q in range(epochs):
        piece = [("s", i) for i in range(q * shared_rows, min((q + 1) * shared_rows, HALF))]
        while len(piece) < rows and amp < COMPS:
            piece.append(("a", amp))
            amp += 1
        pieces.append(piece + [None] * (rows - len(piece)))
    return shared_rows, rows, pieces


def row_of(band, entry):
    kind, i = entry
    if kind == "a":
        return 2 + 6 * i + 4 + band, None
    k, c = divmod(HALF * band + i, COMPS)
    return 2 + 6 * c + k, (k if k < 2 else None)


def split3(x):
    hi = x.astype(BF16)
    rest = x - hi.astype(F32)
    mid = rest.astype(BF16)
    low = (rest - mid.astype(F32)).astype(BF16)
    return jnp.concatenate([hi, mid, low], axis=0)


def pick(matrix, rows):
    wide = jnp.concatenate([matrix, matrix, matrix], axis=1).astype(BF16)
    return jnp.dot(wide, split3(rows), preferred_element_type=F32)


def vmem():
    return pl.BlockSpec(memory_space=pltpu.VMEM)


def smem():
    return pl.BlockSpec(memory_space=pltpu.SMEM)


def f32(*shape):
    return jax.ShapeDtypeStruct(shape, F32)


def params(mib=4):
    return pltpu.CompilerParams(vmem_limit_bytes=mib * MIB)


def half_rows():
    return [("s", i) for i in range(HALF)] + [("a", j) for j in range(COMPS)]


def pack_kernel(spacing, lists_ref, params_ref, out_ref):
    band = lax.axis_index("band")
    for b in range(BANDS):

        @pl.when(band == b)
        def _():
            for p, entry in enumerate(half_rows()):
                row, position = row_of(b, entry)
                value = params_ref[row]
                if position is not None:
                    value = spacing * params_ref[position] + value
                out_ref[p] = value

    tiles, slots = lists_ref.shape
    lane = lax.broadcasted_iota(jnp.int32, (8, 128), 1)
    ids = jnp.zeros((8, 128), jnp.int32)
    for t in range(tiles):
        for s in range(slots):
            ids = jnp.where(lane == t * slots + s, lists_ref[t, s], ids)
    out_ref[HALF + COMPS] = ids.astype(F32)


def select_kernel(wide, *refs):
    rows = HALF + COMPS
    got, (out_ref, short_ref, match_ref, place_ref) = refs[:-4], refs[-4:]
    owners = len(got)
    blocks = got[0].shape[1]
    me = lax.axis_index("tile")
    own_line = got[0][rows, :1, :]
    own_column = jnp.broadcast_to(own_line, (128, 128)).T[:wide]

    shape = (wide, owners * blocks)
    lane = lax.broadcasted_iota(jnp.int32, shape, 1)
    held = lax.rem(me - lane // blocks + owners, owners) * blocks + lane % blocks
    choose = (own_column[:, : owners * blocks] == held.astype(F32)).astype(F32)
    for p in range(rows):
        chosen = pick(choose, jnp.concatenate([ref[p] for ref in got], axis=0))
        out_ref[p] = chosen
        if p < HALF:
            short_ref[p] = chosen

    lists = jnp.concatenate([ref[rows, :1, :wide] for ref in got], axis=1)
    match_ref[:wide] = (own_column[:, :1] == lists).astype(F32)
    own_blocks = me * blocks + lax.broadcasted_iota(jnp.int32, (blocks, owners * wide), 0)
    match_ref[wide:] = (own_blocks.astype(F32) == lists).astype(F32)
    line = lax.broadcasted_iota(jnp.int32, (owners * blocks, wide), 0)
    target = lax.rem(me + line // blocks, owners) * blocks + line % blocks
    place_ref[...] = (own_line[:, :wide] == target.astype(F32)).astype(F32)


def put_together(layout, band, epoch, ins, half, other, shared, amps):
    shared_rows, rows, pieces = layout
    epochs = len(pieces)
    for k in range(epochs):
        q = lax.rem(epoch - k + epochs, epochs)
        half[q] = ins[k][...]
        other[q] = ins[epochs + k][...]
    for q, piece in enumerate(pieces):
        for p, entry in enumerate(piece):
            if entry is None:
                continue
            kind, i = entry
            if kind == "s":
                shared[band, i] = half[q, p]
                shared[1 - band, i] = other[q, p]
            else:
                amps[i] = half[q, p]


def step_kernel(layout, later, counts_ref, offsets_ref, psf_ref, data_ref, weight_ref, *refs):
    shared_rows, rows, pieces = layout
    epochs = len(pieces)
    (mine, others), refs = refs[:2], refs[2:]
    taken = 2 * epochs if later else 0
    ins, refs = refs[:taken], refs[taken:]
    outs, refs = refs[: 2 * epochs], refs[2 * epochs :]
    shared, amps, derived, prof_x, prof_y, pieces_x, pieces_y, image, sums, half, other = refs[:11]
    band, epoch = lax.axis_index("band"), lax.axis_index("epoch")
    tiles = data_ref.shape[0]
    pixels = data_ref.shape[-1]
    wide = shared.shape[2]
    slots = wide // tiles
    spacing = pixels / 8.0

    shared[band] = mine[:HALF]
    shared[1 - band] = others[...]
    amps[...] = mine[HALF:]

    def row(k, c):
        r = k * COMPS + c
        return r // HALF, r % HALF

    if later:
        moved, moved_amps = refs[11:]
        put_together(layout, band, epoch, ins, half, other, moved, moved_amps)
        for k in range(4):
            shift = 0.0
            if k < 2:
                shift = functools.reduce(lambda a, b: a + b, [moved[row(k, c)] for c in range(COMPS)])
                shift = shift * (spacing * spacing * POSITION_RATE)
            for c in range(COMPS):
                shared[row(k, c)] = shared[row(k, c)] - STEP * (moved[row(k, c)] + shift)
        for c in range(COMPS):
            amps[c] = amps[c] - STEP * moved_amps[c]

    psf = psf_ref[0, 0]
    line_of = lax.broadcasted_iota(jnp.int32, (wide, 128), 0)
    live = jnp.zeros((wide, 128), jnp.bool_)
    for t in range(tiles):
        live = live | ((line_of >= t * slots) & (line_of < t * slots + counts_ref[t]))
    off_x = off_y = jnp.zeros((wide, 128), jnp.int32)
    for t in range(tiles):
        for s in range(slots):
            at = line_of == t * slots + s
            off_x = jnp.where(at, offsets_ref[t, 0, s], off_x)
            off_y = jnp.where(at, offsets_ref[t, 1, s], off_y)
    off_x, off_y = off_x.astype(F32), off_y.astype(F32)
    for c in range(COMPS):
        lw, an = shared[row(2, c)], shared[row(3, c)]
        derived[0, c] = shared[row(0, c)] + off_x
        derived[1, c] = shared[row(1, c)] + off_y
        derived[2, c] = (-0.5 * LOG2E) / (jnp.exp(2.0 * (lw + an)) + psf * psf)
        derived[3, c] = (-0.5 * LOG2E) / (jnp.exp(2.0 * (lw - an)) + psf * psf)
        derived[4, c] = jnp.where(live, amps[c], 0.0)
        derived[5, c] = derived[4, c] * SPLIT_SCALE
    sums[...] = jnp.zeros_like(sums)

    grid = lax.broadcasted_iota(jnp.int32, (pixels, 128), 0).astype(F32)

    def cut(x, large):
        hi = (x + large) - large
        return jnp.concatenate([hi, x - hi], axis=0)

    def stack(x):
        hi = x.astype(BF16).astype(F32)
        return jnp.concatenate([hi, hi, x - hi], axis=1)

    def times(left, right):
        return jnp.dot(left, jnp.concatenate([right, right[:pixels]], axis=0), preferred_element_type=F32)

    middle = pixels // 2
    inner = lax.broadcasted_iota(jnp.int32, (8, 128), 0).astype(F32)

    def running(groups):
        sum_0 = sum_1 = sum_2 = groups[0]
        for group in groups[1:]:
            sum_0 = sum_0 + group
            sum_1 = sum_1 + sum_0
            sum_2 = sum_2 + sum_1
        return sum_0, sum_1, sum_2

    def moments(x):
        groups = [x[r : r + 8] for r in range(0, pixels, 8)]
        high = running(groups[len(groups) // 2 :][::-1])
        low = running(groups[: len(groups) // 2])
        m0 = high[0] + low[0]
        m1 = high[1] - high[0] - low[1]
        m2 = 2.0 * (high[2] + low[2]) - 2.0 * high[1] - (high[1] - high[0]) - low[1]
        first = inner * m0 + 8.0 * m1
        second = inner * (first + 8.0 * m1) + 64.0 * m2
        return [jnp.sum(m, axis=0, keepdims=True) for m in (m0, first, second)]

    def line(index, c, s):
        return derived[index, c, pl.ds(s, 1), :]

    together = 2
    for t in range(tiles):
        trips = (counts_ref[t] + together - 1) // together
        image[...] = jnp.zeros_like(image)

        def render(i, carry):
            for u in range(together):
                s = i * together + u
                g = t * slots + s
                for c in range(COMPS):
                    d = grid - line(0, c, g)
                    e = jnp.exp2(d * d * line(2, c, g))
                    prof_x[s * COMPS + c] = e
                    pieces_x[s, :, c * 128 : (c + 1) * 128] = cut(e, SPLIT_UNIT)
                    d = grid - line(1, c, g)
                    e = jnp.exp2(d * d * line(3, c, g))
                    prof_y[s * COMPS + c] = e
                    pieces_y[s, :, c * 128 : (c + 1) * 128] = cut(e * line(4, c, g), line(5, c, g))
                image[...] += lax.dot_general(
                    pieces_x[s], pieces_y[s], (((1,), (1,)), ((), ())), preferred_element_type=F32
                )
            return carry

        lax.fori_loop(0, trips, render, 0)

        model = (image[:pixels, :pixels] + image[pixels:, pixels:]) + (
            image[:pixels, pixels:] + image[pixels:, :pixels]
        )
        cotangent = weight_ref[t, 0, 0] * (model - data_ref[t, 0, 0])
        left_x, left_y = stack(cotangent), stack(cotangent.T)

        def pull(i, carry):
            for u in range(together):
                s = i * together + u
                g = t * slots + s
                for first in range(0, COMPS, 2):
                    here = min(2, COMPS - first)
                    span = pl.ds(first * 128, 128 * here)
                    by_x = times(left_x, pieces_y[s, :, span])
                    by_y = times(left_y, pieces_x[s, :, span])
                    for n in range(here):
                        c = first + n
                        at = slice(n * 128, (n + 1) * 128)
                        for k, value in enumerate(moments(prof_x[s * COMPS + c] * by_x[:, at])):
                            sums[k, c, pl.ds(g, 1), :] = value
                        for k, value in enumerate(moments(prof_y[s * COMPS + c] * by_y[:, at])):
                            sums[3 + k, c, pl.ds(g, 1), :] = value
            return carry

        lax.fori_loop(0, trips, pull, 0)

    def keep(x):
        return jnp.where(live, x, 0.0)

    for c in range(COMPS):
        lw, an = shared[row(2, c)], shared[row(3, c)]
        wide_x, wide_y = jnp.exp(2.0 * (lw + an)), jnp.exp(2.0 * (lw - an))
        inv_x, inv_y = 1.0 / (wide_x + psf * psf), 1.0 / (wide_y + psf * psf)
        amp = amps[c]
        shift_x, shift_y = middle - derived[0, c], middle - derived[1, c]
        first_x = sums[1, c] + shift_x * sums[0, c]
        first_y = sums[4, c] + shift_y * sums[3, c]
        second_x = sums[2, c] + shift_x * (sums[1, c] + first_x)
        second_y = sums[5, c] + shift_y * (sums[4, c] + first_y)
        var_x = keep(second_x * inv_x * (inv_x * wide_x))
        var_y = keep(amp * second_y * inv_y * (inv_y * wide_y))
        shared[row(0, c)] = keep(first_x * inv_x)
        shared[row(1, c)] = keep(amp * first_y * inv_y)
        shared[row(2, c)] = var_x + var_y
        shared[row(3, c)] = var_x - var_y
        amps[c] = keep(sums[3, c])
    none = jnp.zeros((wide, 128), F32)
    for q, piece in enumerate(pieces):
        for p, entry in enumerate(piece):
            is_shared = entry is not None and entry[0] == "s"
            if is_shared:
                half[q, p] = shared[band, entry[1]]
            else:
                half[q, p] = none if entry is None else amps[entry[1]]
            if p < shared_rows:
                other[q, p] = shared[1 - band, entry[1]] if is_shared else none
    for k in range(epochs):
        outs[k][...] = half[lax.rem(epoch + k, epochs)]
        outs[epochs + k][...] = other[lax.rem(epoch + k, epochs)]


def step_gradient(layout, counts, offsets, psf, data, weight, slot_rows, moved):
    shared_rows, rows, pieces = layout
    epochs = len(pieces)
    later = moved is not None
    tiles, _, slots = offsets.shape
    pixels = data.shape[-1]
    wide = tiles * slots
    shapes = [(rows, wide, 128)] * epochs + [(shared_rows, wide, 128)] * epochs
    ins = slot_rows + (moved or [])
    together = [pltpu.VMEM((BANDS, HALF, wide, 128), F32), pltpu.VMEM((COMPS, wide, 128), F32)]
    return pl.pallas_call(
        functools.partial(step_kernel, layout, later),
        out_shape=[f32(*s) for s in shapes],
        in_specs=[smem()] * 3 + [vmem()] * (2 + len(ins)),
        out_specs=[vmem()] * len(shapes),
        scratch_shapes=together
        + [
            pltpu.VMEM((6, COMPS, wide, 128), F32),
            pltpu.VMEM((slots * COMPS, pixels, 128), F32),
            pltpu.VMEM((slots * COMPS, pixels, 128), F32),
            pltpu.VMEM((slots, 2 * pixels, COMPS * 128), F32),
            pltpu.VMEM((slots, 2 * pixels, COMPS * 128), F32),
            pltpu.VMEM((2 * pixels, 2 * pixels), F32),
            pltpu.VMEM((6, COMPS, wide, 128), F32),
            pltpu.VMEM((epochs, rows, wide, 128), F32),
            pltpu.VMEM((epochs, shared_rows, wide, 128), F32),
        ]
        + (together if later else []),
        compiler_params=params(40),
        name="later_step" if later else "first_step",
    )(counts, offsets, psf, data, weight, *ins)


def combine_kernel(layout, match_ref, *refs):
    shared_rows, rows, pieces = layout
    got, (out_ref, short_ref, own_ref) = refs[:-3], refs[-3:]
    wide = out_ref.shape[1]
    match = match_ref[...]
    for p in range(rows):
        both = pick(match, jnp.concatenate([ref[p] for ref in got], axis=0))
        out_ref[p] = both[:wide]
        if p < shared_rows:
            short_ref[p] = both[:wide]
        own_ref[p] = both[wide:]


def dense_kernel(rows, place_ref, grads, *outs):
    blocks = outs[0].shape[1]
    place = place_ref[...]
    for p in range(rows):
        dense = pick(place, grads[p])
        for k, out in enumerate(outs):
            out[p] = dense[k * blocks : (k + 1) * blocks]


def final_kernel(layout, spacing, params_ref, *refs):
    shared_rows, rows, pieces = layout
    epochs = len(pieces)
    ins, (out_ref, held) = refs[: 2 * epochs], refs[2 * epochs :]
    band, epoch = lax.axis_index("band"), lax.axis_index("epoch")
    for k in range(epochs):
        q = lax.rem(epoch - k + epochs, epochs)
        held[band, q] = ins[k][...]
        held[1 - band, q] = ins[epochs + k][...]
    shift = [0.0, 0.0]
    for b in range(BANDS):
        for q, piece in enumerate(pieces):
            for p, entry in enumerate(piece):
                if entry is None:
                    continue
                row, position = row_of(b, entry)
                grad = held[b, q, p]
                out_ref[row] = params_ref[row] - STEP * grad
                if position is not None:
                    shift[position] = shift[position] + grad
    for k in range(2):
        out_ref[k] = params_ref[k] - (STEP * POSITION_RATE * spacing) * shift[k]


def shards(source_params, pixel_data, pixel_weight, psf_width, block_lists, block_counts, block_offsets):
    owners, epochs = lax.axis_size("tile"), lax.axis_size("epoch")
    blocks, param_rows, sources = source_params.shape
    tiles, slots = block_lists.shape
    wide = tiles * slots
    spacing = pixel_data.shape[-1] / 8.0
    layout = quarter_layout(epochs)
    shared_rows, rows, pieces = layout

    def to_peers(same, other):
        kept = [same[0]]
        for k in range(1, epochs):
            kept.append(lax.ppermute(same[k], "epoch", [(i, (i + k) % epochs) for i in range(epochs)]))
        for k in range(epochs):
            pairs = [
                (i * BANDS + b, (i + k) % epochs * BANDS + 1 - b)
                for i in range(epochs)
                for b in range(BANDS)
            ]
            kept.append(lax.ppermute(other[k], ("epoch", "band"), pairs))
        return kept

    def round_tiles(arrays):
        return [arrays[0]] + [
            lax.ppermute(arrays[k], "tile", [(i, (i + k) % owners) for i in range(owners)])
            for k in range(1, owners)
        ]

    def spread(piece, other):
        return to_peers([piece] * epochs, [other] * epochs)

    def summed(parts):
        near = functools.reduce(lambda a, b: a + b, parts[:epochs])
        far = functools.reduce(lambda a, b: a + b, parts[epochs:])
        return near + jnp.pad(far, ((0, rows - shared_rows), (0, 0), (0, 0)))

    by_row = jnp.transpose(source_params, (1, 0, 2))
    offsets = jnp.transpose(block_offsets, (0, 2, 1))
    packed = pl.pallas_call(
        functools.partial(pack_kernel, spacing),
        out_shape=f32(HALF + COMPS + 1, blocks, sources),
        in_specs=[smem(), vmem()],
        out_specs=vmem(),
        compiler_params=params(),
        name="pack",
    )(block_lists, by_row)
    got = round_tiles([packed] * owners)
    slot_half, slot_short, match, place = pl.pallas_call(
        functools.partial(select_kernel, wide),
        out_shape=[
            f32(HALF + COMPS, wide, sources),
            f32(HALF, wide, sources),
            f32(wide + blocks, owners * wide),
            f32(owners * blocks, wide),
        ],
        in_specs=[vmem()] * owners,
        out_specs=[vmem()] * 4,
        compiler_params=params(),
        name="select",
    )(*got)
    slot_rows = [slot_half, lax.ppermute(slot_short, "band", [(b, 1 - b) for b in range(BANDS)])]

    def gradient(moved):
        parts = step_gradient(
            layout, block_counts, offsets, psf_width, pixel_data, pixel_weight, slot_rows, moved
        )
        return summed(to_peers(parts[:epochs], parts[epochs:]))

    got = round_tiles([gradient(None)] * owners)
    slot_piece, slot_short, own_first = pl.pallas_call(
        functools.partial(combine_kernel, layout),
        out_shape=[
            f32(rows, wide, sources),
            f32(shared_rows, wide, sources),
            f32(rows, blocks, sources),
        ],
        in_specs=[vmem()] * (1 + owners),
        out_specs=[vmem()] * 3,
        compiler_params=params(),
        name="combine",
    )(match, *got)

    dense = pl.pallas_call(
        functools.partial(dense_kernel, rows),
        out_shape=[f32(rows, blocks, sources)] * owners,
        in_specs=[vmem()] * 2,
        out_specs=[vmem()] * owners,
        compiler_params=params(),
        name="dense",
    )(place, gradient(spread(slot_piece, slot_short)))
    own = functools.reduce(lambda a, b: a + b, round_tiles(dense), own_first)
    whole = pl.pallas_call(
        functools.partial(final_kernel, layout, spacing),
        out_shape=f32(param_rows, blocks, sources),
        in_specs=[vmem()] * (1 + 2 * epochs),
        out_specs=vmem(),
        scratch_shapes=[pltpu.VMEM((BANDS, epochs, rows, blocks, sources), F32)],
        compiler_params=params(),
        name="final",
    )(by_row, *spread(own, own))
    return jnp.transpose(whole, (1, 0, 2))


def solution(mesh):
    return jax.shard_map(
        shards,
        mesh=mesh,
        in_specs=(
            P(("region", "tile"), None, None),
            P(("region", "tile"), "epoch", "band", None, None),
            P(("region", "tile"), "epoch", "band", None, None),
            P(("region", "epoch"), "band"),
            P(("region", "tile"), None),
            P(("region", "tile")),
            P(("region", "tile"), None, None),
        ),
        out_specs=P(("region", "tile"), None, None),
        check_vma=False,
    )
```

```python
import functools
import math

import jax
import jax.numpy as jnp
from jax import lax
from jax.experimental import pallas as pl
from jax.experimental.pallas import tpu as pltpu
from jax.sharding import PartitionSpec as P

ITERS = 2
STEP = 0.005
POSITION_RATE = 1.0 / 64.0
COMPS = 7
BANDS = 2
SHARED = 4 * COMPS
HALF = SHARED // BANDS
SPLIT_UNIT = 49152.0
SPLIT_SCALE = 65536.0
LOG2E = math.log2(math.e)
F32 = jnp.float32
BF16 = jnp.bfloat16
MIB = 1024 * 1024


def quarter_layout(epochs):
    shared_rows = -(-HALF // epochs)
    rows = -(-(HALF + COMPS) // epochs)
    pieces, amp = [], 0
    for q in range(epochs):
        piece = [("s", i) for i in range(q * shared_rows, min((q + 1) * shared_rows, HALF))]
        while len(piece) < rows and amp < COMPS:
            piece.append(("a", amp))
            amp += 1
        pieces.append(piece + [None] * (rows - len(piece)))
    return shared_rows, rows, pieces


def row_of(band, entry):
    kind, i = entry
    if kind == "a":
        return 2 + 6 * i + 4 + band, None
    k, c = divmod(HALF * band + i, COMPS)
    return 2 + 6 * c + k, (k if k < 2 else None)


def split3(x):
    hi = x.astype(BF16)
    rest = x - hi.astype(F32)
    mid = rest.astype(BF16)
    low = (rest - mid.astype(F32)).astype(BF16)
    return jnp.concatenate([hi, mid, low], axis=0)


def pick(matrix, rows):
    wide = jnp.concatenate([matrix, matrix, matrix], axis=1).astype(BF16)
    return jnp.dot(wide, split3(rows), preferred_element_type=F32)


def vmem():
    return pl.BlockSpec(memory_space=pltpu.VMEM)


def smem():
    return pl.BlockSpec(memory_space=pltpu.SMEM)


def f32(*shape):
    return jax.ShapeDtypeStruct(shape, F32)


def params(mib=4):
    return pltpu.CompilerParams(vmem_limit_bytes=mib * MIB)


def half_rows():
    return [("s", i) for i in range(HALF)] + [("a", j) for j in range(COMPS)]


def pack_kernel(spacing, lists_ref, params_ref, out_ref):
    band = lax.axis_index("band")
    for b in range(BANDS):

        @pl.when(band == b)
        def _():
            for p, entry in enumerate(half_rows()):
                row, position = row_of(b, entry)
                value = params_ref[row]
                if position is not None:
                    value = spacing * params_ref[position] + value
                out_ref[p] = value

    tiles, slots = lists_ref.shape
    lane = lax.broadcasted_iota(jnp.int32, (8, 128), 1)
    ids = jnp.zeros((8, 128), jnp.int32)
    for t in range(tiles):
        for s in range(slots):
            ids = jnp.where(lane == t * slots + s, lists_ref[t, s], ids)
    out_ref[HALF + COMPS] = ids.astype(F32)


def select_kernel(wide, *refs):
    rows = HALF + COMPS
    got, (out_ref, short_ref, match_ref, place_ref) = refs[:-4], refs[-4:]
    owners = len(got)
    blocks = got[0].shape[1]
    me = lax.axis_index("tile")
    own_line = got[0][rows, :1, :]
    own_column = jnp.broadcast_to(own_line, (128, 128)).T[:wide]

    shape = (wide, owners * blocks)
    lane = lax.broadcasted_iota(jnp.int32, shape, 1)
    held = lax.rem(me - lane // blocks + owners, owners) * blocks + lane % blocks
    choose = (own_column[:, : owners * blocks] == held.astype(F32)).astype(F32)
    for p in range(rows):
        chosen = pick(choose, jnp.concatenate([ref[p] for ref in got], axis=0))
        out_ref[p] = chosen
        if p < HALF:
            short_ref[p] = chosen

    lists = jnp.concatenate([ref[rows, :1, :wide] for ref in got], axis=1)
    match_ref[:wide] = (own_column[:, :1] == lists).astype(F32)
    own_blocks = me * blocks + lax.broadcasted_iota(jnp.int32, (blocks, owners * wide), 0)
    match_ref[wide:] = (own_blocks.astype(F32) == lists).astype(F32)
    line = lax.broadcasted_iota(jnp.int32, (owners * blocks, wide), 0)
    target = lax.rem(me + line // blocks, owners) * blocks + line % blocks
    place_ref[...] = (own_line[:, :wide] == target.astype(F32)).astype(F32)


def put_together(layout, band, epoch, ins, half, other, shared, amps):
    shared_rows, rows, pieces = layout
    epochs = len(pieces)
    for k in range(epochs):
        q = lax.rem(epoch - k + epochs, epochs)
        half[q] = ins[k][...]
        other[q] = ins[epochs + k][...]
    for q, piece in enumerate(pieces):
        for p, entry in enumerate(piece):
            if entry is None:
                continue
            kind, i = entry
            if kind == "s":
                shared[band, i] = half[q, p]
                shared[1 - band, i] = other[q, p]
            else:
                amps[i] = half[q, p]


def step_kernel(layout, later, counts_any, offsets_any, psf_ref, data_ref, weight_ref, *refs):
    refs, (counts_ref, offsets_ref, sems) = refs[:-3], refs[-3:]
    copies = [
        pltpu.make_async_copy(source, target, sems.at[n])
        for n, (source, target) in enumerate(
            [(counts_any, counts_ref), (offsets_any, offsets_ref)]
        )
    ]
    for copy in copies:
        copy.start()
    shared_rows, rows, pieces = layout
    epochs = len(pieces)
    (mine, others), refs = refs[:2], refs[2:]
    taken = 2 * epochs if later else 0
    ins, refs = refs[:taken], refs[taken:]
    outs, refs = refs[: 2 * epochs], refs[2 * epochs :]
    shared, amps, derived, prof_x, prof_y, pieces_x, pieces_y, image, sums, half, other = refs[:11]
    band, epoch = lax.axis_index("band"), lax.axis_index("epoch")
    tiles = data_ref.shape[0]
    pixels = data_ref.shape[-1]
    wide = shared.shape[2]
    slots = wide // tiles
    spacing = pixels / 8.0

    shared[band] = mine[:HALF]
    shared[1 - band] = others[...]
    amps[...] = mine[HALF:]

    def row(k, c):
        r = k * COMPS + c
        return r // HALF, r % HALF

    if later:
        moved, moved_amps = refs[11:]
        put_together(layout, band, epoch, ins, half, other, moved, moved_amps)
        for k in range(4):
            shift = 0.0
            if k < 2:
                shift = functools.reduce(lambda a, b: a + b, [moved[row(k, c)] for c in range(COMPS)])
                shift = shift * (spacing * spacing * POSITION_RATE)
            for c in range(COMPS):
                shared[row(k, c)] = shared[row(k, c)] - STEP * (moved[row(k, c)] + shift)
        for c in range(COMPS):
            amps[c] = amps[c] - STEP * moved_amps[c]

    for copy in copies:
        copy.wait()
    psf = psf_ref[0, 0]
    line_of = lax.broadcasted_iota(jnp.int32, (wide, 128), 0)
    live = jnp.zeros((wide, 128), jnp.bool_)
    for t in range(tiles):
        live = live | ((line_of >= t * slots) & (line_of < t * slots + counts_ref[t]))
    off_x = off_y = jnp.zeros((wide, 128), jnp.int32)
    for t in range(tiles):
        for s in range(slots):
            at = line_of == t * slots + s
            off_x = jnp.where(at, offsets_ref[t, 0, s], off_x)
            off_y = jnp.where(at, offsets_ref[t, 1, s], off_y)
    off_x, off_y = off_x.astype(F32), off_y.astype(F32)
    for c in range(COMPS):
        lw, an = shared[row(2, c)], shared[row(3, c)]
        derived[0, c] = shared[row(0, c)] + off_x
        derived[1, c] = shared[row(1, c)] + off_y
        derived[2, c] = (-0.5 * LOG2E) / (jnp.exp(2.0 * (lw + an)) + psf * psf)
        derived[3, c] = (-0.5 * LOG2E) / (jnp.exp(2.0 * (lw - an)) + psf * psf)
        derived[4, c] = jnp.where(live, amps[c], 0.0)
        derived[5, c] = derived[4, c] * SPLIT_SCALE
    sums[...] = jnp.zeros_like(sums)

    grid = lax.broadcasted_iota(jnp.int32, (pixels, 128), 0).astype(F32)

    def cut(x, large):
        hi = (x + large) - large
        return jnp.concatenate([hi, x - hi], axis=0)

    def stack(x):
        hi = x.astype(BF16).astype(F32)
        return jnp.concatenate([hi, hi, x - hi], axis=1)

    def times(left, right):
        return jnp.dot(left, jnp.concatenate([right, right[:pixels]], axis=0), preferred_element_type=F32)

    middle = pixels // 2
    inner = lax.broadcasted_iota(jnp.int32, (8, 128), 0).astype(F32)

    def running(groups):
        sum_0 = sum_1 = sum_2 = groups[0]
        for group in groups[1:]:
            sum_0 = sum_0 + group
            sum_1 = sum_1 + sum_0
            sum_2 = sum_2 + sum_1
        return sum_0, sum_1, sum_2

    def moments(x):
        groups = [x[r : r + 8] for r in range(0, pixels, 8)]
        high = running(groups[len(groups) // 2 :][::-1])
        low = running(groups[: len(groups) // 2])
        m0 = high[0] + low[0]
        m1 = high[1] - high[0] - low[1]
        m2 = 2.0 * (high[2] + low[2]) - 2.0 * high[1] - (high[1] - high[0]) - low[1]
        first = inner * m0 + 8.0 * m1
        second = inner * (first + 8.0 * m1) + 64.0 * m2
        return [jnp.sum(m, axis=0, keepdims=True) for m in (m0, first, second)]

    def line(index, c, s):
        return derived[index, c, pl.ds(s, 1), :]

    together = 2
    for t in range(tiles):
        trips = (counts_ref[t] + together - 1) // together
        image[...] = jnp.zeros_like(image)

        def render(i, carry):
            for u in range(together):
                s = i * together + u
                g = t * slots + s
                for c in range(COMPS):
                    d = grid - line(0, c, g)
                    e = jnp.exp2(d * d * line(2, c, g))
                    prof_x[s * COMPS + c] = e
                    pieces_x[s, :, c * 128 : (c + 1) * 128] = cut(e, SPLIT_UNIT)
                    d = grid - line(1, c, g)
                    e = jnp.exp2(d * d * line(3, c, g))
                    prof_y[s * COMPS + c] = e
                    pieces_y[s, :, c * 128 : (c + 1) * 128] = cut(e * line(4, c, g), line(5, c, g))
                image[...] += lax.dot_general(
                    pieces_x[s], pieces_y[s], (((1,), (1,)), ((), ())), preferred_element_type=F32
                )
            return carry

        lax.fori_loop(0, trips, render, 0)

        model = (image[:pixels, :pixels] + image[pixels:, pixels:]) + (
            image[:pixels, pixels:] + image[pixels:, :pixels]
        )
        cotangent = weight_ref[t, 0, 0] * (model - data_ref[t, 0, 0])
        left_x, left_y = stack(cotangent), stack(cotangent.T)

        def pull(i, carry):
            for u in range(together):
                s = i * together + u
                g = t * slots + s
                for first in range(0, COMPS, 2):
                    here = min(2, COMPS - first)
                    span = pl.ds(first * 128, 128 * here)
                    by_x = times(left_x, pieces_y[s, :, span])
                    by_y = times(left_y, pieces_x[s, :, span])
                    for n in range(here):
                        c = first + n
                        at = slice(n * 128, (n + 1) * 128)
                        for k, value in enumerate(moments(prof_x[s * COMPS + c] * by_x[:, at])):
                            sums[k, c, pl.ds(g, 1), :] = value
                        for k, value in enumerate(moments(prof_y[s * COMPS + c] * by_y[:, at])):
                            sums[3 + k, c, pl.ds(g, 1), :] = value
            return carry

        lax.fori_loop(0, trips, pull, 0)

    def keep(x):
        return jnp.where(live, x, 0.0)

    for c in range(COMPS):
        lw, an = shared[row(2, c)], shared[row(3, c)]
        wide_x, wide_y = jnp.exp(2.0 * (lw + an)), jnp.exp(2.0 * (lw - an))
        inv_x, inv_y = 1.0 / (wide_x + psf * psf), 1.0 / (wide_y + psf * psf)
        amp = amps[c]
        shift_x, shift_y = middle - derived[0, c], middle - derived[1, c]
        first_x = sums[1, c] + shift_x * sums[0, c]
        first_y = sums[4, c] + shift_y * sums[3, c]
        second_x = sums[2, c] + shift_x * (sums[1, c] + first_x)
        second_y = sums[5, c] + shift_y * (sums[4, c] + first_y)
        var_x = keep(second_x * inv_x * (inv_x * wide_x))
        var_y = keep(amp * second_y * inv_y * (inv_y * wide_y))
        shared[row(0, c)] = keep(first_x * inv_x)
        shared[row(1, c)] = keep(amp * first_y * inv_y)
        shared[row(2, c)] = var_x + var_y
        shared[row(3, c)] = var_x - var_y
        amps[c] = keep(sums[3, c])
    none = jnp.zeros((wide, 128), F32)
    for q, piece in enumerate(pieces):
        for p, entry in enumerate(piece):
            is_shared = entry is not None and entry[0] == "s"
            if is_shared:
                half[q, p] = shared[band, entry[1]]
            else:
                half[q, p] = none if entry is None else amps[entry[1]]
            if p < shared_rows:
                other[q, p] = shared[1 - band, entry[1]] if is_shared else none
    for k in range(epochs):
        outs[k][...] = half[lax.rem(epoch + k, epochs)]
        outs[epochs + k][...] = other[lax.rem(epoch + k, epochs)]


def step_gradient(layout, counts, offsets, psf, data, weight, slot_rows, moved):
    shared_rows, rows, pieces = layout
    epochs = len(pieces)
    later = moved is not None
    tiles, _, slots = offsets.shape
    pixels = data.shape[-1]
    wide = tiles * slots
    shapes = [(rows, wide, 128)] * epochs + [(shared_rows, wide, 128)] * epochs
    ins = slot_rows + (moved or [])
    together = [pltpu.VMEM((BANDS, HALF, wide, 128), F32), pltpu.VMEM((COMPS, wide, 128), F32)]
    return pl.pallas_call(
        functools.partial(step_kernel, layout, later),
        out_shape=[f32(*s) for s in shapes],
        in_specs=[pl.BlockSpec(memory_space=pl.ANY)] * 2 + [smem()] + [vmem()] * (2 + len(ins)),
        out_specs=[vmem()] * len(shapes),
        scratch_shapes=together
        + [
            pltpu.VMEM((6, COMPS, wide, 128), F32),
            pltpu.VMEM((slots * COMPS, pixels, 128), F32),
            pltpu.VMEM((slots * COMPS, pixels, 128), F32),
            pltpu.VMEM((slots, 2 * pixels, COMPS * 128), F32),
            pltpu.VMEM((slots, 2 * pixels, COMPS * 128), F32),
            pltpu.VMEM((2 * pixels, 2 * pixels), F32),
            pltpu.VMEM((6, COMPS, wide, 128), F32),
            pltpu.VMEM((epochs, rows, wide, 128), F32),
            pltpu.VMEM((epochs, shared_rows, wide, 128), F32),
        ]
        + (together if later else [])
        + [
            pltpu.SMEM((tiles,), jnp.int32),
            pltpu.SMEM((tiles, 2, slots), jnp.int32),
            pltpu.SemaphoreType.DMA((2,)),
        ],
        compiler_params=params(40),
        name="later_step" if later else "first_step",
    )(counts, offsets, psf, data, weight, *ins)


def combine_kernel(layout, match_ref, *refs):
    shared_rows, rows, pieces = layout
    got, (out_ref, short_ref, own_ref) = refs[:-3], refs[-3:]
    wide = out_ref.shape[1]
    match = match_ref[...]
    for p in range(rows):
        both = pick(match, jnp.concatenate([ref[p] for ref in got], axis=0))
        out_ref[p] = both[:wide]
        if p < shared_rows:
            short_ref[p] = both[:wide]
        own_ref[p] = both[wide:]


def dense_kernel(rows, place_ref, grads, *outs):
    blocks = outs[0].shape[1]
    place = place_ref[...]
    for p in range(rows):
        dense = pick(place, grads[p])
        for k, out in enumerate(outs):
            out[p] = dense[k * blocks : (k + 1) * blocks]


def final_kernel(layout, spacing, params_ref, *refs):
    shared_rows, rows, pieces = layout
    epochs = len(pieces)
    ins, (out_ref, held) = refs[: 2 * epochs], refs[2 * epochs :]
    band, epoch = lax.axis_index("band"), lax.axis_index("epoch")
    for k in range(epochs):
        q = lax.rem(epoch - k + epochs, epochs)
        held[band, q] = ins[k][...]
        held[1 - band, q] = ins[epochs + k][...]
    shift = [0.0, 0.0]
    for b in range(BANDS):
        for q, piece in enumerate(pieces):
            for p, entry in enumerate(piece):
                if entry is None:
                    continue
                row, position = row_of(b, entry)
                grad = held[b, q, p]
                out_ref[row] = params_ref[row] - STEP * grad
                if position is not None:
                    shift[position] = shift[position] + grad
    for k in range(2):
        out_ref[k] = params_ref[k] - (STEP * POSITION_RATE * spacing) * shift[k]


def shards(source_params, pixel_data, pixel_weight, psf_width, block_lists, block_counts, block_offsets):
    owners, epochs = lax.axis_size("tile"), lax.axis_size("epoch")
    blocks, param_rows, sources = source_params.shape
    tiles, slots = block_lists.shape
    wide = tiles * slots
    spacing = pixel_data.shape[-1] / 8.0
    layout = quarter_layout(epochs)
    shared_rows, rows, pieces = layout

    def to_peers(same, other):
        kept = [same[0]]
        for k in range(1, epochs):
            kept.append(lax.ppermute(same[k], "epoch", [(i, (i + k) % epochs) for i in range(epochs)]))
        for k in range(epochs):
            pairs = [
                (i * BANDS + b, (i + k) % epochs * BANDS + 1 - b)
                for i in range(epochs)
                for b in range(BANDS)
            ]
            kept.append(lax.ppermute(other[k], ("epoch", "band"), pairs))
        return kept

    def round_tiles(arrays):
        return [arrays[0]] + [
            lax.ppermute(arrays[k], "tile", [(i, (i + k) % owners) for i in range(owners)])
            for k in range(1, owners)
        ]

    def spread(piece, other):
        return to_peers([piece] * epochs, [other] * epochs)

    def summed(parts):
        near = functools.reduce(lambda a, b: a + b, parts[:epochs])
        far = functools.reduce(lambda a, b: a + b, parts[epochs:])
        return near + jnp.pad(far, ((0, rows - shared_rows), (0, 0), (0, 0)))

    by_row = jnp.transpose(source_params, (1, 0, 2))
    offsets = jnp.transpose(block_offsets, (0, 2, 1))
    packed = pl.pallas_call(
        functools.partial(pack_kernel, spacing),
        out_shape=f32(HALF + COMPS + 1, blocks, sources),
        in_specs=[smem(), vmem()],
        out_specs=vmem(),
        compiler_params=params(),
        name="pack",
    )(block_lists, by_row)
    got = round_tiles([packed] * owners)
    slot_half, slot_short, match, place = pl.pallas_call(
        functools.partial(select_kernel, wide),
        out_shape=[
            f32(HALF + COMPS, wide, sources),
            f32(HALF, wide, sources),
            f32(wide + blocks, owners * wide),
            f32(owners * blocks, wide),
        ],
        in_specs=[vmem()] * owners,
        out_specs=[vmem()] * 4,
        compiler_params=params(),
        name="select",
    )(*got)
    slot_rows = [slot_half, lax.ppermute(slot_short, "band", [(b, 1 - b) for b in range(BANDS)])]

    def gradient(moved):
        parts = step_gradient(
            layout, block_counts, offsets, psf_width, pixel_data, pixel_weight, slot_rows, moved
        )
        return summed(to_peers(parts[:epochs], parts[epochs:]))

    got = round_tiles([gradient(None)] * owners)
    slot_piece, slot_short, own_first = pl.pallas_call(
        functools.partial(combine_kernel, layout),
        out_shape=[
            f32(rows, wide, sources),
            f32(shared_rows, wide, sources),
            f32(rows, blocks, sources),
        ],
        in_specs=[vmem()] * (1 + owners),
        out_specs=[vmem()] * 3,
        compiler_params=params(),
        name="combine",
    )(match, *got)

    dense = pl.pallas_call(
        functools.partial(dense_kernel, rows),
        out_shape=[f32(rows, blocks, sources)] * owners,
        in_specs=[vmem()] * 2,
        out_specs=[vmem()] * owners,
        compiler_params=params(),
        name="dense",
    )(place, gradient(spread(slot_piece, slot_short)))
    own = functools.reduce(lambda a, b: a + b, round_tiles(dense), own_first)
    whole = pl.pallas_call(
        functools.partial(final_kernel, layout, spacing),
        out_shape=f32(param_rows, blocks, sources),
        in_specs=[vmem()] * (1 + 2 * epochs),
        out_specs=vmem(),
        scratch_shapes=[pltpu.VMEM((BANDS, epochs, rows, blocks, sources), F32)],
        compiler_params=params(),
        name="final",
    )(by_row, *spread(own, own))
    return jnp.transpose(whole, (1, 0, 2))


def solution(mesh):
    return jax.shard_map(
        shards,
        mesh=mesh,
        in_specs=(
            P(("region", "tile"), None, None),
            P(("region", "tile"), "epoch", "band", None, None),
            P(("region", "tile"), "epoch", "band", None, None),
            P(("region", "epoch"), "band"),
            P(("region", "tile"), None),
            P(("region", "tile")),
            P(("region", "tile"), None, None),
        ),
        out_specs=P(("region", "tile"), None, None),
        check_vma=False,
    )
```

```python
import functools
import math

import jax
import jax.numpy as jnp
from jax import lax
from jax.experimental import pallas as pl
from jax.experimental.pallas import tpu as pltpu
from jax.sharding import PartitionSpec as P

ITERS = 2
STEP = 0.005
POSITION_RATE = 1.0 / 64.0
COMPS = 7
BANDS = 2
TOGETHER = 2
SHARED = 4 * COMPS
HALF = SHARED // BANDS
SPLIT_UNIT = 49152.0
SPLIT_SCALE = 65536.0
LOG2E = math.log2(math.e)
F32 = jnp.float32
BF16 = jnp.bfloat16
MIB = 1024 * 1024


def quarter_layout(epochs):
    shared_rows = -(-HALF // epochs)
    rows = -(-(HALF + COMPS) // epochs)
    pieces, amp = [], 0
    for q in range(epochs):
        piece = [("s", i) for i in range(q * shared_rows, min((q + 1) * shared_rows, HALF))]
        while len(piece) < rows and amp < COMPS:
            piece.append(("a", amp))
            amp += 1
        pieces.append(piece + [None] * (rows - len(piece)))
    return shared_rows, rows, pieces


def row_of(band, entry):
    kind, i = entry
    if kind == "a":
        return 2 + 6 * i + 4 + band, None
    k, c = divmod(HALF * band + i, COMPS)
    return 2 + 6 * c + k, (k if k < 2 else None)


def split3(x):
    hi = x.astype(BF16)
    rest = x - hi.astype(F32)
    mid = rest.astype(BF16)
    low = (rest - mid.astype(F32)).astype(BF16)
    return jnp.concatenate([hi, mid, low], axis=0)


def pick(matrix, rows):
    wide = jnp.concatenate([matrix, matrix, matrix], axis=1).astype(BF16)
    return jnp.dot(wide, split3(rows), preferred_element_type=F32)


def vmem():
    return pl.BlockSpec(memory_space=pltpu.VMEM)


def smem():
    return pl.BlockSpec(memory_space=pltpu.SMEM)


def f32(*shape):
    return jax.ShapeDtypeStruct(shape, F32)


def params(mib=4):
    return pltpu.CompilerParams(vmem_limit_bytes=mib * MIB)


def half_rows():
    return [("s", i) for i in range(HALF)] + [("a", j) for j in range(COMPS)]


def pack_kernel(spacing, lists_ref, params_ref, out_ref):
    band = lax.axis_index("band")
    for b in range(BANDS):

        @pl.when(band == b)
        def _():
            for p, entry in enumerate(half_rows()):
                row, position = row_of(b, entry)
                value = params_ref[row]
                if position is not None:
                    value = spacing * params_ref[position] + value
                out_ref[p] = value

    tiles, slots = lists_ref.shape
    lane = lax.broadcasted_iota(jnp.int32, (8, 128), 1)
    ids = jnp.zeros((8, 128), jnp.int32)
    for t in range(tiles):
        for s in range(slots):
            ids = jnp.where(lane == t * slots + s, lists_ref[t, s], ids)
    out_ref[HALF + COMPS] = ids.astype(F32)


def select_kernel(wide, *refs):
    rows = HALF + COMPS
    got, (out_ref, short_ref, match_ref, place_ref) = refs[:-4], refs[-4:]
    owners = len(got)
    blocks = got[0].shape[1]
    me = lax.axis_index("tile")
    own_line = got[0][rows, :1, :]
    own_column = jnp.broadcast_to(own_line, (128, 128)).T[:wide]

    shape = (wide, owners * blocks)
    lane = lax.broadcasted_iota(jnp.int32, shape, 1)
    held = lax.rem(me - lane // blocks + owners, owners) * blocks + lane % blocks
    choose = (own_column[:, : owners * blocks] == held.astype(F32)).astype(F32)
    for p in range(rows):
        chosen = pick(choose, jnp.concatenate([ref[p] for ref in got], axis=0))
        out_ref[p] = chosen
        if p < HALF:
            short_ref[p] = chosen

    lists = jnp.concatenate([ref[rows, :1, :wide] for ref in got], axis=1)
    match_ref[:wide] = (own_column[:, :1] == lists).astype(F32)
    own_blocks = me * blocks + lax.broadcasted_iota(jnp.int32, (blocks, owners * wide), 0)
    match_ref[wide:] = (own_blocks.astype(F32) == lists).astype(F32)
    line = lax.broadcasted_iota(jnp.int32, (owners * blocks, wide), 0)
    target = lax.rem(me + line // blocks, owners) * blocks + line % blocks
    place_ref[...] = (own_line[:, :wide] == target.astype(F32)).astype(F32)


def put_together(layout, band, epoch, ins, half, other, shared, amps):
    shared_rows, rows, pieces = layout
    epochs = len(pieces)
    for k in range(epochs):
        q = lax.rem(epoch - k + epochs, epochs)
        half[q] = ins[k][...]
        other[q] = ins[epochs + k][...]
    for q, piece in enumerate(pieces):
        for p, entry in enumerate(piece):
            if entry is None:
                continue
            kind, i = entry
            if kind == "s":
                shared[band, i] = half[q, p]
                shared[1 - band, i] = other[q, p]
            else:
                amps[i] = half[q, p]


def step_kernel(layout, later, counts_ref, offsets_ref, psf_ref, data_ref, weight_ref, *refs):
    shared_rows, rows, pieces = layout
    epochs = len(pieces)
    (mine, others), refs = refs[:2], refs[2:]
    taken = 2 * epochs if later else 0
    ins, refs = refs[:taken], refs[taken:]
    outs, refs = refs[: 2 * epochs], refs[2 * epochs :]
    shared, amps, derived, image, left_x, left_y, sums, half, other = refs[:9]
    tiles = data_ref.shape[0]
    prof_x, prof_y, pieces_x, pieces_y = (refs[9 + n * tiles : 9 + (n + 1) * tiles] for n in range(4))
    band, epoch = lax.axis_index("band"), lax.axis_index("epoch")
    pixels = data_ref.shape[-1]
    wide = shared.shape[2]
    slots = wide // tiles
    spacing = pixels / 8.0

    shared[band] = mine[:HALF]
    shared[1 - band] = others[...]
    amps[...] = mine[HALF:]

    def row(k, c):
        r = k * COMPS + c
        return r // HALF, r % HALF

    if later:
        moved, moved_amps = refs[9 + 4 * tiles :]
        put_together(layout, band, epoch, ins, half, other, moved, moved_amps)
        for k in range(4):
            shift = 0.0
            if k < 2:
                shift = functools.reduce(lambda a, b: a + b, [moved[row(k, c)] for c in range(COMPS)])
                shift = shift * (spacing * spacing * POSITION_RATE)
            for c in range(COMPS):
                shared[row(k, c)] = shared[row(k, c)] - STEP * (moved[row(k, c)] + shift)
        for c in range(COMPS):
            amps[c] = amps[c] - STEP * moved_amps[c]

    psf = psf_ref[0, 0]
    line_of = lax.broadcasted_iota(jnp.int32, (wide, 128), 0)
    live = jnp.zeros((wide, 128), jnp.bool_)
    for t in range(tiles):
        live = live | ((line_of >= t * slots) & (line_of < t * slots + counts_ref[t]))
    off_x = off_y = jnp.zeros((wide, 128), jnp.int32)
    for t in range(tiles):
        for s in range(slots):
            at = line_of == t * slots + s
            off_x = jnp.where(at, offsets_ref[t, 0, s], off_x)
            off_y = jnp.where(at, offsets_ref[t, 1, s], off_y)
    off_x, off_y = off_x.astype(F32), off_y.astype(F32)
    for c in range(COMPS):
        lw, an = shared[row(2, c)], shared[row(3, c)]
        derived[0, c] = shared[row(0, c)] + off_x
        derived[1, c] = shared[row(1, c)] + off_y
        derived[2, c] = (-0.5 * LOG2E) / (jnp.exp(2.0 * (lw + an)) + psf * psf)
        derived[3, c] = (-0.5 * LOG2E) / (jnp.exp(2.0 * (lw - an)) + psf * psf)
        derived[4, c] = jnp.where(live, amps[c], 0.0)
        derived[5, c] = derived[4, c] * SPLIT_SCALE
    sums[...] = jnp.zeros_like(sums)

    grid = lax.broadcasted_iota(jnp.int32, (pixels, 128), 0).astype(F32)

    def cut(x, large):
        hi = (x + large) - large
        return jnp.concatenate([hi, x - hi], axis=0)

    def stack(x):
        hi = x.astype(BF16).astype(F32)
        return jnp.concatenate([hi, hi, x - hi], axis=1)

    def times(left, right):
        return jnp.dot(left, jnp.concatenate([right, right[:pixels]], axis=0), preferred_element_type=F32)

    middle = pixels // 2
    inner = lax.broadcasted_iota(jnp.int32, (8, 128), 0).astype(F32)

    def running(groups):
        sum_0 = sum_1 = sum_2 = groups[0]
        for group in groups[1:]:
            sum_0 = sum_0 + group
            sum_1 = sum_1 + sum_0
            sum_2 = sum_2 + sum_1
        return sum_0, sum_1, sum_2

    def moments(x):
        groups = [x[r : r + 8] for r in range(0, pixels, 8)]
        high = running(groups[len(groups) // 2 :][::-1])
        low = running(groups[: len(groups) // 2])
        m0 = high[0] + low[0]
        m1 = high[1] - high[0] - low[1]
        m2 = 2.0 * (high[2] + low[2]) - 2.0 * high[1] - (high[1] - high[0]) - low[1]
        first = inner * m0 + 8.0 * m1
        second = inner * (first + 8.0 * m1) + 64.0 * m2
        return [jnp.sum(m, axis=0, keepdims=True) for m in (m0, first, second)]

    def line(index, c, s):
        return derived[index, c, pl.ds(s, 1), :]

    def profiles(t, s, c):
        g = t * slots + s
        at = slice(c * 128, (c + 1) * 128)
        d = grid - line(0, c, g)
        e = jnp.exp2(d * d * line(2, c, g))
        prof_x[t][s * COMPS + c] = e
        pieces_x[t][s, :, at] = cut(e, SPLIT_UNIT)
        d = grid - line(1, c, g)
        e = jnp.exp2(d * d * line(3, c, g))
        prof_y[t][s * COMPS + c] = e
        pieces_y[t][s, :, at] = cut(e * line(4, c, g), line(5, c, g))

    def add_image(t, s):
        image[...] += lax.dot_general(
            pieces_x[t][s], pieces_y[t][s], (((1,), (1,)), ((), ())), preferred_element_type=F32
        )

    def pull_pair(t, s, first):
        g = t * slots + s
        here = min(2, COMPS - first)
        span = slice(first * 128, (first + here) * 128)
        by_x = times(left_x[...], pieces_y[t][s, :, span])
        by_y = times(left_y[...], pieces_x[t][s, :, span])
        for n in range(here):
            c = first + n
            at = slice(n * 128, (n + 1) * 128)
            for k, value in enumerate(moments(prof_x[t][s * COMPS + c] * by_x[:, at])):
                sums[k, c, pl.ds(g, 1), :] = value
            for k, value in enumerate(moments(prof_y[t][s * COMPS + c] * by_y[:, at])):
                sums[3 + k, c, pl.ds(g, 1), :] = value

    def loop(first, last, rendered=None, pulled=None):
        def body(i, carry):
            for u in range(TOGETHER):
                s = i * TOGETHER + u
                for c in range(COMPS):
                    if rendered is not None:
                        profiles(rendered, s, c)
                    if pulled is not None and c % 2 == 0:
                        pull_pair(pulled, s, c)
                if rendered is not None:
                    add_image(rendered, s)
            return carry

        lax.fori_loop(first, last, body, 0)

    trips = [(counts_ref[t] + TOGETHER - 1) // TOGETHER for t in range(tiles)]
    for t in range(tiles):
        image[...] = jnp.zeros_like(image)
        common = 0
        if t > 0:
            common = jnp.minimum(trips[t - 1], trips[t])
            loop(0, common, rendered=t, pulled=t - 1)
            loop(common, trips[t - 1], pulled=t - 1)
        loop(common, trips[t], rendered=t)
        model = (image[:pixels, :pixels] + image[pixels:, pixels:]) + (
            image[:pixels, pixels:] + image[pixels:, :pixels]
        )
        cotangent = weight_ref[t, 0, 0] * (model - data_ref[t, 0, 0])
        left_x[...] = stack(cotangent)
        left_y[...] = stack(cotangent.T)
    loop(0, trips[tiles - 1], pulled=tiles - 1)

    def keep(x):
        return jnp.where(live, x, 0.0)

    for c in range(COMPS):
        lw, an = shared[row(2, c)], shared[row(3, c)]
        wide_x, wide_y = jnp.exp(2.0 * (lw + an)), jnp.exp(2.0 * (lw - an))
        inv_x, inv_y = 1.0 / (wide_x + psf * psf), 1.0 / (wide_y + psf * psf)
        amp = amps[c]
        shift_x, shift_y = middle - derived[0, c], middle - derived[1, c]
        first_x = sums[1, c] + shift_x * sums[0, c]
        first_y = sums[4, c] + shift_y * sums[3, c]
        second_x = sums[2, c] + shift_x * (sums[1, c] + first_x)
        second_y = sums[5, c] + shift_y * (sums[4, c] + first_y)
        var_x = keep(second_x * inv_x * (inv_x * wide_x))
        var_y = keep(amp * second_y * inv_y * (inv_y * wide_y))
        shared[row(0, c)] = keep(first_x * inv_x)
        shared[row(1, c)] = keep(amp * first_y * inv_y)
        shared[row(2, c)] = var_x + var_y
        shared[row(3, c)] = var_x - var_y
        amps[c] = keep(sums[3, c])
    none = jnp.zeros((wide, 128), F32)
    for q, piece in enumerate(pieces):
        for p, entry in enumerate(piece):
            is_shared = entry is not None and entry[0] == "s"
            if is_shared:
                half[q, p] = shared[band, entry[1]]
            else:
                half[q, p] = none if entry is None else amps[entry[1]]
            if p < shared_rows:
                other[q, p] = shared[1 - band, entry[1]] if is_shared else none
    for k in range(epochs):
        outs[k][...] = half[lax.rem(epoch + k, epochs)]
        outs[epochs + k][...] = other[lax.rem(epoch + k, epochs)]


def step_gradient(layout, counts, offsets, psf, data, weight, slot_rows, moved):
    shared_rows, rows, pieces = layout
    epochs = len(pieces)
    later = moved is not None
    tiles, _, slots = offsets.shape
    pixels = data.shape[-1]
    wide = tiles * slots
    shapes = [(rows, wide, 128)] * epochs + [(shared_rows, wide, 128)] * epochs
    ins = slot_rows + (moved or [])
    together = [pltpu.VMEM((BANDS, HALF, wide, 128), F32), pltpu.VMEM((COMPS, wide, 128), F32)]
    return pl.pallas_call(
        functools.partial(step_kernel, layout, later),
        out_shape=[f32(*s) for s in shapes],
        in_specs=[smem()] * 3 + [vmem()] * (2 + len(ins)),
        out_specs=[vmem()] * len(shapes),
        scratch_shapes=together
        + [
            pltpu.VMEM((6, COMPS, wide, 128), F32),
            pltpu.VMEM((2 * pixels, 2 * pixels), F32),
            pltpu.VMEM((pixels, 3 * pixels), F32),
            pltpu.VMEM((pixels, 3 * pixels), F32),
            pltpu.VMEM((6, COMPS, wide, 128), F32),
            pltpu.VMEM((epochs, rows, wide, 128), F32),
            pltpu.VMEM((epochs, shared_rows, wide, 128), F32),
        ]
        + [pltpu.VMEM((slots * COMPS, pixels, 128), F32)] * (2 * tiles)
        + [pltpu.VMEM((slots, 2 * pixels, COMPS * 128), F32)] * (2 * tiles)
        + (together if later else []),
        compiler_params=params(52),
        name="later_step" if later else "first_step",
    )(counts, offsets, psf, data, weight, *ins)


def combine_kernel(layout, match_ref, *refs):
    shared_rows, rows, pieces = layout
    got, (out_ref, short_ref, own_ref) = refs[:-3], refs[-3:]
    wide = out_ref.shape[1]
    match = match_ref[...]
    for p in range(rows):
        both = pick(match, jnp.concatenate([ref[p] for ref in got], axis=0))
        out_ref[p] = both[:wide]
        if p < shared_rows:
            short_ref[p] = both[:wide]
        own_ref[p] = both[wide:]


def dense_kernel(rows, place_ref, grads, *outs):
    blocks = outs[0].shape[1]
    place = place_ref[...]
    for p in range(rows):
        dense = pick(place, grads[p])
        for k, out in enumerate(outs):
            out[p] = dense[k * blocks : (k + 1) * blocks]


def final_kernel(layout, spacing, params_ref, *refs):
    shared_rows, rows, pieces = layout
    epochs = len(pieces)
    ins, (out_ref, held) = refs[: 2 * epochs], refs[2 * epochs :]
    band, epoch = lax.axis_index("band"), lax.axis_index("epoch")
    for k in range(epochs):
        q = lax.rem(epoch - k + epochs, epochs)
        held[band, q] = ins[k][...]
        held[1 - band, q] = ins[epochs + k][...]
    shift = [0.0, 0.0]
    for b in range(BANDS):
        for q, piece in enumerate(pieces):
            for p, entry in enumerate(piece):
                if entry is None:
                    continue
                row, position = row_of(b, entry)
                grad = held[b, q, p]
                out_ref[row] = params_ref[row] - STEP * grad
                if position is not None:
                    shift[position] = shift[position] + grad
    for k in range(2):
        out_ref[k] = params_ref[k] - (STEP * POSITION_RATE * spacing) * shift[k]


def shards(source_params, pixel_data, pixel_weight, psf_width, block_lists, block_counts, block_offsets):
    owners, epochs = lax.axis_size("tile"), lax.axis_size("epoch")
    blocks, param_rows, sources = source_params.shape
    tiles, slots = block_lists.shape
    wide = tiles * slots
    spacing = pixel_data.shape[-1] / 8.0
    layout = quarter_layout(epochs)
    shared_rows, rows, pieces = layout

    def to_peers(same, other):
        kept = [same[0]]
        for k in range(1, epochs):
            kept.append(lax.ppermute(same[k], "epoch", [(i, (i + k) % epochs) for i in range(epochs)]))
        for k in range(epochs):
            pairs = [
                (i * BANDS + b, (i + k) % epochs * BANDS + 1 - b)
                for i in range(epochs)
                for b in range(BANDS)
            ]
            kept.append(lax.ppermute(other[k], ("epoch", "band"), pairs))
        return kept

    def round_tiles(arrays):
        return [arrays[0]] + [
            lax.ppermute(arrays[k], "tile", [(i, (i + k) % owners) for i in range(owners)])
            for k in range(1, owners)
        ]

    def spread(piece, other):
        return to_peers([piece] * epochs, [other] * epochs)

    def summed(parts):
        near = functools.reduce(lambda a, b: a + b, parts[:epochs])
        far = functools.reduce(lambda a, b: a + b, parts[epochs:])
        return near + jnp.pad(far, ((0, rows - shared_rows), (0, 0), (0, 0)))

    by_row = jnp.transpose(source_params, (1, 0, 2))
    offsets = jnp.transpose(block_offsets, (0, 2, 1))
    packed = pl.pallas_call(
        functools.partial(pack_kernel, spacing),
        out_shape=f32(HALF + COMPS + 1, blocks, sources),
        in_specs=[smem(), vmem()],
        out_specs=vmem(),
        compiler_params=params(),
        name="pack",
    )(block_lists, by_row)
    got = round_tiles([packed] * owners)
    slot_half, slot_short, match, place = pl.pallas_call(
        functools.partial(select_kernel, wide),
        out_shape=[
            f32(HALF + COMPS, wide, sources),
            f32(HALF, wide, sources),
            f32(wide + blocks, owners * wide),
            f32(owners * blocks, wide),
        ],
        in_specs=[vmem()] * owners,
        out_specs=[vmem()] * 4,
        compiler_params=params(),
        name="select",
    )(*got)
    slot_rows = [slot_half, lax.ppermute(slot_short, "band", [(b, 1 - b) for b in range(BANDS)])]

    def gradient(moved):
        parts = step_gradient(
            layout, block_counts, offsets, psf_width, pixel_data, pixel_weight, slot_rows, moved
        )
        return summed(to_peers(parts[:epochs], parts[epochs:]))

    got = round_tiles([gradient(None)] * owners)
    slot_piece, slot_short, own_first = pl.pallas_call(
        functools.partial(combine_kernel, layout),
        out_shape=[
            f32(rows, wide, sources),
            f32(shared_rows, wide, sources),
            f32(rows, blocks, sources),
        ],
        in_specs=[vmem()] * (1 + owners),
        out_specs=[vmem()] * 3,
        compiler_params=params(),
        name="combine",
    )(match, *got)

    dense = pl.pallas_call(
        functools.partial(dense_kernel, rows),
        out_shape=[f32(rows, blocks, sources)] * owners,
        in_specs=[vmem()] * 2,
        out_specs=[vmem()] * owners,
        compiler_params=params(),
        name="dense",
    )(place, gradient(spread(slot_piece, slot_short)))
    own = functools.reduce(lambda a, b: a + b, round_tiles(dense), own_first)
    whole = pl.pallas_call(
        functools.partial(final_kernel, layout, spacing),
        out_shape=f32(param_rows, blocks, sources),
        in_specs=[vmem()] * (1 + 2 * epochs),
        out_specs=vmem(),
        scratch_shapes=[pltpu.VMEM((BANDS, epochs, rows, blocks, sources), F32)],
        compiler_params=params(),
        name="final",
    )(by_row, *spread(own, own))
    return jnp.transpose(whole, (1, 0, 2))


def solution(mesh):
    return jax.shard_map(
        shards,
        mesh=mesh,
        in_specs=(
            P(("region", "tile"), None, None),
            P(("region", "tile"), "epoch", "band", None, None),
            P(("region", "tile"), "epoch", "band", None, None),
            P(("region", "epoch"), "band"),
            P(("region", "tile"), None),
            P(("region", "tile")),
            P(("region", "tile"), None, None),
        ),
        out_specs=P(("region", "tile"), None, None),
        check_vma=False,
    )
```

```python
import functools
import math

import jax
import jax.numpy as jnp
from jax import lax
from jax.experimental import pallas as pl
from jax.experimental.pallas import tpu as pltpu
from jax.sharding import PartitionSpec as P

ITERS = 2
STEP = 0.005
POSITION_RATE = 1.0 / 64.0
COMPS = 7
BANDS = 2
TOGETHER = 2
SHARED = 4 * COMPS
HALF = SHARED // BANDS
SPLIT_UNIT = 49152.0
SPLIT_SCALE = 65536.0
LOG2E = math.log2(math.e)
F32 = jnp.float32
BF16 = jnp.bfloat16
MIB = 1024 * 1024


def quarter_layout(epochs):
    shared_rows = -(-HALF // epochs)
    rows = -(-(HALF + COMPS) // epochs)
    pieces, amp = [], 0
    for q in range(epochs):
        piece = [("s", i) for i in range(q * shared_rows, min((q + 1) * shared_rows, HALF))]
        while len(piece) < rows and amp < COMPS:
            piece.append(("a", amp))
            amp += 1
        pieces.append(piece + [None] * (rows - len(piece)))
    return shared_rows, rows, pieces


def row_of(band, entry):
    kind, i = entry
    if kind == "a":
        return 2 + 6 * i + 4 + band, None
    k, c = divmod(HALF * band + i, COMPS)
    return 2 + 6 * c + k, (k if k < 2 else None)


def split3(x):
    hi = x.astype(BF16)
    rest = x - hi.astype(F32)
    mid = rest.astype(BF16)
    low = (rest - mid.astype(F32)).astype(BF16)
    return jnp.concatenate([hi, mid, low], axis=0)


def pick(matrix, rows):
    wide = jnp.concatenate([matrix, matrix, matrix], axis=1).astype(BF16)
    return jnp.dot(wide, split3(rows), preferred_element_type=F32)


def vmem():
    return pl.BlockSpec(memory_space=pltpu.VMEM)


def smem():
    return pl.BlockSpec(memory_space=pltpu.SMEM)


def f32(*shape):
    return jax.ShapeDtypeStruct(shape, F32)


def params(mib=4):
    return pltpu.CompilerParams(vmem_limit_bytes=mib * MIB)


def half_rows():
    return [("s", i) for i in range(HALF)] + [("a", j) for j in range(COMPS)]


def pack_kernel(spacing, lists_ref, params_ref, out_ref):
    band = lax.axis_index("band")
    for b in range(BANDS):

        @pl.when(band == b)
        def _():
            for p, entry in enumerate(half_rows()):
                row, position = row_of(b, entry)
                value = params_ref[row]
                if position is not None:
                    value = spacing * params_ref[position] + value
                out_ref[p] = value

    tiles, slots = lists_ref.shape
    lane = lax.broadcasted_iota(jnp.int32, (8, 128), 1)
    ids = jnp.zeros((8, 128), jnp.int32)
    for t in range(tiles):
        for s in range(slots):
            ids = jnp.where(lane == t * slots + s, lists_ref[t, s], ids)
    out_ref[HALF + COMPS] = ids.astype(F32)


def select_kernel(wide, *refs):
    rows = HALF + COMPS
    got, (out_ref, short_ref, match_ref, place_ref) = refs[:-4], refs[-4:]
    owners = len(got)
    blocks = got[0].shape[1]
    me = lax.axis_index("tile")
    own_line = got[0][rows, :1, :]
    own_column = jnp.broadcast_to(own_line, (128, 128)).T[:wide]

    shape = (wide, owners * blocks)
    lane = lax.broadcasted_iota(jnp.int32, shape, 1)
    held = lax.rem(me - lane // blocks + owners, owners) * blocks + lane % blocks
    choose = (own_column[:, : owners * blocks] == held.astype(F32)).astype(F32)
    for p in range(rows):
        chosen = pick(choose, jnp.concatenate([ref[p] for ref in got], axis=0))
        out_ref[p] = chosen
        if p < HALF:
            short_ref[p] = chosen

    lists = jnp.concatenate([ref[rows, :1, :wide] for ref in got], axis=1)
    match_ref[:wide] = (own_column[:, :1] == lists).astype(F32)
    own_blocks = me * blocks + lax.broadcasted_iota(jnp.int32, (blocks, owners * wide), 0)
    match_ref[wide:] = (own_blocks.astype(F32) == lists).astype(F32)
    line = lax.broadcasted_iota(jnp.int32, (owners * blocks, wide), 0)
    target = lax.rem(me + line // blocks, owners) * blocks + line % blocks
    place_ref[...] = (own_line[:, :wide] == target.astype(F32)).astype(F32)


def put_together(layout, band, epoch, ins, half, other, shared, amps):
    shared_rows, rows, pieces = layout
    epochs = len(pieces)
    for k in range(epochs):
        q = lax.rem(epoch - k + epochs, epochs)
        half[q] = ins[k][...]
        other[q] = ins[epochs + k][...]
    for q, piece in enumerate(pieces):
        for p, entry in enumerate(piece):
            if entry is None:
                continue
            kind, i = entry
            if kind == "s":
                shared[band, i] = half[q, p]
                shared[1 - band, i] = other[q, p]
            else:
                amps[i] = half[q, p]


def step_kernel(layout, later, counts_ref, offsets_ref, psf_ref, data_ref, weight_ref, *refs):
    shared_rows, rows, pieces = layout
    epochs = len(pieces)
    (mine, others), refs = refs[:2], refs[2:]
    taken = 2 * epochs if later else 0
    ins, refs = refs[:taken], refs[taken:]
    outs, refs = refs[: 2 * epochs], refs[2 * epochs :]
    shared, amps, derived, image, left_x, left_y, sums, half, other = refs[:9]
    tiles = data_ref.shape[0]
    prof_x, prof_y, pieces_x, pieces_y = (refs[9 + n * tiles : 9 + (n + 1) * tiles] for n in range(4))
    band, epoch = lax.axis_index("band"), lax.axis_index("epoch")
    pixels = data_ref.shape[-1]
    wide = shared.shape[2]
    slots = wide // tiles
    spacing = pixels / 8.0

    shared[band] = mine[:HALF]
    shared[1 - band] = others[...]
    amps[...] = mine[HALF:]

    def row(k, c):
        r = k * COMPS + c
        return r // HALF, r % HALF

    if later:
        moved, moved_amps = refs[9 + 4 * tiles :]
        put_together(layout, band, epoch, ins, half, other, moved, moved_amps)
        for k in range(4):
            shift = 0.0
            if k < 2:
                shift = functools.reduce(lambda a, b: a + b, [moved[row(k, c)] for c in range(COMPS)])
                shift = shift * (spacing * spacing * POSITION_RATE)
            for c in range(COMPS):
                shared[row(k, c)] = shared[row(k, c)] - STEP * (moved[row(k, c)] + shift)
        for c in range(COMPS):
            amps[c] = amps[c] - STEP * moved_amps[c]

    psf = psf_ref[0, 0]
    line_of = lax.broadcasted_iota(jnp.int32, (wide, 128), 0)
    live = jnp.zeros((wide, 128), jnp.bool_)
    for t in range(tiles):
        live = live | ((line_of >= t * slots) & (line_of < t * slots + counts_ref[t]))
    off_x = off_y = jnp.zeros((wide, 128), jnp.int32)
    for t in range(tiles):
        for s in range(slots):
            at = line_of == t * slots + s
            off_x = jnp.where(at, offsets_ref[t, 0, s], off_x)
            off_y = jnp.where(at, offsets_ref[t, 1, s], off_y)
    off_x, off_y = off_x.astype(F32), off_y.astype(F32)
    for c in range(COMPS):
        lw, an = shared[row(2, c)], shared[row(3, c)]
        derived[0, c] = shared[row(0, c)] + off_x
        derived[1, c] = shared[row(1, c)] + off_y
        derived[2, c] = (-0.5 * LOG2E) / (jnp.exp(2.0 * (lw + an)) + psf * psf)
        derived[3, c] = (-0.5 * LOG2E) / (jnp.exp(2.0 * (lw - an)) + psf * psf)
        derived[4, c] = jnp.where(live, amps[c], 0.0)
        derived[5, c] = derived[4, c] * SPLIT_SCALE
    sums[...] = jnp.zeros_like(sums)

    grid = lax.broadcasted_iota(jnp.int32, (pixels, 128), 0).astype(F32)

    def cut(x, large):
        hi = (x + large) - large
        return jnp.concatenate([hi, x - hi], axis=0)

    def stack(x):
        hi = x.astype(BF16).astype(F32)
        return jnp.concatenate([hi, hi, x - hi], axis=1)

    def times(left, right):
        return jnp.dot(left, jnp.concatenate([right, right[:pixels]], axis=0), preferred_element_type=F32)

    middle = pixels // 2
    inner = lax.broadcasted_iota(jnp.int32, (8, 128), 0).astype(F32)

    def running(groups):
        sum_0 = sum_1 = sum_2 = groups[0]
        for group in groups[1:]:
            sum_0 = sum_0 + group
            sum_1 = sum_1 + sum_0
            sum_2 = sum_2 + sum_1
        return sum_0, sum_1, sum_2

    def moments(x):
        groups = [x[r : r + 8] for r in range(0, pixels, 8)]
        high = running(groups[len(groups) // 2 :][::-1])
        low = running(groups[: len(groups) // 2])
        m0 = high[0] + low[0]
        m1 = high[1] - high[0] - low[1]
        m2 = 2.0 * (high[2] + low[2]) - 2.0 * high[1] - (high[1] - high[0]) - low[1]
        first = inner * m0 + 8.0 * m1
        second = inner * (first + 8.0 * m1) + 64.0 * m2
        return [jnp.sum(m, axis=0, keepdims=True) for m in (m0, first, second)]

    def line(index, c, s):
        return derived[index, c, pl.ds(s, 1), :]

    def profiles(t, s, c):
        g = t * slots + s
        at = slice(c * 128, (c + 1) * 128)
        d = grid - line(0, c, g)
        e = jnp.exp2(d * d * line(2, c, g))
        prof_x[t][s * COMPS + c] = e
        pieces_x[t][s, :, at] = cut(e, SPLIT_UNIT)
        d = grid - line(1, c, g)
        e = jnp.exp2(d * d * line(3, c, g))
        prof_y[t][s * COMPS + c] = e
        pieces_y[t][s, :, at] = cut(e * line(4, c, g), line(5, c, g))

    def add_image(t, s):
        lanes = (((1,), (1,)), ((), ()))
        hi, lo = pieces_x[t][s, :pixels], pieces_x[t][s, pixels:]
        image[:, : 2 * pixels] += lax.dot_general(hi, pieces_y[t][s], lanes, preferred_element_type=F32)
        image[:, 2 * pixels :] += lax.dot_general(
            lo, pieces_y[t][s, :pixels], lanes, preferred_element_type=F32
        )

    def pull_pair(t, s, first):
        g = t * slots + s
        here = min(2, COMPS - first)
        span = slice(first * 128, (first + here) * 128)
        by_x = times(left_x[...], pieces_y[t][s, :, span])
        by_y = times(left_y[...], pieces_x[t][s, :, span])
        for n in range(here):
            c = first + n
            at = slice(n * 128, (n + 1) * 128)
            for k, value in enumerate(moments(prof_x[t][s * COMPS + c] * by_x[:, at])):
                sums[k, c, pl.ds(g, 1), :] = value
            for k, value in enumerate(moments(prof_y[t][s * COMPS + c] * by_y[:, at])):
                sums[3 + k, c, pl.ds(g, 1), :] = value

    def loop(first, last, rendered=None, pulled=None):
        def body(i, carry):
            for u in range(TOGETHER):
                s = i * TOGETHER + u
                for c in range(COMPS):
                    if rendered is not None:
                        profiles(rendered, s, c)
                    if pulled is not None and c % 2 == 0:
                        pull_pair(pulled, s, c)
                if rendered is not None:
                    add_image(rendered, s)
            return carry

        lax.fori_loop(first, last, body, 0)

    trips = [(counts_ref[t] + TOGETHER - 1) // TOGETHER for t in range(tiles)]
    for t in range(tiles):
        image[...] = jnp.zeros_like(image)
        common = 0
        if t > 0:
            common = jnp.minimum(trips[t - 1], trips[t])
            loop(0, common, rendered=t, pulled=t - 1)
            loop(common, trips[t - 1], pulled=t - 1)
        loop(common, trips[t], rendered=t)
        model = image[:, :pixels] + (image[:, pixels : 2 * pixels] + image[:, 2 * pixels :])
        cotangent = weight_ref[t, 0, 0] * (model - data_ref[t, 0, 0])
        left_x[...] = stack(cotangent)
        left_y[...] = stack(cotangent.T)
    loop(0, trips[tiles - 1], pulled=tiles - 1)

    def keep(x):
        return jnp.where(live, x, 0.0)

    for c in range(COMPS):
        lw, an = shared[row(2, c)], shared[row(3, c)]
        wide_x, wide_y = jnp.exp(2.0 * (lw + an)), jnp.exp(2.0 * (lw - an))
        inv_x, inv_y = 1.0 / (wide_x + psf * psf), 1.0 / (wide_y + psf * psf)
        amp = amps[c]
        shift_x, shift_y = middle - derived[0, c], middle - derived[1, c]
        first_x = sums[1, c] + shift_x * sums[0, c]
        first_y = sums[4, c] + shift_y * sums[3, c]
        second_x = sums[2, c] + shift_x * (sums[1, c] + first_x)
        second_y = sums[5, c] + shift_y * (sums[4, c] + first_y)
        var_x = keep(second_x * inv_x * (inv_x * wide_x))
        var_y = keep(amp * second_y * inv_y * (inv_y * wide_y))
        shared[row(0, c)] = keep(first_x * inv_x)
        shared[row(1, c)] = keep(amp * first_y * inv_y)
        shared[row(2, c)] = var_x + var_y
        shared[row(3, c)] = var_x - var_y
        amps[c] = keep(sums[3, c])
    none = jnp.zeros((wide, 128), F32)
    for q, piece in enumerate(pieces):
        for p, entry in enumerate(piece):
            is_shared = entry is not None and entry[0] == "s"
            if is_shared:
                half[q, p] = shared[band, entry[1]]
            else:
                half[q, p] = none if entry is None else amps[entry[1]]
            if p < shared_rows:
                other[q, p] = shared[1 - band, entry[1]] if is_shared else none
    for k in range(epochs):
        outs[k][...] = half[lax.rem(epoch + k, epochs)]
        outs[epochs + k][...] = other[lax.rem(epoch + k, epochs)]


def step_gradient(layout, counts, offsets, psf, data, weight, slot_rows, moved):
    shared_rows, rows, pieces = layout
    epochs = len(pieces)
    later = moved is not None
    tiles, _, slots = offsets.shape
    pixels = data.shape[-1]
    wide = tiles * slots
    shapes = [(rows, wide, 128)] * epochs + [(shared_rows, wide, 128)] * epochs
    ins = slot_rows + (moved or [])
    together = [pltpu.VMEM((BANDS, HALF, wide, 128), F32), pltpu.VMEM((COMPS, wide, 128), F32)]
    return pl.pallas_call(
        functools.partial(step_kernel, layout, later),
        out_shape=[f32(*s) for s in shapes],
        in_specs=[smem()] * 3 + [vmem()] * (2 + len(ins)),
        out_specs=[vmem()] * len(shapes),
        scratch_shapes=together
        + [
            pltpu.VMEM((6, COMPS, wide, 128), F32),
            pltpu.VMEM((pixels, 3 * pixels), F32),
            pltpu.VMEM((pixels, 3 * pixels), F32),
            pltpu.VMEM((pixels, 3 * pixels), F32),
            pltpu.VMEM((6, COMPS, wide, 128), F32),
            pltpu.VMEM((epochs, rows, wide, 128), F32),
            pltpu.VMEM((epochs, shared_rows, wide, 128), F32),
        ]
        + [pltpu.VMEM((slots * COMPS, pixels, 128), F32)] * (2 * tiles)
        + [pltpu.VMEM((slots, 2 * pixels, COMPS * 128), F32)] * (2 * tiles)
        + (together if later else []),
        compiler_params=params(52),
        name="later_step" if later else "first_step",
    )(counts, offsets, psf, data, weight, *ins)


def combine_kernel(layout, match_ref, *refs):
    shared_rows, rows, pieces = layout
    got, (out_ref, short_ref, own_ref) = refs[:-3], refs[-3:]
    wide = out_ref.shape[1]
    match = match_ref[...]
    for p in range(rows):
        both = pick(match, jnp.concatenate([ref[p] for ref in got], axis=0))
        out_ref[p] = both[:wide]
        if p < shared_rows:
            short_ref[p] = both[:wide]
        own_ref[p] = both[wide:]


def dense_kernel(rows, place_ref, grads, *outs):
    blocks = outs[0].shape[1]
    place = place_ref[...]
    for p in range(rows):
        dense = pick(place, grads[p])
        for k, out in enumerate(outs):
            out[p] = dense[k * blocks : (k + 1) * blocks]


def final_kernel(layout, spacing, params_ref, *refs):
    shared_rows, rows, pieces = layout
    epochs = len(pieces)
    ins, (out_ref, held) = refs[: 2 * epochs], refs[2 * epochs :]
    band, epoch = lax.axis_index("band"), lax.axis_index("epoch")
    for k in range(epochs):
        q = lax.rem(epoch - k + epochs, epochs)
        held[band, q] = ins[k][...]
        held[1 - band, q] = ins[epochs + k][...]
    shift = [0.0, 0.0]
    for b in range(BANDS):
        for q, piece in enumerate(pieces):
            for p, entry in enumerate(piece):
                if entry is None:
                    continue
                row, position = row_of(b, entry)
                grad = held[b, q, p]
                out_ref[row] = params_ref[row] - STEP * grad
                if position is not None:
                    shift[position] = shift[position] + grad
    for k in range(2):
        out_ref[k] = params_ref[k] - (STEP * POSITION_RATE * spacing) * shift[k]


def shards(source_params, pixel_data, pixel_weight, psf_width, block_lists, block_counts, block_offsets):
    owners, epochs = lax.axis_size("tile"), lax.axis_size("epoch")
    blocks, param_rows, sources = source_params.shape
    tiles, slots = block_lists.shape
    wide = tiles * slots
    spacing = pixel_data.shape[-1] / 8.0
    layout = quarter_layout(epochs)
    shared_rows, rows, pieces = layout

    def to_peers(same, other):
        kept = [same[0]]
        for k in range(1, epochs):
            kept.append(lax.ppermute(same[k], "epoch", [(i, (i + k) % epochs) for i in range(epochs)]))
        for k in range(epochs):
            pairs = [
                (i * BANDS + b, (i + k) % epochs * BANDS + 1 - b)
                for i in range(epochs)
                for b in range(BANDS)
            ]
            kept.append(lax.ppermute(other[k], ("epoch", "band"), pairs))
        return kept

    def round_tiles(arrays):
        return [arrays[0]] + [
            lax.ppermute(arrays[k], "tile", [(i, (i + k) % owners) for i in range(owners)])
            for k in range(1, owners)
        ]

    def spread(piece, other):
        return to_peers([piece] * epochs, [other] * epochs)

    def summed(parts):
        near = functools.reduce(lambda a, b: a + b, parts[:epochs])
        far = functools.reduce(lambda a, b: a + b, parts[epochs:])
        return near + jnp.pad(far, ((0, rows - shared_rows), (0, 0), (0, 0)))

    by_row = jnp.transpose(source_params, (1, 0, 2))
    offsets = jnp.transpose(block_offsets, (0, 2, 1))
    packed = pl.pallas_call(
        functools.partial(pack_kernel, spacing),
        out_shape=f32(HALF + COMPS + 1, blocks, sources),
        in_specs=[smem(), vmem()],
        out_specs=vmem(),
        compiler_params=params(),
        name="pack",
    )(block_lists, by_row)
    got = round_tiles([packed] * owners)
    slot_half, slot_short, match, place = pl.pallas_call(
        functools.partial(select_kernel, wide),
        out_shape=[
            f32(HALF + COMPS, wide, sources),
            f32(HALF, wide, sources),
            f32(wide + blocks, owners * wide),
            f32(owners * blocks, wide),
        ],
        in_specs=[vmem()] * owners,
        out_specs=[vmem()] * 4,
        compiler_params=params(),
        name="select",
    )(*got)
    slot_rows = [slot_half, lax.ppermute(slot_short, "band", [(b, 1 - b) for b in range(BANDS)])]

    def gradient(moved):
        parts = step_gradient(
            layout, block_counts, offsets, psf_width, pixel_data, pixel_weight, slot_rows, moved
        )
        return summed(to_peers(parts[:epochs], parts[epochs:]))

    got = round_tiles([gradient(None)] * owners)
    slot_piece, slot_short, own_first = pl.pallas_call(
        functools.partial(combine_kernel, layout),
        out_shape=[
            f32(rows, wide, sources),
            f32(shared_rows, wide, sources),
            f32(rows, blocks, sources),
        ],
        in_specs=[vmem()] * (1 + owners),
        out_specs=[vmem()] * 3,
        compiler_params=params(),
        name="combine",
    )(match, *got)

    dense = pl.pallas_call(
        functools.partial(dense_kernel, rows),
        out_shape=[f32(rows, blocks, sources)] * owners,
        in_specs=[vmem()] * 2,
        out_specs=[vmem()] * owners,
        compiler_params=params(),
        name="dense",
    )(place, gradient(spread(slot_piece, slot_short)))
    own = functools.reduce(lambda a, b: a + b, round_tiles(dense), own_first)
    whole = pl.pallas_call(
        functools.partial(final_kernel, layout, spacing),
        out_shape=f32(param_rows, blocks, sources),
        in_specs=[vmem()] * (1 + 2 * epochs),
        out_specs=vmem(),
        scratch_shapes=[pltpu.VMEM((BANDS, epochs, rows, blocks, sources), F32)],
        compiler_params=params(),
        name="final",
    )(by_row, *spread(own, own))
    return jnp.transpose(whole, (1, 0, 2))


def solution(mesh):
    return jax.shard_map(
        shards,
        mesh=mesh,
        in_specs=(
            P(("region", "tile"), None, None),
            P(("region", "tile"), "epoch", "band", None, None),
            P(("region", "tile"), "epoch", "band", None, None),
            P(("region", "epoch"), "band"),
            P(("region", "tile"), None),
            P(("region", "tile")),
            P(("region", "tile"), None, None),
        ),
        out_specs=P(("region", "tile"), None, None),
        check_vma=False,
    )
```

```python
import functools
import math

import jax
import jax.numpy as jnp
from jax import lax
from jax.experimental import pallas as pl
from jax.experimental.pallas import tpu as pltpu
from jax.sharding import PartitionSpec as P

ITERS = 2
STEP = 0.005
POSITION_RATE = 1.0 / 64.0
COMPS = 7
BANDS = 2
TOGETHER = 2
SHARED = 4 * COMPS
HALF = SHARED // BANDS
SPLIT_UNIT = 49152.0
SPLIT_SCALE = 65536.0
LOG2E = math.log2(math.e)
F32 = jnp.float32
BF16 = jnp.bfloat16
MIB = 1024 * 1024


def quarter_layout(epochs):
    shared_rows = -(-HALF // epochs)
    rows = -(-(HALF + COMPS) // epochs)
    pieces, amp = [], 0
    for q in range(epochs):
        piece = [("s", i) for i in range(q * shared_rows, min((q + 1) * shared_rows, HALF))]
        while len(piece) < rows and amp < COMPS:
            piece.append(("a", amp))
            amp += 1
        pieces.append(piece + [None] * (rows - len(piece)))
    return shared_rows, rows, pieces


def row_of(band, entry):
    kind, i = entry
    if kind == "a":
        return 2 + 6 * i + 4 + band, None
    k, c = divmod(HALF * band + i, COMPS)
    return 2 + 6 * c + k, (k if k < 2 else None)


def split3(x):
    hi = x.astype(BF16)
    rest = x - hi.astype(F32)
    mid = rest.astype(BF16)
    low = (rest - mid.astype(F32)).astype(BF16)
    return jnp.concatenate([hi, mid, low], axis=0)


def pick(matrix, rows):
    wide = jnp.concatenate([matrix, matrix, matrix], axis=1).astype(BF16)
    return jnp.dot(wide, split3(rows), preferred_element_type=F32)


def vmem():
    return pl.BlockSpec(memory_space=pltpu.VMEM)


def smem():
    return pl.BlockSpec(memory_space=pltpu.SMEM)


def f32(*shape):
    return jax.ShapeDtypeStruct(shape, F32)


def params(mib=4):
    return pltpu.CompilerParams(vmem_limit_bytes=mib * MIB)


def half_rows():
    return [("s", i) for i in range(HALF)] + [("a", j) for j in range(COMPS)]


def pack_kernel(spacing, lists_ref, params_ref, out_ref):
    band = lax.axis_index("band")
    for b in range(BANDS):

        @pl.when(band == b)
        def _():
            for p, entry in enumerate(half_rows()):
                row, position = row_of(b, entry)
                value = params_ref[row]
                if position is not None:
                    value = spacing * params_ref[position] + value
                out_ref[p] = value

    tiles, slots = lists_ref.shape
    lane = lax.broadcasted_iota(jnp.int32, (8, 128), 1)
    ids = jnp.zeros((8, 128), jnp.int32)
    for t in range(tiles):
        for s in range(slots):
            ids = jnp.where(lane == t * slots + s, lists_ref[t, s], ids)
    out_ref[HALF + COMPS] = ids.astype(F32)


def select_kernel(wide, *refs):
    rows = HALF + COMPS
    got, (out_ref, short_ref, match_ref, place_ref) = refs[:-4], refs[-4:]
    owners = len(got)
    blocks = got[0].shape[1]
    me = lax.axis_index("tile")
    own_line = got[0][rows, :1, :]
    own_column = jnp.broadcast_to(own_line, (128, 128)).T[:wide]

    shape = (wide, owners * blocks)
    lane = lax.broadcasted_iota(jnp.int32, shape, 1)
    held = lax.rem(me - lane // blocks + owners, owners) * blocks + lane % blocks
    choose = (own_column[:, : owners * blocks] == held.astype(F32)).astype(F32)
    for p in range(rows):
        chosen = pick(choose, jnp.concatenate([ref[p] for ref in got], axis=0))
        out_ref[p] = chosen
        if p < HALF:
            short_ref[p] = chosen

    lists = jnp.concatenate([ref[rows, :1, :wide] for ref in got], axis=1)
    match_ref[:wide] = (own_column[:, :1] == lists).astype(F32)
    own_blocks = me * blocks + lax.broadcasted_iota(jnp.int32, (blocks, owners * wide), 0)
    match_ref[wide:] = (own_blocks.astype(F32) == lists).astype(F32)
    line = lax.broadcasted_iota(jnp.int32, (owners * blocks, wide), 0)
    target = lax.rem(me + line // blocks, owners) * blocks + line % blocks
    place_ref[...] = (own_line[:, :wide] == target.astype(F32)).astype(F32)


def put_together(layout, band, epoch, ins, half, other, shared, amps):
    shared_rows, rows, pieces = layout
    epochs = len(pieces)
    for k in range(epochs):
        q = lax.rem(epoch - k + epochs, epochs)
        half[q] = ins[k][...]
        other[q] = ins[epochs + k][...]
    for q, piece in enumerate(pieces):
        for p, entry in enumerate(piece):
            if entry is None:
                continue
            kind, i = entry
            if kind == "s":
                shared[band, i] = half[q, p]
                shared[1 - band, i] = other[q, p]
            else:
                amps[i] = half[q, p]


def step_kernel(layout, later, counts_ref, offsets_ref, psf_ref, data_ref, weight_ref, *refs):
    shared_rows, rows, pieces = layout
    epochs = len(pieces)
    (mine, others), refs = refs[:2], refs[2:]
    taken = 2 * epochs if later else 0
    ins, refs = refs[:taken], refs[taken:]
    outs, refs = refs[: 2 * epochs], refs[2 * epochs :]
    shared, amps, derived, image, left_x, left_y, sums, half, other = refs[:9]
    tiles = data_ref.shape[0]
    prof_x, prof_y, pieces_x, pieces_y = (refs[9 + n * tiles : 9 + (n + 1) * tiles] for n in range(4))
    band, epoch = lax.axis_index("band"), lax.axis_index("epoch")
    pixels = data_ref.shape[-1]
    wide = shared.shape[2]
    slots = wide // tiles
    spacing = pixels / 8.0

    shared[band] = mine[:HALF]
    shared[1 - band] = others[...]
    amps[...] = mine[HALF:]

    def row(k, c):
        r = k * COMPS + c
        return r // HALF, r % HALF

    if later:
        moved, moved_amps = refs[9 + 4 * tiles :]
        put_together(layout, band, epoch, ins, half, other, moved, moved_amps)
        for k in range(4):
            shift = 0.0
            if k < 2:
                shift = functools.reduce(lambda a, b: a + b, [moved[row(k, c)] for c in range(COMPS)])
                shift = shift * (spacing * spacing * POSITION_RATE)
            for c in range(COMPS):
                shared[row(k, c)] = shared[row(k, c)] - STEP * (moved[row(k, c)] + shift)
        for c in range(COMPS):
            amps[c] = amps[c] - STEP * moved_amps[c]

    psf = psf_ref[0, 0]
    line_of = lax.broadcasted_iota(jnp.int32, (wide, 128), 0)
    live = jnp.zeros((wide, 128), jnp.bool_)
    for t in range(tiles):
        live = live | ((line_of >= t * slots) & (line_of < t * slots + counts_ref[t]))
    off_x = off_y = jnp.zeros((wide, 128), jnp.int32)
    for t in range(tiles):
        for s in range(slots):
            at = line_of == t * slots + s
            off_x = jnp.where(at, offsets_ref[t, 0, s], off_x)
            off_y = jnp.where(at, offsets_ref[t, 1, s], off_y)
    off_x, off_y = off_x.astype(F32), off_y.astype(F32)
    for c in range(COMPS):
        lw, an = shared[row(2, c)], shared[row(3, c)]
        derived[0, c] = shared[row(0, c)] + off_x
        derived[1, c] = shared[row(1, c)] + off_y
        derived[2, c] = (-0.5 * LOG2E) / (jnp.exp(2.0 * (lw + an)) + psf * psf)
        derived[3, c] = (-0.5 * LOG2E) / (jnp.exp(2.0 * (lw - an)) + psf * psf)
        derived[4, c] = jnp.where(live, amps[c], 0.0)
        derived[5, c] = derived[4, c] * SPLIT_SCALE
    sums[...] = jnp.zeros_like(sums)

    grid = lax.broadcasted_iota(jnp.int32, (pixels, 128), 0).astype(F32)

    def cut(x, large):
        hi = (x + large) - large
        return jnp.concatenate([hi, x - hi], axis=0)

    def stack(x):
        hi = x.astype(BF16).astype(F32)
        return jnp.concatenate([hi, hi, x - hi], axis=1)

    def times(left, right):
        return jnp.dot(left, jnp.concatenate([right, right[:pixels]], axis=0), preferred_element_type=F32)

    middle = pixels // 2
    inner = lax.broadcasted_iota(jnp.int32, (8, 128), 0).astype(F32)

    def running(groups):
        sum_0 = sum_1 = sum_2 = groups[0]
        for group in groups[1:]:
            sum_0 = sum_0 + group
            sum_1 = sum_1 + sum_0
            sum_2 = sum_2 + sum_1
        return sum_0, sum_1, sum_2

    def moments(x):
        groups = [x[r : r + 8] for r in range(0, pixels, 8)]
        high = running(groups[len(groups) // 2 :][::-1])
        low = running(groups[: len(groups) // 2])
        m0 = high[0] + low[0]
        m1 = high[1] - high[0] - low[1]
        m2 = 2.0 * (high[2] + low[2]) - 2.0 * high[1] - (high[1] - high[0]) - low[1]
        first = inner * m0 + 8.0 * m1
        second = inner * (first + 8.0 * m1) + 64.0 * m2
        return [jnp.sum(m, axis=0, keepdims=True) for m in (m0, first, second)]

    def line(index, c, s):
        return derived[index, c, pl.ds(s, 1), :]

    columns = TOGETHER * COMPS

    def profiles(t, i, n):
        c = n % COMPS
        g = t * slots + i * TOGETHER + n // COMPS
        at = slice(n * 128, (n + 1) * 128)
        d = grid - line(0, c, g)
        e = jnp.exp2(d * d * line(2, c, g))
        prof_x[t][i * columns + n] = e
        pieces_x[t][i, :, at] = cut(e, SPLIT_UNIT)
        d = grid - line(1, c, g)
        e = jnp.exp2(d * d * line(3, c, g))
        prof_y[t][i * columns + n] = e
        pieces_y[t][i, :, at] = cut(e * line(4, c, g), line(5, c, g))

    def add_image(t, i):
        image[...] += lax.dot_general(
            pieces_x[t][i], pieces_y[t][i], (((1,), (1,)), ((), ())), preferred_element_type=F32
        )

    def pull_pair(t, i, first):
        span = slice(first * 128, (first + 2) * 128)
        by_x = times(left_x[...], pieces_y[t][i, :, span])
        by_y = times(left_y[...], pieces_x[t][i, :, span])
        for n in (first, first + 1):
            c = n % COMPS
            g = t * slots + i * TOGETHER + n // COMPS
            at = slice((n - first) * 128, (n - first + 1) * 128)
            for k, value in enumerate(moments(prof_x[t][i * columns + n] * by_x[:, at])):
                sums[k, c, pl.ds(g, 1), :] = value
            for k, value in enumerate(moments(prof_y[t][i * columns + n] * by_y[:, at])):
                sums[3 + k, c, pl.ds(g, 1), :] = value

    def loop(first, last, rendered=None, pulled=None):
        def body(i, carry):
            for n in range(columns):
                if rendered is not None:
                    profiles(rendered, i, n)
                if pulled is not None and n % 2 == 0:
                    pull_pair(pulled, i, n)
            if rendered is not None:
                add_image(rendered, i)
            return carry

        lax.fori_loop(first, last, body, 0)

    trips = [(counts_ref[t] + TOGETHER - 1) // TOGETHER for t in range(tiles)]
    for t in range(tiles):
        image[...] = jnp.zeros_like(image)
        common = 0
        if t > 0:
            common = jnp.minimum(trips[t - 1], trips[t])
            loop(0, common, rendered=t, pulled=t - 1)
            loop(common, trips[t - 1], pulled=t - 1)
        loop(common, trips[t], rendered=t)
        model = (image[:pixels, :pixels] + image[pixels:, pixels:]) + (
            image[:pixels, pixels:] + image[pixels:, :pixels]
        )
        cotangent = weight_ref[t, 0, 0] * (model - data_ref[t, 0, 0])
        left_x[...] = stack(cotangent)
        left_y[...] = stack(cotangent.T)
    loop(0, trips[tiles - 1], pulled=tiles - 1)

    def keep(x):
        return jnp.where(live, x, 0.0)

    for c in range(COMPS):
        lw, an = shared[row(2, c)], shared[row(3, c)]
        wide_x, wide_y = jnp.exp(2.0 * (lw + an)), jnp.exp(2.0 * (lw - an))
        inv_x, inv_y = 1.0 / (wide_x + psf * psf), 1.0 / (wide_y + psf * psf)
        amp = amps[c]
        shift_x, shift_y = middle - derived[0, c], middle - derived[1, c]
        first_x = sums[1, c] + shift_x * sums[0, c]
        first_y = sums[4, c] + shift_y * sums[3, c]
        second_x = sums[2, c] + shift_x * (sums[1, c] + first_x)
        second_y = sums[5, c] + shift_y * (sums[4, c] + first_y)
        var_x = keep(second_x * inv_x * (inv_x * wide_x))
        var_y = keep(amp * second_y * inv_y * (inv_y * wide_y))
        shared[row(0, c)] = keep(first_x * inv_x)
        shared[row(1, c)] = keep(amp * first_y * inv_y)
        shared[row(2, c)] = var_x + var_y
        shared[row(3, c)] = var_x - var_y
        amps[c] = keep(sums[3, c])
    none = jnp.zeros((wide, 128), F32)
    for q, piece in enumerate(pieces):
        for p, entry in enumerate(piece):
            is_shared = entry is not None and entry[0] == "s"
            if is_shared:
                half[q, p] = shared[band, entry[1]]
            else:
                half[q, p] = none if entry is None else amps[entry[1]]
            if p < shared_rows:
                other[q, p] = shared[1 - band, entry[1]] if is_shared else none
    for k in range(epochs):
        outs[k][...] = half[lax.rem(epoch + k, epochs)]
        outs[epochs + k][...] = other[lax.rem(epoch + k, epochs)]


def step_gradient(layout, counts, offsets, psf, data, weight, slot_rows, moved):
    shared_rows, rows, pieces = layout
    epochs = len(pieces)
    later = moved is not None
    tiles, _, slots = offsets.shape
    pixels = data.shape[-1]
    wide = tiles * slots
    shapes = [(rows, wide, 128)] * epochs + [(shared_rows, wide, 128)] * epochs
    ins = slot_rows + (moved or [])
    together = [pltpu.VMEM((BANDS, HALF, wide, 128), F32), pltpu.VMEM((COMPS, wide, 128), F32)]
    return pl.pallas_call(
        functools.partial(step_kernel, layout, later),
        out_shape=[f32(*s) for s in shapes],
        in_specs=[smem()] * 3 + [vmem()] * (2 + len(ins)),
        out_specs=[vmem()] * len(shapes),
        scratch_shapes=together
        + [
            pltpu.VMEM((6, COMPS, wide, 128), F32),
            pltpu.VMEM((2 * pixels, 2 * pixels), F32),
            pltpu.VMEM((pixels, 3 * pixels), F32),
            pltpu.VMEM((pixels, 3 * pixels), F32),
            pltpu.VMEM((6, COMPS, wide, 128), F32),
            pltpu.VMEM((epochs, rows, wide, 128), F32),
            pltpu.VMEM((epochs, shared_rows, wide, 128), F32),
        ]
        + [pltpu.VMEM((slots * COMPS, pixels, 128), F32)] * (2 * tiles)
        + [pltpu.VMEM((slots // TOGETHER, 2 * pixels, TOGETHER * COMPS * 128), F32)] * (2 * tiles)
        + (together if later else []),
        compiler_params=params(52),
        name="later_step" if later else "first_step",
    )(counts, offsets, psf, data, weight, *ins)


def combine_kernel(layout, match_ref, *refs):
    shared_rows, rows, pieces = layout
    got, (out_ref, short_ref, own_ref) = refs[:-3], refs[-3:]
    wide = out_ref.shape[1]
    match = match_ref[...]
    for p in range(rows):
        both = pick(match, jnp.concatenate([ref[p] for ref in got], axis=0))
        out_ref[p] = both[:wide]
        if p < shared_rows:
            short_ref[p] = both[:wide]
        own_ref[p] = both[wide:]


def dense_kernel(rows, place_ref, grads, *outs):
    blocks = outs[0].shape[1]
    place = place_ref[...]
    for p in range(rows):
        dense = pick(place, grads[p])
        for k, out in enumerate(outs):
            out[p] = dense[k * blocks : (k + 1) * blocks]


def final_kernel(layout, spacing, params_ref, *refs):
    shared_rows, rows, pieces = layout
    epochs = len(pieces)
    ins, (out_ref, held) = refs[: 2 * epochs], refs[2 * epochs :]
    band, epoch = lax.axis_index("band"), lax.axis_index("epoch")
    for k in range(epochs):
        q = lax.rem(epoch - k + epochs, epochs)
        held[band, q] = ins[k][...]
        held[1 - band, q] = ins[epochs + k][...]
    shift = [0.0, 0.0]
    for b in range(BANDS):
        for q, piece in enumerate(pieces):
            for p, entry in enumerate(piece):
                if entry is None:
                    continue
                row, position = row_of(b, entry)
                grad = held[b, q, p]
                out_ref[row] = params_ref[row] - STEP * grad
                if position is not None:
                    shift[position] = shift[position] + grad
    for k in range(2):
        out_ref[k] = params_ref[k] - (STEP * POSITION_RATE * spacing) * shift[k]


def shards(source_params, pixel_data, pixel_weight, psf_width, block_lists, block_counts, block_offsets):
    owners, epochs = lax.axis_size("tile"), lax.axis_size("epoch")
    blocks, param_rows, sources = source_params.shape
    tiles, slots = block_lists.shape
    wide = tiles * slots
    spacing = pixel_data.shape[-1] / 8.0
    layout = quarter_layout(epochs)
    shared_rows, rows, pieces = layout

    def to_peers(same, other):
        kept = [same[0]]
        for k in range(1, epochs):
            kept.append(lax.ppermute(same[k], "epoch", [(i, (i + k) % epochs) for i in range(epochs)]))
        for k in range(epochs):
            pairs = [
                (i * BANDS + b, (i + k) % epochs * BANDS + 1 - b)
                for i in range(epochs)
                for b in range(BANDS)
            ]
            kept.append(lax.ppermute(other[k], ("epoch", "band"), pairs))
        return kept

    def round_tiles(arrays):
        return [arrays[0]] + [
            lax.ppermute(arrays[k], "tile", [(i, (i + k) % owners) for i in range(owners)])
            for k in range(1, owners)
        ]

    def spread(piece, other):
        return to_peers([piece] * epochs, [other] * epochs)

    def summed(parts):
        near = functools.reduce(lambda a, b: a + b, parts[:epochs])
        far = functools.reduce(lambda a, b: a + b, parts[epochs:])
        return near + jnp.pad(far, ((0, rows - shared_rows), (0, 0), (0, 0)))

    by_row = jnp.transpose(source_params, (1, 0, 2))
    offsets = jnp.transpose(block_offsets, (0, 2, 1))
    packed = pl.pallas_call(
        functools.partial(pack_kernel, spacing),
        out_shape=f32(HALF + COMPS + 1, blocks, sources),
        in_specs=[smem(), vmem()],
        out_specs=vmem(),
        compiler_params=params(),
        name="pack",
    )(block_lists, by_row)
    got = round_tiles([packed] * owners)
    slot_half, slot_short, match, place = pl.pallas_call(
        functools.partial(select_kernel, wide),
        out_shape=[
            f32(HALF + COMPS, wide, sources),
            f32(HALF, wide, sources),
            f32(wide + blocks, owners * wide),
            f32(owners * blocks, wide),
        ],
        in_specs=[vmem()] * owners,
        out_specs=[vmem()] * 4,
        compiler_params=params(),
        name="select",
    )(*got)
    slot_rows = [slot_half, lax.ppermute(slot_short, "band", [(b, 1 - b) for b in range(BANDS)])]

    def gradient(moved):
        parts = step_gradient(
            layout, block_counts, offsets, psf_width, pixel_data, pixel_weight, slot_rows, moved
        )
        return summed(to_peers(parts[:epochs], parts[epochs:]))

    got = round_tiles([gradient(None)] * owners)
    slot_piece, slot_short, own_first = pl.pallas_call(
        functools.partial(combine_kernel, layout),
        out_shape=[
            f32(rows, wide, sources),
            f32(shared_rows, wide, sources),
            f32(rows, blocks, sources),
        ],
        in_specs=[vmem()] * (1 + owners),
        out_specs=[vmem()] * 3,
        compiler_params=params(),
        name="combine",
    )(match, *got)

    dense = pl.pallas_call(
        functools.partial(dense_kernel, rows),
        out_shape=[f32(rows, blocks, sources)] * owners,
        in_specs=[vmem()] * 2,
        out_specs=[vmem()] * owners,
        compiler_params=params(),
        name="dense",
    )(place, gradient(spread(slot_piece, slot_short)))
    own = functools.reduce(lambda a, b: a + b, round_tiles(dense), own_first)
    whole = pl.pallas_call(
        functools.partial(final_kernel, layout, spacing),
        out_shape=f32(param_rows, blocks, sources),
        in_specs=[vmem()] * (1 + 2 * epochs),
        out_specs=vmem(),
        scratch_shapes=[pltpu.VMEM((BANDS, epochs, rows, blocks, sources), F32)],
        compiler_params=params(),
        name="final",
    )(by_row, *spread(own, own))
    return jnp.transpose(whole, (1, 0, 2))


def solution(mesh):
    return jax.shard_map(
        shards,
        mesh=mesh,
        in_specs=(
            P(("region", "tile"), None, None),
            P(("region", "tile"), "epoch", "band", None, None),
            P(("region", "tile"), "epoch", "band", None, None),
            P(("region", "epoch"), "band"),
            P(("region", "tile"), None),
            P(("region", "tile")),
            P(("region", "tile"), None, None),
        ),
        out_specs=P(("region", "tile"), None, None),
        check_vma=False,
    )
```
